128 devices in a mesh: dp: 2 (over core), expert: 64 (over z, y, x).
Axes of the slice: x: 4, y: 4, z: 4, core: 2. Of those that a mesh axis runs over, the one named last changes fastest.
Arguments:
- block_entry_states: bfloat16 [64, 256, 2048], P('expert', 'dp'), may hold values from -6 to 6
- block_result_cotangent: bfloat16 [64, 256, 2048], P('expert', 'dp'), may hold values from -6 to 6
- token_assignments: int32 [64, 256, 8], P('expert', 'dp'), may hold values from 0 to 63, all different within a row
- packed_segment_sizes: int32 [64, 4], P('expert'), may hold values from 1 to 192, 256 in all within a row
- admitted_route_quota: int32 [64], replicated, may hold values from 6 to 12, as said below
- mixing_scale_factor: float32 [2048], replicated, may hold values from 0.25 to 1.75
- asker_projection: bfloat16 [2048, 2048], P('expert', 'dp'), may hold values from -0.125 to 0.125
- lookup_projection: bfloat16 [2048, 2048], P('expert', 'dp'), may hold values from -0.125 to 0.125
- content_projection: bfloat16 [2048, 2048], P('expert', 'dp'), may hold values from -0.125 to 0.125
- mixing_projection_back: bfloat16 [2048, 2048], P(('dp', 'expert')), may hold values from -0.75 to 0.75
- asker_scale_factor: float32 [2048], replicated, may hold values from 0.3 to 2.8
- lookup_scale_factor: float32 [2048], replicated, may hold values from 0.3 to 2.8
- specialist_scale_factor: float32 [2048], replicated, may hold values from 0.25 to 1.75
- dispatcher_projection: bfloat16 [2048, 64], replicated, may hold values from -0.15625 to 0.15625
- specialist_switch_tensor: bfloat16 [64, 2048, 1024], P('expert'), may hold values from -0.125 to 0.125
- specialist_widen_tensor: bfloat16 [64, 2048, 1024], P('expert'), may hold values from -0.125 to 0.125
- specialist_shrink_tensor: bfloat16 [64, 1024, 2048], P('expert'), may hold values from -6 to 6
Outputs:
- block_output: float32 [64, 256, 2048], P('expert', 'dp')
- input_grad: float32 [64, 256, 2048], P('expert', 'dp')
- attn_gain_grad: float32 [2048], replicated
- query_weight_grad: float32 [2048, 2048], P('expert', 'dp')
- key_weight_grad: float32 [2048, 2048], P('expert', 'dp')
- value_weight_grad: float32 [2048, 2048], P('expert', 'dp')
- output_weight_grad: float32 [2048, 2048], P(('dp', 'expert'))
- query_gain_grad: float32 [2048], replicated
- key_gain_grad: float32 [2048], replicated
- moe_gain_grad: float32 [2048], replicated
- router_weight_grad: float32 [2048, 64], replicated
- gate_weight_grad: float32 [64, 2048, 1024], P('expert', None, 'dp')
- up_weight_grad: float32 [64, 2048, 1024], P('expert', None, 'dp')
- down_weight_grad: float32 [64, 1024, 2048], P('expert', 'dp')
- expert_counts: int32 [64, 128], P('expert', 'dp')
The draws below stay inside these ranges and needn't reach their ends.
Inputs may be any that keep to these rules, and one draw needn't show every extreme that they name: `token_assignments`: each token names 8 different experts, and every expert is named by some token. `packed_segment_sizes`: the 4 lengths of a row sum to 256, and the longest is 192. `admitted_route_quota`: some expert accepts 12.
All inputs are finite; a program needn't handle non-finite values.
Results may differ from the reference program's by a relative error of at most 0.023.
Values may be sent and summed in bfloat16 or wider, within the bound.
No kernel may reach another device: no remote copies, remote signals or barrier semaphores. Data moves between devices by JAX's collectives and lax.ppermute only.
A program may use at most 256 MiB of HBM per device.

```python
import math
import jax
import jax.numpy as jnp
import numpy as np
from jax import lax

D = 2048
HEADS = 16
HEAD_DIM = 128
FF = 1024
TOP = 8
TOK_DEV = 128
DOCS = 4
EXPERTS = 64
LEN = 256
ROWS = 64
MOST_DOC = 192
CAP = 12
N_DP = 2
N_EXPERT = 64


def draw_admitted_route_quota(key, part):
    key = jax.random.fold_in(key, 11)
    first_key, second_key = jax.random.split(key)
    accepted = jax.random.randint(first_key, (EXPERTS,), max(2, CAP // 2), CAP + 1)
    fullest = jax.random.randint(second_key, (), 0, EXPERTS)
    return jnp.where(jnp.arange(EXPERTS) == fullest, CAP, accepted).astype(jnp.int32)


def trending_gain(key, ratio, lower, upper):
    first_key, second_key = jax.random.split(key)
    place = jnp.arange(D, dtype=jnp.float32) / (D - 1) - 0.5
    direction = jnp.where(jax.random.randint(first_key, (), 0, 2) == 0, 1.0, -1.0)
    rough = jax.random.uniform(second_key, (D,), jnp.float32, lower, upper)
    return (rough * ratio ** (direction * place)).astype(jnp.float32)


def draw_asker_scale_factor(key, part):
    key = jax.random.fold_in(key, 12)
    return trending_gain(key, 3.0, 0.8, 1.2)


def draw_lookup_scale_factor(key, part):
    key = jax.random.fold_in(key, 13)
    return trending_gain(key, 3.0, 0.8, 1.2)


def shard_levels(own_key, dims, cuts, least, largest):
    level, own = 1.0, jax.random.fold_in(own_key, 6)
    for axis_at, parts in cuts:
        heights = jnp.exp(jax.random.uniform(jax.random.fold_in(own, axis_at), (parts,), jnp.float32, least / len(cuts), largest / len(cuts)))
        level = level * jnp.repeat(heights, dims[axis_at] // parts).reshape([-1 if axis == axis_at else 1 for axis in range(len(dims))])
    return level


def distinct(rng, rows, number_of, top, lift):
    order = jax.random.permutation(jax.random.fold_in(rng, 1), number_of)
    favour = order
    for power in range(3):
        favour = favour * favour // number_of
    favour = favour * lift // number_of
    tickets = jax.random.randint(jax.random.fold_in(rng, 2), (rows, number_of), 0, 4096) + favour
    holders = jax.random.permutation(jax.random.fold_in(rng, 3), rows)[jnp.arange(number_of) % rows]
    tickets = jnp.where(jnp.arange(rows)[:, None] == holders[None, :], 1 << 14, tickets)
    score = tickets * number_of + jnp.arange(number_of)
    return lax.top_k(score.astype(jnp.int32), top)[1].astype(jnp.int32)


def profile(number_of, total, most, skew):
    portions = [(1 << 20) // math.isqrt(rank ** skew) + 1 for rank in range(2, number_of + 1)]
    spare, given = total - most - (number_of - 1), [1] * (number_of - 1)
    while spare > 0:
        movable = [i for i in range(number_of - 1) if given[i] < most]
        whole, remaining = sum([portions[i] for i in movable]), spare
        for i in movable:
            addition = min(most - given[i], max(1, remaining * portions[i] // whole), spare)
            given[i] = given[i] + addition
            spare = spare - addition
    return np.array([most] + given)


def uneven(key, number_of, total, limit, skew):
    if number_of == 2:
        one = jax.random.randint(key, (), max(1, total - limit), min(limit, total - 1) + 1)
        return jnp.stack([one, total - one])
    tallies = jnp.asarray(profile(number_of, total, limit, skew), jnp.int32)
    couples = (number_of - 1) // 2
    donor, receiver = tallies[1:1 + 2 * couples:2], tallies[2:2 + 2 * couples:2]
    room = jnp.minimum(donor - 1, limit - receiver)
    shifted = jax.random.randint(jax.random.fold_in(key, 1), (couples,), 0, 1 << 20) % (room + 1)
    tallies = tallies.at[1:1 + 2 * couples:2].set(donor - shifted).at[2:2 + 2 * couples:2].set(receiver + shifted)
    return tallies[jax.random.permutation(jax.random.fold_in(key, 2), number_of)]


def gaussian(key, dims, deviation, reach, cuts=(), kind=jnp.bfloat16):
    result = deviation * jax.random.normal(key, dims, jnp.float32)
    if cuts:
        result = result * shard_levels(key, dims, cuts, -0.22, 0.18)
    return jnp.clip(result, -reach, reach).astype(kind)


def setup_inputs(seed: int = 0) -> dict:
    splits = jax.random.split(jax.random.key(seed), 18)
    return {
        "block_entry_states": gaussian(splits[0], (ROWS, LEN, D), 1.0, 6.0, ((0, 64), (1, 2))),
        "block_result_cotangent": gaussian(splits[1], (ROWS, LEN, D), 1.0, 6.0, ((0, 64), (1, 2))),
        "token_assignments": distinct(splits[2], ROWS * LEN, EXPERTS, TOP, 1024).reshape((ROWS, LEN, TOP)),
        "packed_segment_sizes": jax.vmap(lambda own: uneven(own, DOCS, LEN, MOST_DOC, 2))(jax.random.split(splits[3], ROWS)).reshape((ROWS, DOCS)).astype(jnp.int32),
        "admitted_route_quota": draw_admitted_route_quota(jax.random.fold_in(splits[17], 71), 0),
        "mixing_scale_factor": jnp.clip(1.0 + 0.15 * jax.random.normal(splits[5], (D,), jnp.float32), 0.25, 1.75),
        "asker_projection": gaussian(splits[6], (D, D), D ** -0.5, 0.125, ((0, 64), (1, 2))),
        "lookup_projection": gaussian(splits[7], (D, D), D ** -0.5, 0.125, ((0, 64), (1, 2))),
        "content_projection": gaussian(splits[8], (D, D), D ** -0.5, 0.125, ((0, 64), (1, 2))),
        "mixing_projection_back": gaussian(splits[9], (D, D), (D // 32) ** -0.5, 0.75, ((0, 128),)),
        "asker_scale_factor": draw_asker_scale_factor(jax.random.fold_in(splits[17], 71), 0),
        "lookup_scale_factor": draw_lookup_scale_factor(jax.random.fold_in(splits[17], 71), 0),
        "specialist_scale_factor": jnp.clip(1.0 + 0.15 * jax.random.normal(splits[12], (D,), jnp.float32), 0.25, 1.75),
        "dispatcher_projection": gaussian(splits[13], (D, EXPERTS), (0.5 / D ** 0.5), 0.15625),
        "specialist_switch_tensor": gaussian(splits[14], (EXPERTS, D, FF), D ** -0.5, 0.125, ((0, 64),)),
        "specialist_widen_tensor": gaussian(splits[15], (EXPERTS, D, FF), D ** -0.5, 0.125, ((0, 64),)),
        "specialist_shrink_tensor": gaussian(splits[16], (EXPERTS, FF, D), (0.75 * EXPERTS / FF ** 0.5), 6.0, ((0, 64),)),
    }


EPS = 1e-05
THETA = 10000.0
NEG = -1e+30
HIGH = lax.Precision.HIGHEST

@jax.custom_vjp
def low(v):
    return lax.optimization_barrier(v.astype(jnp.bfloat16)).astype(jnp.float32)

@jax.custom_vjp
def low_back(v):
    return v

def low_keep(v):
    return (low(v), None)

def low_pass(kept, grad):
    return (grad,)

def back_keep(v):
    return (v, None)

def back_low(kept, grad):
    return (low(grad),)
low.defvjp(low_keep, low_pass)
low_back.defvjp(back_keep, back_low)

def rms_norm(values, gain):
    return values * lax.rsqrt(lax.optimization_barrier(jnp.mean(values * values, axis=-1, keepdims=True)) + EPS) * gain

def doc_places(lengths, places):
    ends = jnp.cumsum(lengths, dtype=jnp.int32)
    done = ends[None, :] <= places[:, None]
    doc_ids = lax.optimization_barrier(jnp.sum(done.astype(jnp.int32), axis=1, dtype=jnp.int32))
    starts = lax.optimization_barrier(jnp.sum(jnp.where(done, lengths[None, :], 0), axis=1, dtype=jnp.int32))
    return (doc_ids, places - starts)

def row_places(lengths):
    return doc_places(lengths, jnp.arange(LEN, dtype=jnp.int32))

def rope_tables(offsets, head_width):
    half_width = head_width // 2
    inverse = THETA ** (-jnp.arange(half_width, dtype=jnp.float32) * 2.0 / head_width)
    angles = offsets.astype(jnp.float32)[..., None] * inverse
    return (jnp.cos(angles)[..., None, :], jnp.sin(angles)[..., None, :])

def rotate(values, cos_table, sin_table):
    half_width = values.shape[-1] // 2
    first, second = (values[..., :half_width], values[..., half_width:])
    return jnp.concatenate([first * cos_table - second * sin_table, second * cos_table + first * sin_table], axis=-1)

def softmax_last(values):
    row_max = lax.optimization_barrier(jnp.max(values, axis=-1, keepdims=True))
    exponent = jnp.exp(values - row_max)
    return exponent / lax.optimization_barrier(jnp.sum(exponent, axis=-1, keepdims=True))

def reference(block_entry_states, block_result_cotangent, token_assignments, packed_segment_sizes, admitted_route_quota, mixing_scale_factor, asker_projection, lookup_projection, content_projection, mixing_projection_back, asker_scale_factor, lookup_scale_factor, specialist_scale_factor, dispatcher_projection, specialist_switch_tensor, specialist_widen_tensor, specialist_shrink_tensor):
    blocks = ROWS * N_DP
    per_block = TOK_DEV * TOP
    total_slots = EXPERTS * blocks * CAP
    doc_ids, doc_offset = jax.vmap(row_places)(packed_segment_sizes)
    cos_table, sin_table = rope_tables(doc_offset, HEAD_DIM)
    expert_ids = token_assignments.reshape(blocks, per_block).astype(jnp.int32)
    selected_specialists = (expert_ids[:, :, None] == jnp.arange(EXPERTS, dtype=jnp.int32)[None, None, :]).astype(jnp.int32)
    before = jnp.cumsum(selected_specialists, axis=1, dtype=jnp.int32) - selected_specialists
    route_rank = lax.optimization_barrier(jnp.sum(before * selected_specialists, axis=2, dtype=jnp.int32))
    specialist_slot_ceilings = lax.optimization_barrier(jnp.sum(selected_specialists * admitted_route_quota[None, None, :], axis=2, dtype=jnp.int32))
    kept_mask = route_rank < specialist_slot_ceilings
    counts = lax.optimization_barrier(jnp.sum(selected_specialists * kept_mask[:, :, None].astype(jnp.int32), axis=1, dtype=jnp.int32))
    expert_counts = counts.reshape(N_EXPERT, N_DP, EXPERTS).transpose(2, 1, 0).reshape(EXPERTS, N_DP * N_EXPERT)
    block_ids = jnp.arange(blocks, dtype=jnp.int32)[:, None]
    slot_index = jnp.where(kept_mask, expert_ids * (blocks * CAP) + block_ids * CAP + route_rank, total_slots)
    token_owner = (jnp.arange(blocks * per_block, dtype=jnp.int32) // TOP).reshape(blocks, per_block)
    slot_token = jnp.zeros((total_slots,), jnp.int32).at[slot_index.reshape(-1)].set(token_owner.reshape(-1), mode='drop')
    filled = jnp.zeros((total_slots,), jnp.float32).at[slot_index.reshape(-1)].set(1.0, mode='drop')
    per_expert = (EXPERTS, blocks * CAP)
    slot_token = slot_token.reshape(per_expert)
    filled = filled.reshape(per_expert)
    group_rows = math.gcd(ROWS, max(1, 4096 // LEN))
    score_scale = HEAD_DIM ** (-0.5)
    places = jnp.arange(LEN, dtype=jnp.int32)
    causal = places[None, :] <= places[:, None]
    head_shape = (ROWS, LEN, HEADS, HEAD_DIM)

    def grouped(values):
        return values.reshape((ROWS // group_rows, group_rows) + values.shape[1:])

    def attend(pieces):
        queries, keys, values, row_docs = pieces
        raw_scores = low_back(jnp.einsum('gqhd,gkhd->ghqk', queries, keys, precision=HIGH) * score_scale)
        allowed = (row_docs[:, :, None] == row_docs[:, None, :]) & causal[None]
        attn_probs = softmax_last(jnp.where(allowed[:, None], raw_scores, NEG))
        return jnp.einsum('ghqk,gkhd->gqhd', low(attn_probs), values, precision=HIGH)

    def forward(inputs, mixing_scale_factor, asker_projection, lookup_projection, content_projection, mixing_projection_back, asker_scale_factor, lookup_scale_factor, specialist_scale_factor, dispatcher_projection, specialist_switch_tensor, specialist_widen_tensor, specialist_shrink_tensor):
        normed_in = low(rms_norm(inputs, mixing_scale_factor))
        query_proj = low_back(jnp.einsum('rld,de->rle', normed_in, asker_projection, precision=HIGH))
        key_proj = low_back(jnp.einsum('rld,de->rle', normed_in, lookup_projection, precision=HIGH))
        value_low = low(low_back(jnp.einsum('rld,de->rle', normed_in, content_projection, precision=HIGH)))
        queries = low(rotate(rms_norm(query_proj, asker_scale_factor).reshape(head_shape), cos_table, sin_table))
        keys = low(rotate(rms_norm(key_proj, lookup_scale_factor).reshape(head_shape), cos_table, sin_table))
        mixed_heads = lax.map(jax.checkpoint(attend), (grouped(queries), grouped(keys), grouped(value_low.reshape(head_shape)), grouped(doc_ids)))
        mixed_heads = low(low_back(mixed_heads.reshape(ROWS, LEN, D)))
        hidden = inputs + low_back(jnp.einsum('rld,de->rle', mixed_heads, mixing_projection_back, precision=HIGH))
        normed_moe = low(rms_norm(hidden, specialist_scale_factor)).reshape(ROWS * LEN, D)
        logits = low_back(jnp.dot(normed_moe, dispatcher_projection, precision=HIGH))
        route_probs = softmax_last(logits)

        def expert(pieces):
            index, fill, gate_one, up_one, down_one = pieces
            rows_in = low_back(normed_moe[index] * fill[:, None])
            gate_pre = low_back(jnp.dot(rows_in, gate_one, precision=HIGH))
            up_pre = low_back(jnp.dot(rows_in, up_one, precision=HIGH))
            activation = low(gate_pre * jax.nn.sigmoid(gate_pre) * up_pre)
            return low_back(low(jnp.dot(activation, down_one, precision=HIGH)))
        expert_out = lax.map(jax.checkpoint(expert), (slot_token, filled, specialist_switch_tensor, specialist_widen_tensor, specialist_shrink_tensor))
        slot_gate = route_probs[slot_token, jnp.arange(EXPERTS, dtype=jnp.int32)[:, None]] * filled
        weighted = (expert_out * slot_gate[:, :, None]).reshape(-1, D)
        moe_part = jnp.zeros((ROWS * LEN, D), jnp.float32).at[slot_token.reshape(-1)].add(weighted)
        return hidden + moe_part.reshape(ROWS, LEN, D)
    floats = (block_entry_states.astype(jnp.float32), mixing_scale_factor, asker_projection.astype(jnp.float32), lookup_projection.astype(jnp.float32), content_projection.astype(jnp.float32), mixing_projection_back.astype(jnp.float32), asker_scale_factor, lookup_scale_factor, specialist_scale_factor, dispatcher_projection.astype(jnp.float32), specialist_switch_tensor.astype(jnp.float32), specialist_widen_tensor.astype(jnp.float32), specialist_shrink_tensor.astype(jnp.float32))
    block_output, pullback = jax.vjp(forward, *floats)
    grads = pullback(block_result_cotangent.astype(jnp.float32))
    return (block_output, grads[0], grads[1], grads[2], grads[3], grads[4], grads[5], grads[6], grads[7], grads[8], grads[9], grads[10], grads[11], grads[12], expert_counts)
```

```python
import jax
import jax.numpy as jnp
from jax import lax
from jax.experimental import pallas as pl
from jax.experimental.pallas import tpu as pltpu
from jax.sharding import PartitionSpec as P

HEADS = 16
EPS = 1e-05
THETA = 10000.0
NEG = -1e30
BOTH = ("dp", "expert")

FLIPS = ((1, 4, 16), (3, 12, 48))
STEPS = 6


def flip_of(core, part, step):
    return FLIPS[core][step] if step < 3 else FLIPS[1 - core][(step + part) % 3]


def mask_of(core, part, index):
    mask = 0
    for step in range(STEPS):
        if (index >> step) & 1:
            mask ^= flip_of(core, part, step)
    return mask


def permute_step(value, part, step):
    pairs = []
    for core in range(2):
        flip = flip_of(core, part, step)
        pairs += [(64 * core + d, 64 * core + (d ^ flip)) for d in range(64)]
    return lax.ppermute(value, BOTH, pairs)


def relative_order(core, me, part):
    tables = [jnp.array([mask_of(c, part, r) for r in range(64)], jnp.int32) for c in range(2)]
    return jnp.where(core == 0, tables[0], tables[1]) ^ me


def natural_order(order):
    return jnp.argmax(order[None, :] == jnp.arange(64, dtype=jnp.int32)[:, None], axis=1)


def reorder(rows, order):
    blocks = rows.reshape(64, rows.shape[0] // 64, rows.shape[1])
    return jnp.take(blocks, order, axis=0, mode="clip").reshape(rows.shape)


def sum_everywhere(rows, core, part):
    half = rows.shape[1] // 2
    own = lax.dynamic_slice_in_dim(rows, core * half, half, axis=1)
    own = own + swap(lax.dynamic_slice_in_dim(rows, (1 - core) * half, half, axis=1))
    for step in range(STEPS):
        own = own + permute_step(own, part, step)
    other = swap(own)
    return jnp.concatenate(
        [jnp.where(core == 0, own, other), jnp.where(core == 0, other, own)], axis=1
    )


def swap(value):
    return lax.ppermute(value, "dp", [(0, 1), (1, 0)])


def dot(left, right):
    return jnp.dot(left, right, preferred_element_type=jnp.float32)


def dot_tn(left, right):
    return lax.dot_general(
        left, right, (((0,), (0,)), ((), ())), preferred_element_type=jnp.float32
    )


def dot_nt(left, right):
    return lax.dot_general(
        left, right, (((1,), (1,)), ((), ())), preferred_element_type=jnp.float32
    )


def rms_factor(values):
    return lax.rsqrt(jnp.mean(values * values, axis=-1, keepdims=True) + EPS)


def norm_back(grad_normed, source, factor, gain):
    scaled = grad_normed * gain
    grad_source = factor * (
        scaled - source * factor * factor * jnp.mean(scaled * source, axis=-1, keepdims=True)
    )
    grad_gain = jnp.sum(grad_normed * source * factor, axis=0)
    return (grad_source, grad_gain)


def doc_places(lengths, places):
    ends = jnp.cumsum(lengths, dtype=jnp.int32)
    done = ends[None, :] <= places[:, None]
    doc_ids = jnp.sum(done.astype(jnp.int32), axis=1, dtype=jnp.int32)
    starts = jnp.sum(jnp.where(done, lengths[None, :], 0), axis=1, dtype=jnp.int32)
    return (doc_ids, places - starts)


def rope_tables(offsets, head_width):
    half_width = head_width // 2
    inverse = THETA ** (-jnp.arange(half_width, dtype=jnp.float32) * 2.0 / head_width)
    angles = offsets.astype(jnp.float32)[..., None] * inverse
    return (jnp.cos(angles)[..., None, :], jnp.sin(angles)[..., None, :])


def rotate(values, cos_table, sin_table):
    half_width = values.shape[-1] // 2
    first, second = (values[..., :half_width], values[..., half_width:])
    return jnp.concatenate(
        [first * cos_table - second * sin_table, second * cos_table + first * sin_table], axis=-1
    )


def unrotate(grads, cos_table, sin_table):
    half_width = grads.shape[-1] // 2
    first, second = (grads[..., :half_width], grads[..., half_width:])
    return jnp.concatenate(
        [first * cos_table + second * sin_table, second * cos_table - first * sin_table], axis=-1
    )


def softmax_rows(values):
    exponent = jnp.exp(values - jnp.max(values, axis=-1, keepdims=True))
    return exponent / jnp.sum(exponent, axis=-1, keepdims=True)


def half_picker(count, half):
    rows = lax.broadcasted_iota(jnp.int32, (count // 2, count), 0)
    cols = lax.broadcasted_iota(jnp.int32, (count // 2, count), 1)
    return (cols == 2 * rows + half).astype(jnp.float32).astype(jnp.bfloat16)


def unpack_block(packed):
    count, width = packed.shape[0], packed.shape[1] * 2 // 3
    spare = packed[:, width:]
    rest = [dot(half_picker(count, h), spare).astype(jnp.bfloat16) for h in range(2)]
    return packed[:, :width], rest


def pack_block(rows, out_ref):
    count, width = out_ref.shape[0], rows.shape[1]
    half = width // 2
    out_ref[:, :width] = rows[:count]
    out_ref[:, width:] = (
        dot_tn(half_picker(count, 0), rows[count:, :half])
        + dot_tn(half_picker(count, 1), rows[count:, half:])
    ).astype(jnp.bfloat16)


def unpack_body(packed_ref, rows_ref):
    main, rest = unpack_block(packed_ref[...])
    count, width = main.shape
    rows_ref[:count] = main
    rows_ref[count:, : width // 2] = rest[0]
    rows_ref[count:, width // 2 :] = rest[1]


def unpack(packed):
    count, width = packed.shape[0], packed.shape[1] * 2 // 3
    block = count // 2
    return pl.pallas_call(
        unpack_body,
        grid=(2,),
        in_specs=[pl.BlockSpec((block, width * 3 // 2), lambda i: (i, 0))],
        out_specs=pl.BlockSpec((block * 3 // 2, width), lambda i: (i, 0)),
        out_shape=jax.ShapeDtypeStruct((count * 3 // 2, width), jnp.bfloat16),
        compiler_params=pltpu.CompilerParams(vmem_limit_bytes=32 * 1024 * 1024),
    )(packed)


def send_body(main_ref, spare_ref, rows_ref, out_ref):
    width = rows_ref.shape[1]
    half, count = width // 2, rows_ref.shape[0]
    out_ref[:, :width] = dot_tn(main_ref[...], rows_ref[...]).astype(jnp.bfloat16)
    out_ref[:, width:] = (
        dot_tn(spare_ref[:count], rows_ref[:, :half])
        + dot_tn(spare_ref[count:], rows_ref[:, half:])
    ).astype(jnp.bfloat16)


def to_experts(main, spare, rows):
    tokens, lines = main.shape
    width, block = rows.shape[1], lines // 2
    return pl.pallas_call(
        send_body,
        grid=(2,),
        in_specs=[
            pl.BlockSpec((tokens, block), lambda i: (0, i)),
            pl.BlockSpec((2 * tokens, block), lambda i: (0, i)),
            pl.BlockSpec((tokens, width), lambda i: (0, 0)),
        ],
        out_specs=pl.BlockSpec((block, width * 3 // 2), lambda i: (i, 0)),
        out_shape=jax.ShapeDtypeStruct((lines, width * 3 // 2), jnp.bfloat16),
        compiler_params=pltpu.CompilerParams(vmem_limit_bytes=32 * 1024 * 1024),
    )(main, spare, rows)


def combine_body(main_ref, spare_ref, lines_ref, out_ref):
    tokens, width = out_ref.shape
    half = width // 2
    spare_lines = lines_ref[:, width:]
    out_ref[:, :half] = dot(main_ref[...], lines_ref[:, :half]) + dot(
        spare_ref[:tokens], spare_lines
    )
    out_ref[:, half:] = dot(main_ref[...], lines_ref[:, half:width]) + dot(
        spare_ref[tokens:], spare_lines
    )


def from_experts(main, spare, lines):
    return pl.pallas_call(
        combine_body,
        out_shape=jax.ShapeDtypeStruct((main.shape[0], lines.shape[1] * 2 // 3), jnp.float32),
        compiler_params=pltpu.CompilerParams(vmem_limit_bytes=32 * 1024 * 1024),
    )(main, spare, lines)


def out_body(core_ref, act_ref, own_ref, other_ref, out_ref):
    rows = dot(act_ref[0], own_ref[...]) + dot(act_ref[1], other_ref[...])
    pack_block(rows.astype(jnp.bfloat16), out_ref)


def expert_results(acts, down_w, core):
    _, count, units = acts.shape
    width, block = down_w.shape[1], count // 2
    return pl.pallas_call(
        out_body,
        grid_spec=pltpu.PrefetchScalarGridSpec(
            num_scalar_prefetch=1,
            grid=(2,),
            in_specs=[
                pl.BlockSpec((2, block, units), lambda i, c: (0, i, 0)),
                pl.BlockSpec((units, width), lambda i, c: (c[0], 0)),
                pl.BlockSpec((units, width), lambda i, c: (1 - c[0], 0)),
            ],
            out_specs=pl.BlockSpec((block * 2 // 3, width * 3 // 2), lambda i, c: (i, 0)),
        ),
        out_shape=jax.ShapeDtypeStruct((count * 2 // 3, width * 3 // 2), jnp.bfloat16),
        compiler_params=pltpu.CompilerParams(vmem_limit_bytes=40 * 1024 * 1024),
        cost_estimate=pl.CostEstimate(
            flops=4 * count * width * units, bytes_accessed=12 * 1024 * 1024, transcendentals=0
        ),
    )(core[None].astype(jnp.int32), acts, down_w, down_w)


def exchange(rows):
    return lax.all_to_all(rows, "expert", split_axis=0, concat_axis=0, tiled=True)


def expert_body(
    core_ref, mine_ref, packed_ref, act_grad_ref, gate_w_ref, up_w_ref, router_ref,
    back_ref, x_ref, gate_out_ref, up_out_ref, act_out_ref, logit_ref,
    total, probs_ref, gate_ref, gate_grad_ref,
):
    f32, bf16 = jnp.float32, jnp.bfloat16
    step = pl.program_id(1)

    @pl.when(step == 0)
    def _():
        unpack_body(packed_ref, x_ref)
        probs = softmax_rows(dot(x_ref[...], router_ref[...]))
        probs_ref[...] = probs
        gate_ref[...] = jnp.sum(probs * mine_ref[...], axis=1, keepdims=True)
        gate_grad_ref[...] = jnp.zeros_like(gate_grad_ref)

    x = x_ref[...]
    gate_w, up_w, gate = gate_w_ref[...], up_w_ref[...], gate_ref[...]
    gate_pre, up_pre = dot(x, gate_w), dot(x, up_w)
    plain = act_grad_ref[...]
    sigmoid = 1.0 / (1.0 + jnp.exp(-gate_pre))
    silu = gate_pre * sigmoid
    act = silu * up_pre
    gate_grad_ref[...] += jnp.sum(act * plain, axis=1, keepdims=True)
    act_grad = gate * plain
    gate_pre_grad = (act_grad * up_pre * sigmoid * (1.0 + gate_pre * (1.0 - sigmoid))).astype(bf16)
    up_pre_grad = (act_grad * silu).astype(bf16)
    gate_out_ref[0] = gate_pre_grad
    up_out_ref[0] = up_pre_grad
    act_out_ref[0] = (gate * act).astype(bf16)
    part = dot_nt(gate_pre_grad, gate_w) + dot_nt(up_pre_grad, up_w)

    @pl.when(step == 0)
    def _():
        total[...] = part

    @pl.when(step > 0)
    def _():
        total[...] += part

    @pl.when(step == pl.num_programs(1) - 1)
    def _():
        logit = (gate_grad_ref[...] * gate * (mine_ref[...] - probs_ref[...])).astype(bf16)
        logit_ref[...] = logit
        pack_block((total[...] + dot_nt(logit, router_ref[...])).astype(bf16), back_ref)


def expert_rows(packed, plain_act_grad, gate_w, up_w, router, core, me):
    f32, bf16 = jnp.float32, jnp.bfloat16
    lines = packed.shape[0]
    width, units = gate_w.shape
    count, experts = lines * 3 // 2, router.shape[1]
    tiles = 4
    block, tile, cut = count // 2, units // tiles, tiles // 2
    mine = (jnp.arange(experts, dtype=jnp.int32) == me).astype(f32)[None, :]
    halves = jax.ShapeDtypeStruct((2, count, units // 2), bf16)
    half_spec = pl.BlockSpec((1, block, tile), lambda i, j, c: ((j // cut + c[0]) % 2, i, j % cut))
    packed_spec = pl.BlockSpec((lines // 2, width * 3 // 2), lambda i, j, c: (i, 0))
    return pl.pallas_call(
        expert_body,
        grid_spec=pltpu.PrefetchScalarGridSpec(
            num_scalar_prefetch=1,
            grid=(2, tiles),
            in_specs=[
                pl.BlockSpec((1, experts), lambda i, j, c: (0, 0)),
                packed_spec,
                pl.BlockSpec((block, tile), lambda i, j, c: (i, j)),
                pl.BlockSpec((width, tile), lambda i, j, c: (0, j)),
                pl.BlockSpec((width, tile), lambda i, j, c: (0, j)),
                pl.BlockSpec((width, experts), lambda i, j, c: (0, 0)),
            ],
            out_specs=[
                packed_spec,
                pl.BlockSpec((block, width), lambda i, j, c: (i, 0)),
                half_spec,
                half_spec,
                half_spec,
                pl.BlockSpec((block, experts), lambda i, j, c: (i, 0)),
            ],
            scratch_shapes=[
                pltpu.VMEM((block, width), f32),
                pltpu.VMEM((block, experts), f32),
                pltpu.VMEM((block, 1), f32),
                pltpu.VMEM((block, 1), f32),
            ],
        ),
        out_shape=[
            jax.ShapeDtypeStruct(packed.shape, bf16),
            jax.ShapeDtypeStruct((count, width), bf16),
            halves,
            halves,
            halves,
            jax.ShapeDtypeStruct((count, experts), bf16),
        ],
        compiler_params=pltpu.CompilerParams(vmem_limit_bytes=48 * 1024 * 1024),
        cost_estimate=pl.CostEstimate(
            flops=8 * count * width * units, bytes_accessed=36 * 1024 * 1024, transcendentals=count * units
        ),
    )(core[None].astype(jnp.int32), mine, packed, plain_act_grad, gate_w, up_w, router)


def output_body(core_ref, heads_ref, weight_ref, inputs_ref, own_ref, other_ref):
    count, half = own_ref.shape
    weight = weight_ref[...].reshape(half, half)
    first = pl.multiple_of(core_ref[0] * count, count)
    second = pl.multiple_of((1 - core_ref[0]) * count, count)
    other_ref[...] = dot(heads_ref[pl.ds(second, count), :], weight).astype(jnp.bfloat16)
    own_ref[...] = dot(heads_ref[pl.ds(first, count), :], weight) + inputs_ref[...].astype(
        jnp.float32
    )


def output_shares(heads, stacked, inputs, core):
    tokens, width = inputs.shape
    half = width // 2
    return pl.pallas_call(
        output_body,
        grid_spec=pltpu.PrefetchScalarGridSpec(
            num_scalar_prefetch=1,
            grid=(2,),
            in_specs=[
                pl.BlockSpec((2 * tokens, half), lambda h, c: (0, 0)),
                pl.BlockSpec((64, half // 64, half), lambda h, c: (0, h, 1)),
                pl.BlockSpec((tokens, half), lambda h, c: (0, h)),
            ],
            out_specs=[pl.BlockSpec((tokens, half), lambda h, c: (0, h))] * 2,
        ),
        out_shape=[
            jax.ShapeDtypeStruct((tokens, width), jnp.float32),
            jax.ShapeDtypeStruct((tokens, width), jnp.bfloat16),
        ],
        compiler_params=pltpu.CompilerParams(vmem_limit_bytes=32 * 1024 * 1024),
    )(core[None].astype(jnp.int32), heads, stacked, inputs)


def heads_body(grad_ref, weight_ref, out_ref, total):
    half = out_ref.shape[1]
    part = dot_nt(grad_ref[...], weight_ref[...].reshape(half, half))

    @pl.when(pl.program_id(0) == 0)
    def _():
        total[...] = part

    @pl.when(pl.program_id(0) == 1)
    def _():
        out_ref[...] = (total[...] + part).astype(jnp.bfloat16)


def heads_grad(grad, stacked):
    tokens, width = grad.shape
    half = width // 2
    return pl.pallas_call(
        heads_body,
        grid=(2,),
        in_specs=[
            pl.BlockSpec((tokens, half), lambda h: (0, h)),
            pl.BlockSpec((64, half // 64, half), lambda h: (0, h, 1)),
        ],
        out_specs=pl.BlockSpec((tokens, half), lambda h: (0, 0)),
        out_shape=jax.ShapeDtypeStruct((tokens, half), jnp.bfloat16),
        scratch_shapes=[pltpu.VMEM((tokens, half), jnp.float32)],
        compiler_params=pltpu.CompilerParams(vmem_limit_bytes=32 * 1024 * 1024),
    )(grad, stacked)


def share_body(core_ref, lows_ref, both_w_ref, value_w_ref, own_ref, other_ref):
    tokens = own_ref.shape[0]
    middle = both_w_ref.shape[1]
    first = pl.ds(pl.multiple_of(core_ref[0] * tokens, tokens), tokens)
    second = pl.ds(pl.multiple_of((1 - core_ref[0]) * tokens, tokens), tokens)
    for rows, out_ref in ((second, other_ref), (first, own_ref)):
        share = dot_nt(lows_ref[rows, :middle], both_w_ref[...]) + dot_nt(
            lows_ref[rows, middle:], value_w_ref[...]
        )
        out_ref[...] = share.astype(out_ref.dtype)


def input_shares(lows, both_w, value_w, core):
    tokens, width = lows.shape[0] // 2, both_w.shape[0]
    half, tile = value_w.shape[1] // 2, width // 8
    return pl.pallas_call(
        share_body,
        grid_spec=pltpu.PrefetchScalarGridSpec(
            num_scalar_prefetch=1,
            grid=(8,),
            in_specs=[
                pl.BlockSpec(lows.shape, lambda i, c: (0, 0)),
                pl.BlockSpec((tile, width), lambda i, c: (i, 0)),
                pl.BlockSpec((tile, half), lambda i, c: (i, 0)),
            ],
            out_specs=[pl.BlockSpec((tokens, tile), lambda i, c: (0, i))] * 2,
        ),
        out_shape=[
            jax.ShapeDtypeStruct((tokens, width), jnp.float32),
            jax.ShapeDtypeStruct((tokens, width), jnp.bfloat16),
        ],
        compiler_params=pltpu.CompilerParams(vmem_limit_bytes=32 * 1024 * 1024),
        cost_estimate=pl.CostEstimate(
            flops=24 * 1000 * 1000 * 1000, bytes_accessed=16 * 1024 * 1024, transcendentals=0
        ),
    )(core[None].astype(jnp.int32), lows, both_w, value_w)


def shards(
    block_entry_states,
    block_result_cotangent,
    token_assignments,
    packed_segment_sizes,
    admitted_route_quota,
    mixing_scale_factor,
    asker_projection,
    lookup_projection,
    content_projection,
    mixing_projection_back,
    asker_scale_factor,
    lookup_scale_factor,
    specialist_scale_factor,
    dispatcher_projection,
    specialist_switch_tensor,
    specialist_widen_tensor,
    specialist_shrink_tensor,
):
    bf16, f32 = jnp.bfloat16, jnp.float32
    tokens_dev = block_entry_states.shape[1]
    width = block_entry_states.shape[2]
    core = lax.axis_index("dp")
    me = lax.axis_index("expert")
    row_len = tokens_dev * 2
    heads_local = HEADS // 2
    head_width = width // HEADS
    half_width = width // 2
    score_scale = head_width ** (-0.5)
    experts = dispatcher_projection.shape[1]

    stacked_output = jnp.concatenate(
        [mixing_projection_back[:, :half_width], mixing_projection_back[:, half_width:]], axis=0
    )
    value_output = lax.all_gather(
        jnp.concatenate([content_projection, stacked_output], axis=1),
        "expert",
        axis=0,
        tiled=True,
    )
    stacked_output = value_output.reshape(64, width // 64, width)
    blocks = jnp.concatenate([asker_projection, lookup_projection], axis=1)
    for step in range(3):
        blocks = jnp.concatenate([blocks, permute_step(blocks, 0, step)], axis=0)
    cuts = (0, 768, 1408, 2048)
    pieces = [[blocks[:, cuts[k] : cuts[k + 1]]] for k in range(3)]
    for k in range(3):
        got = permute_step(pieces[k][0], k, 3)
        pieces[k] = [jnp.concatenate([pieces[k][0], got], axis=0)]
    for k in range(3):
        pieces[k].append(permute_step(pieces[k][0], k, 4))
    for k in range(3):
        pieces[k] += [permute_step(piece, k, 5) for piece in pieces[k]]
    orders = [relative_order(core, me, part) for part in range(3)]
    inverses = [natural_order(order) for order in orders]

    assigned = token_assignments[0]
    expert_iota = jnp.arange(experts, dtype=jnp.int32)
    chosen = jnp.any(assigned[:, :, None] == expert_iota[None, None, :], axis=1)
    token_iota = jnp.arange(tokens_dev, dtype=jnp.int32)
    earlier = (token_iota[:, None] > token_iota[None, :]).astype(bf16)
    rank = dot(earlier, chosen.astype(bf16))
    kept = chosen & (rank < admitted_route_quota.astype(f32)[None, :])
    sent_counts = jnp.sum(kept.astype(jnp.int32), axis=0, dtype=jnp.int32)
    line_iota = jnp.arange(experts * 8, dtype=jnp.int32)
    line = line_iota % 8
    spread = (expert_iota[:, None] == (line_iota // 8)[None, :]).astype(bf16)
    slot_of_line = dot(jnp.where(kept, rank, -1.0).astype(bf16), spread).astype(jnp.int32)
    main = (slot_of_line == line[None, :]).astype(bf16)
    spare_hit = slot_of_line == (8 + line // 2)[None, :]
    spare = jnp.concatenate(
        [spare_hit & (line % 2 == half)[None, :] for half in range(2)], axis=0
    ).astype(bf16)

    lengths = packed_segment_sizes[0]
    row_positions = jnp.arange(row_len, dtype=jnp.int32)
    doc_ids, doc_offset = doc_places(lengths, row_positions)
    allowed = (doc_ids[None, :] == doc_ids[:, None]) & (
        row_positions[None, :] <= row_positions[:, None]
    )
    cos_table, sin_table = rope_tables(doc_offset, head_width)
    head_shape = (row_len, heads_local, head_width)
    column_start = core * half_width
    query_half_gain = lax.dynamic_slice_in_dim(asker_scale_factor, column_start, half_width)
    key_half_gain = lax.dynamic_slice_in_dim(lookup_scale_factor, column_start, half_width)

    def whole_row(own):
        other = swap(own)
        return jnp.concatenate(
            [jnp.where(core == 0, own, other), jnp.where(core == 0, other, own)], axis=0
        )

    inputs = block_entry_states[0].astype(f32)
    factor_in = rms_factor(inputs)
    normed_in = (inputs * factor_in * mixing_scale_factor).astype(bf16)
    normed_t = whole_row(normed_in).T
    normed_rel = [reorder(normed_t, order) for order in orders]

    def project(left, pieces):
        size = width // len(pieces)
        return sum(dot_tn(left[i * size : (i + 1) * size], p) for i, p in enumerate(pieces))

    both_proj = jnp.concatenate([project(normed_rel[k], pieces[k]) for k in range(3)], axis=1)
    query_proj, key_proj = both_proj[:, :half_width], both_proj[:, half_width:]
    value_low = dot_tn(normed_t, value_output[:, :half_width]).astype(bf16).reshape(head_shape)
    grad_top_low = block_result_cotangent[0]
    send_grads, *_ = lax.optimization_barrier(
        (to_experts(main, spare, grad_top_low), *(pieces[k][-1] for k in range(3)))
    )
    arrived_grads = exchange(send_grads)
    query_sq, key_sq = lax.psum(
        (jnp.sum(query_proj * query_proj, axis=1), jnp.sum(key_proj * key_proj, axis=1)), "dp"
    )
    query_factor = lax.rsqrt(query_sq[:, None] / width + EPS)
    key_factor = lax.rsqrt(key_sq[:, None] / width + EPS)
    queries = rotate(
        (query_proj * query_factor * query_half_gain).reshape(head_shape), cos_table, sin_table
    ).astype(bf16)
    keys = rotate(
        (key_proj * key_factor * key_half_gain).reshape(head_shape), cos_table, sin_table
    ).astype(bf16)
    raw_scores = jnp.einsum("qhd,khd->hqk", queries, keys, preferred_element_type=f32) * score_scale
    attn_probs = softmax_rows(jnp.where(allowed[None], raw_scores, NEG))
    attn_low = attn_probs.astype(bf16)
    mixed_heads = (
        jnp.einsum("hqk,khd->qhd", attn_low, value_low, preferred_element_type=f32)
        .reshape(row_len, half_width)
        .astype(bf16)
    )
    hidden_own, share_other = output_shares(
        mixed_heads, stacked_output, block_entry_states[0], core
    )
    hidden = hidden_own + swap(share_other).astype(f32)
    factor_moe = rms_factor(hidden)
    normed_moe = (hidden * factor_moe * specialist_scale_factor).astype(bf16)

    arrived = exchange(to_experts(main, spare, normed_moe))
    *late_pieces, _ = lax.optimization_barrier((*pieces, normed_moe))
    both_w = jnp.concatenate(
        [reorder(jnp.concatenate(late_pieces[k], axis=0), inverses[k]) for k in range(3)], axis=1
    )
    both_w, arrived = lax.optimization_barrier((both_w, arrived))
    gate_w, up_w, down_w = (
        specialist_switch_tensor[0],
        specialist_widen_tensor[0],
        specialist_shrink_tensor[0],
    )
    top_rows = unpack(arrived_grads)
    plain_act_grad = dot_nt(top_rows, down_w)
    row_grad, rows_in, gate_pre_grad, up_pre_grad, gated_act, logit_grad = expert_rows(
        arrived, plain_act_grad, gate_w, up_w, dispatcher_projection, core, me
    )
    returned_grads = exchange(row_grad)
    send_out, returned_grads = lax.optimization_barrier(
        (expert_results(gated_act, down_w, core), returned_grads)
    )
    returned = exchange(send_out)

    def summed(left, right):
        return left + swap(right.astype(bf16)).astype(f32)

    gate_weight_grad = summed(dot_tn(rows_in, gate_pre_grad[0]), dot_tn(rows_in, gate_pre_grad[1]))
    up_weight_grad = summed(dot_tn(rows_in, up_pre_grad[0]), dot_tn(rows_in, up_pre_grad[1]))
    down_weight_grad = summed(dot_tn(gated_act[0], top_rows), dot_tn(gated_act[1], top_rows))

    moe_in_grad = from_experts(main, spare, returned_grads)
    hidden_norm_grad, moe_gain_local = norm_back(
        moe_in_grad, hidden, factor_moe, specialist_scale_factor
    )
    hidden_grad = grad_top_low.astype(f32) + hidden_norm_grad
    grad_full = whole_row(hidden_grad.astype(bf16))
    mixed_grad = heads_grad(grad_full, stacked_output).reshape(head_shape)
    mixed_rel = reorder(mixed_heads.T, orders[0])
    output_rows, output_got = width // 128, []
    for step in reversed(range(STEPS)):
        low, high = 1 << step, 2 << step
        piece = dot(mixed_rel[low * output_rows : high * output_rows], grad_full)
        for g in output_got:
            piece = piece + g[low * output_rows : high * output_rows].astype(f32)
        output_got.append(permute_step(piece.astype(bf16), 0, step))
    output_weight_grad = dot(mixed_rel[:output_rows], grad_full)
    for g in output_got:
        output_weight_grad = output_weight_grad + g[:output_rows].astype(f32)
    prob_grad_att = jnp.einsum("qhd,khd->hqk", mixed_grad, value_low, preferred_element_type=f32)
    score_grad = (
        attn_probs * (prob_grad_att - jnp.sum(attn_probs * prob_grad_att, axis=-1, keepdims=True))
    ).astype(bf16)
    value_grad = jnp.einsum("hqk,qhd->khd", attn_low, mixed_grad, preferred_element_type=f32)
    query_rot_grad = (
        jnp.einsum("hqk,khd->qhd", score_grad, keys, preferred_element_type=f32) * score_scale
    )
    key_rot_grad = (
        jnp.einsum("hqk,qhd->khd", score_grad, queries, preferred_element_type=f32) * score_scale
    )
    query_norm_grad = unrotate(query_rot_grad, cos_table, sin_table).reshape(row_len, half_width)
    key_norm_grad = unrotate(key_rot_grad, cos_table, sin_table).reshape(row_len, half_width)
    query_scaled = query_norm_grad * query_half_gain
    key_scaled = key_norm_grad * key_half_gain
    query_inner, key_inner = lax.psum(
        (jnp.sum(query_scaled * query_proj, axis=1), jnp.sum(key_scaled * key_proj, axis=1)), "dp"
    )
    query_low = (
        query_factor
        * (query_scaled - query_proj * query_factor * query_factor * (query_inner[:, None] / width))
    ).astype(bf16)
    key_low = (
        key_factor
        * (key_scaled - key_proj * key_factor * key_factor * (key_inner[:, None] / width))
    ).astype(bf16)
    value_proj_low = value_grad.reshape(row_len, half_width).astype(bf16)
    empty_gain = jnp.zeros((width,), f32)
    query_gain_local = lax.dynamic_update_slice_in_dim(
        empty_gain, jnp.sum(query_norm_grad * query_proj * query_factor, axis=0), column_start, 0
    )
    key_gain_local = lax.dynamic_update_slice_in_dim(
        empty_gain, jnp.sum(key_norm_grad * key_proj * key_factor, axis=0), column_start, 0
    )
    lows = (query_low, key_low, value_proj_low)

    def left_of(k, low, high):
        return normed_rel[k][low * (width // 64) : high * (width // 64)]

    sent = [dot(left_of(k, 32, 64), lows[k]).astype(bf16) for k in range(3)]
    *sent, share_lows, returned = lax.optimization_barrier((*sent, lows, returned))
    share_own, share_other = input_shares(
        jnp.concatenate(share_lows, axis=1), both_w, value_output, core
    )
    got = [[permute_step(sent[k], k, 5)] for k in range(3)]
    rows = width // 64
    for step in (4, 3):
        low, high = 1 << step, 2 << step
        for k in range(3):
            piece = dot(left_of(k, low, high), lows[k])
            for g in got[k]:
                piece = piece + g[low * rows : high * rows].astype(f32)
            got[k].append(permute_step(piece.astype(bf16), k, step))
    near = [sum(g[: 8 * rows].astype(f32) for g in got[k]) for k in range(3)]
    projection_grads, output_weight_grad = lax.optimization_barrier(
        (jnp.concatenate(near, axis=1), output_weight_grad)
    )
    low_all = jnp.concatenate(lows, axis=1)
    for step in (2, 1, 0):
        low, high = 1 << step, 2 << step
        piece = dot(left_of(0, low, high), low_all) + projection_grads[low * rows :]
        projection_grads = projection_grads[: low * rows] + permute_step(
            piece.astype(bf16), 0, step
        ).astype(f32)
    projection_grads = projection_grads + dot(left_of(0, 0, 1), low_all)
    block_output = hidden + from_experts(main, spare, returned)
    normed_in_grad = share_own + swap(share_other).astype(f32)
    input_norm_grad, attn_gain_local = norm_back(
        normed_in_grad, inputs, factor_in, mixing_scale_factor
    )
    input_grad = hidden_grad + input_norm_grad

    own_counts = jnp.where(
        (jnp.arange(2)[:, None, None] == core) & (expert_iota[None, :, None] == me),
        sent_counts[None, None, :],
        0,
    ).astype(f32)
    totals = sum_everywhere(
        jnp.concatenate(
            [
                dot_tn(logit_grad, rows_in),
                own_counts.reshape(2 * experts * experts // width, width),
                jnp.stack([attn_gain_local, query_gain_local, key_gain_local, moe_gain_local]),
            ]
        ),
        core,
        1,
    )
    router_weight_grad, all_counts, gains = totals[:experts].T, totals[experts:-4], totals[-4:]
    got_counts = jnp.sum(
        jnp.where(
            (jnp.arange(2)[:, None, None] == core) & (expert_iota[None, None, :] == me),
            all_counts.reshape(2, experts, experts),
            0.0,
        ),
        axis=(0, 2),
    ).astype(jnp.int32)
    return (
        block_output[None],
        input_grad[None],
        gains[0],
        projection_grads[:, :half_width],
        projection_grads[:, half_width : 2 * half_width],
        projection_grads[:, 2 * half_width :],
        output_weight_grad,
        gains[1],
        gains[2],
        gains[3],
        router_weight_grad,
        gate_weight_grad[None],
        up_weight_grad[None],
        down_weight_grad[None],
        got_counts[None],
    )


def solution(mesh):
    placed = (
        P("expert", "dp", None),
        P("expert", "dp", None),
        P("expert", "dp", None),
        P("expert", None),
        P(),
        P(),
        P("expert", "dp"),
        P("expert", "dp"),
        P("expert", "dp"),
        P(("dp", "expert"), None),
        P(),
        P(),
        P(),
        P(),
        P("expert", None, None),
        P("expert", None, None),
        P("expert", None, None),
    )
    return jax.shard_map(
        shards,
        mesh=mesh,
        in_specs=placed,
        out_specs=(
            P("expert", "dp", None),
            P("expert", "dp", None),
            P(),
            P("expert", "dp"),
            P("expert", "dp"),
            P("expert", "dp"),
            P(("dp", "expert"), None),
            P(),
            P(),
            P(),
            P(),
            P("expert", None, "dp"),
            P("expert", None, "dp"),
            P("expert", "dp", None),
            P("expert", "dp"),
        ),
        check_vma=False,
    )
```

```python
import functools

import jax
import jax.numpy as jnp
from jax import lax
from jax.experimental import pallas as pl
from jax.experimental.pallas import tpu as pltpu
from jax.sharding import PartitionSpec as P

HEADS = 16
EPS = 1e-05
THETA = 10000.0
NEG = -1e30
BOTH = ("dp", "expert")

FLIPS = ((1, 4, 16), (3, 12, 48))
STEPS = 6


def flip_of(core, part, step):
    return FLIPS[core][step] if step < 3 else FLIPS[1 - core][(step + part) % 3]


def mask_of(core, part, index):
    mask = 0
    for step in range(STEPS):
        if (index >> step) & 1:
            mask ^= flip_of(core, part, step)
    return mask


def permute_step(value, part, step):
    pairs = []
    for core in range(2):
        flip = flip_of(core, part, step)
        pairs += [(64 * core + d, 64 * core + (d ^ flip)) for d in range(64)]
    return lax.ppermute(value, BOTH, pairs)


def relative_order(core, me, part):
    tables = [jnp.array([mask_of(c, part, r) for r in range(64)], jnp.int32) for c in range(2)]
    return jnp.where(core == 0, tables[0], tables[1]) ^ me


def reorder_body(order_ref, rows_ref, out_ref):
    for k in range(out_ref.shape[0]):
        for r in range(64):
            out_ref[k, r] = rows_ref[order_ref[k, r]]


def reorder(rows, orders):
    blocks = rows.reshape(64, rows.shape[0] // 64, rows.shape[1])
    count = orders.shape[0]
    out = pl.pallas_call(
        reorder_body,
        grid_spec=pltpu.PrefetchScalarGridSpec(
            num_scalar_prefetch=1,
            grid=(1,),
            in_specs=[pl.BlockSpec(blocks.shape, lambda i, o: (0, 0, 0))],
            out_specs=pl.BlockSpec((count, *blocks.shape), lambda i, o: (0, 0, 0, 0)),
        ),
        out_shape=jax.ShapeDtypeStruct((count, *blocks.shape), rows.dtype),
        compiler_params=pltpu.CompilerParams(vmem_limit_bytes=32 * 1024 * 1024),
    )(orders, blocks)
    return [out[k].reshape(rows.shape) for k in range(count)]


def collect_body(cuts, order_ref, *refs):
    pieces, out_ref = refs[:-1], refs[-1]
    count = len(pieces) // (len(cuts) - 1)
    per = 64 // count
    for k in range(len(cuts) - 1):
        for r in range(64):
            rows = pl.ds(pl.multiple_of(order_ref[k, r] * 32, 32), 32)
            out_ref[rows, cuts[k] : cuts[k + 1]] = pieces[k * count + r // per][
                (r % per) * 32 : (r % per + 1) * 32, :
            ]


def collect(pieces, cuts, orders):
    flat = [piece for part in pieces for piece in part]
    return pl.pallas_call(
        functools.partial(collect_body, cuts),
        grid_spec=pltpu.PrefetchScalarGridSpec(
            num_scalar_prefetch=1,
            grid=(1,),
            in_specs=[pl.BlockSpec(a.shape, lambda i, o: (0, 0)) for a in flat],
            out_specs=pl.BlockSpec((64 * 32, cuts[-1]), lambda i, o: (0, 0)),
        ),
        out_shape=jax.ShapeDtypeStruct((64 * 32, cuts[-1]), jnp.bfloat16),
        compiler_params=pltpu.CompilerParams(vmem_limit_bytes=56 * 1024 * 1024),
    )(orders, *flat)


def half_of(rows, core):
    half = rows.shape[1] // 2
    own = lax.dynamic_slice_in_dim(rows, core * half, half, axis=1)
    return own + swap(lax.dynamic_slice_in_dim(rows, (1 - core) * half, half, axis=1))


def beside_other_half(own, core):
    other = swap(own)
    return jnp.concatenate(
        [jnp.where(core == 0, own, other), jnp.where(core == 0, other, own)], axis=1
    )


def swap(value):
    return lax.ppermute(value, "dp", [(0, 1), (1, 0)])


def spanned(flips):
    masks = [0]
    for flip in flips:
        masks += [mask ^ flip for mask in masks]
    return masks


def near_groups():
    groups = []
    for core in range(2):
        masks = spanned(FLIPS[core])
        for d in range(64):
            if d == min(d ^ mask for mask in masks):
                groups.append([64 * core + (d ^ mask) for mask in masks])
    return groups


def near_position(core, me):
    low = (me & 1) | ((me >> 2) & 1) << 1 | ((me >> 4) & 1) << 2
    high = ((me >> 1) & 1) | ((me >> 3) & 1) << 1 | ((me >> 5) & 1) << 2
    return jnp.where(core == 0, low, high)


def dot(left, right):
    return jnp.dot(left, right, preferred_element_type=jnp.float32)


def dot_tn(left, right):
    return lax.dot_general(
        left, right, (((0,), (0,)), ((), ())), preferred_element_type=jnp.float32
    )


def dot_nt(left, right):
    return lax.dot_general(
        left, right, (((1,), (1,)), ((), ())), preferred_element_type=jnp.float32
    )


def rms_factor(values):
    return lax.rsqrt(jnp.mean(values * values, axis=-1, keepdims=True) + EPS)


def norm_back(grad_normed, source, factor, gain):
    scaled = grad_normed * gain
    grad_source = factor * (
        scaled - source * factor * factor * jnp.mean(scaled * source, axis=-1, keepdims=True)
    )
    grad_gain = jnp.sum(grad_normed * source * factor, axis=0)
    return (grad_source, grad_gain)


def doc_places(lengths, places):
    ends = jnp.cumsum(lengths, dtype=jnp.int32)
    done = ends[None, :] <= places[:, None]
    doc_ids = jnp.sum(done.astype(jnp.int32), axis=1, dtype=jnp.int32)
    starts = jnp.sum(jnp.where(done, lengths[None, :], 0), axis=1, dtype=jnp.int32)
    return (doc_ids, places - starts)


def rope_tables(offsets, head_width):
    half_width = head_width // 2
    inverse = THETA ** (-jnp.arange(half_width, dtype=jnp.float32) * 2.0 / head_width)
    angles = offsets.astype(jnp.float32)[..., None] * inverse
    return (jnp.cos(angles)[..., None, :], jnp.sin(angles)[..., None, :])


def rotate(values, cos_table, sin_table):
    half_width = values.shape[-1] // 2
    first, second = (values[..., :half_width], values[..., half_width:])
    return jnp.concatenate(
        [first * cos_table - second * sin_table, second * cos_table + first * sin_table], axis=-1
    )


def unrotate(grads, cos_table, sin_table):
    half_width = grads.shape[-1] // 2
    first, second = (grads[..., :half_width], grads[..., half_width:])
    return jnp.concatenate(
        [first * cos_table + second * sin_table, second * cos_table - first * sin_table], axis=-1
    )


def softmax_rows(values):
    exponent = jnp.exp(values - jnp.max(values, axis=-1, keepdims=True))
    return exponent / jnp.sum(exponent, axis=-1, keepdims=True)


def half_picker(count, half):
    rows = lax.broadcasted_iota(jnp.int32, (count // 2, count), 0)
    cols = lax.broadcasted_iota(jnp.int32, (count // 2, count), 1)
    return (cols == 2 * rows + half).astype(jnp.float32).astype(jnp.bfloat16)


def unpack_block(packed):
    count, width = packed.shape[0], packed.shape[1] * 2 // 3
    spare = packed[:, width:]
    rest = [dot(half_picker(count, h), spare).astype(jnp.bfloat16) for h in range(2)]
    return packed[:, :width], rest


def pack_block(rows, out_ref):
    count, width = out_ref.shape[0], rows.shape[1]
    half = width // 2
    out_ref[:, :width] = rows[:count]
    out_ref[:, width : width + half] = (
        dot_tn(half_picker(count, 0), rows[count:, :half])
        + dot_tn(half_picker(count, 1), rows[count:, half:])
    ).astype(jnp.bfloat16)


def unpack_body(packed_ref, rows_ref):
    main, rest = unpack_block(packed_ref[...])
    count, width = main.shape
    rows_ref[:count] = main
    rows_ref[count:, : width // 2] = rest[0]
    rows_ref[count:, width // 2 :] = rest[1]


def unpack(packed):
    count, width = packed.shape[0], packed.shape[1] * 2 // 3
    return pl.pallas_call(
        unpack_body,
        out_shape=jax.ShapeDtypeStruct((count * 3 // 2, width), jnp.bfloat16),
        compiler_params=pltpu.CompilerParams(vmem_limit_bytes=56 * 1024 * 1024),
    )(packed)


def send_body(main_ref, spare_ref, rows_ref, out_ref):
    width = rows_ref.shape[1]
    half, count = width // 2, rows_ref.shape[0]
    out_ref[:, :width] = dot_tn(main_ref[...], rows_ref[...]).astype(jnp.bfloat16)
    out_ref[:, width:] = (
        dot_tn(spare_ref[:count], rows_ref[:, :half])
        + dot_tn(spare_ref[count:], rows_ref[:, half:])
    ).astype(jnp.bfloat16)


def to_experts(main, spare, rows):
    tokens, lines = main.shape
    width, block = rows.shape[1], lines // 2
    return pl.pallas_call(
        send_body,
        grid=(2,),
        in_specs=[
            pl.BlockSpec((tokens, block), lambda i: (0, i)),
            pl.BlockSpec((2 * tokens, block), lambda i: (0, i)),
            pl.BlockSpec((tokens, width), lambda i: (0, 0)),
        ],
        out_specs=pl.BlockSpec((block, width * 3 // 2), lambda i: (i, 0)),
        out_shape=jax.ShapeDtypeStruct((lines, width * 3 // 2), jnp.bfloat16),
        compiler_params=pltpu.CompilerParams(vmem_limit_bytes=56 * 1024 * 1024),
    )(main, spare, rows)


def combine_body(main_ref, spare_ref, lines_ref, out_ref):
    tokens, width = out_ref.shape
    half = width // 2
    spare_lines = lines_ref[:, width : width + half]
    out_ref[:, :half] = dot(main_ref[...], lines_ref[:, :half]) + dot(
        spare_ref[:tokens], spare_lines
    )
    out_ref[:, half:] = dot(main_ref[...], lines_ref[:, half:width]) + dot(
        spare_ref[tokens:], spare_lines
    )


def from_experts(main, spare, lines, width):
    return pl.pallas_call(
        combine_body,
        out_shape=jax.ShapeDtypeStruct((main.shape[0], width), jnp.float32),
        compiler_params=pltpu.CompilerParams(vmem_limit_bytes=56 * 1024 * 1024),
    )(main, spare, lines)


def out_body(core_ref, act_ref, own_ref, other_ref, extra_ref, out_ref):
    rows = dot(act_ref[0], own_ref[...]) + dot(act_ref[1], other_ref[...])
    pack_block(rows.astype(jnp.bfloat16), out_ref)
    out_ref[:, rows.shape[1] * 3 // 2 :] = extra_ref[...]


def expert_results(acts, down_w, extra, core):
    _, count, units = acts.shape
    width = down_w.shape[1]
    shape = (count * 2 // 3, width * 3 // 2 + extra.shape[1])
    return pl.pallas_call(
        out_body,
        grid_spec=pltpu.PrefetchScalarGridSpec(
            num_scalar_prefetch=1,
            grid=(1,),
            in_specs=[
                pl.BlockSpec((2, count, units), lambda i, c: (0, 0, 0)),
                pl.BlockSpec((units, width), lambda i, c: (c[0], 0)),
                pl.BlockSpec((units, width), lambda i, c: (1 - c[0], 0)),
                pl.BlockSpec(extra.shape, lambda i, c: (0, 0)),
            ],
            out_specs=pl.BlockSpec(shape, lambda i, c: (0, 0)),
        ),
        out_shape=jax.ShapeDtypeStruct(shape, jnp.bfloat16),
        compiler_params=pltpu.CompilerParams(vmem_limit_bytes=56 * 1024 * 1024),
        cost_estimate=pl.CostEstimate(
            flops=4 * count * width * units, bytes_accessed=12 * 1024 * 1024, transcendentals=0
        ),
    )(core[None].astype(jnp.int32), acts, down_w, down_w, extra)


def expert_body(
    core_ref, mine_ref, packed_ref, act_grad_ref, gate_w_ref, up_w_ref, router_ref,
    back_ref, x_out, gate_out_ref, up_out_ref, act_out_ref, logit_ref,
    x_ref, total, probs_ref, gate_ref, gate_grad_ref, sem,
):
    f32, bf16 = jnp.float32, jnp.bfloat16
    step = pl.program_id(0)
    x_copy = pltpu.make_async_copy(x_ref, x_out, sem)

    @pl.when(step == 0)
    def _():
        unpack_body(packed_ref, x_ref)
        x_copy.start()
        probs = softmax_rows(dot(x_ref[...], router_ref[...]))
        probs_ref[...] = probs
        gate_ref[...] = jnp.sum(probs * mine_ref[...], axis=1, keepdims=True)
        gate_grad_ref[...] = jnp.zeros_like(gate_grad_ref)
        total[...] = jnp.zeros_like(total)

    gate_w, up_w = gate_w_ref[...], up_w_ref[...]
    size = x_ref.shape[0] // 3
    for k in range(3):
        rows = pl.ds(k * size, size)
        x, gate = x_ref[rows, :], gate_ref[rows, :]
        gate_pre, up_pre = dot(x, gate_w), dot(x, up_w)
        plain = act_grad_ref[rows, :].astype(f32)
        sigmoid = 1.0 / (1.0 + jnp.exp(-gate_pre))
        silu = gate_pre * sigmoid
        act = silu * up_pre
        gate_grad = jnp.sum(act * plain, axis=1, keepdims=True)
        act_grad = gate * plain
        gate_pre_grad = (act_grad * up_pre * sigmoid * (1.0 + gate_pre * (1.0 - sigmoid))).astype(
            bf16
        )
        up_pre_grad = (act_grad * silu).astype(bf16)
        gate_out_ref[0, rows, :] = gate_pre_grad
        up_out_ref[0, rows, :] = up_pre_grad
        act_out_ref[0, rows, :] = (gate * act).astype(bf16)
        part = dot_nt(gate_pre_grad, gate_w) + dot_nt(up_pre_grad, up_w)

        gate_grad_ref[rows, :] += gate_grad
        total[rows, :] += part

    @pl.when(step == pl.num_programs(0) - 1)
    def _():
        logit = (gate_grad_ref[...] * gate_ref[...] * (mine_ref[...] - probs_ref[...])).astype(bf16)
        logit_ref[...] = logit
        pack_block((total[...] + dot_nt(logit, router_ref[...])).astype(bf16), back_ref)
        x_copy.wait()


def expert_rows(packed, plain_act_grad, gate_w, up_w, router, core, me):
    f32, bf16 = jnp.float32, jnp.bfloat16
    lines = packed.shape[0]
    width, units = gate_w.shape
    count, experts = lines * 3 // 2, router.shape[1]
    tile = units // 4
    mine = (jnp.arange(experts, dtype=jnp.int32) == me).astype(f32)[None, :]
    halves = jax.ShapeDtypeStruct((2, count, units // 2), bf16)
    half_spec = pl.BlockSpec((1, count, tile), lambda j, c: ((j // 2 + c[0]) % 2, 0, j % 2))
    return pl.pallas_call(
        expert_body,
        grid_spec=pltpu.PrefetchScalarGridSpec(
            num_scalar_prefetch=1,
            grid=(4,),
            in_specs=[
                pl.BlockSpec((1, experts), lambda j, c: (0, 0)),
                pl.BlockSpec(packed.shape, lambda j, c: (0, 0)),
                pl.BlockSpec((count, tile), lambda j, c: (0, j)),
                pl.BlockSpec((width, tile), lambda j, c: (0, j)),
                pl.BlockSpec((width, tile), lambda j, c: (0, j)),
                pl.BlockSpec((width, experts), lambda j, c: (0, 0)),
            ],
            out_specs=[
                pl.BlockSpec(packed.shape, lambda j, c: (0, 0)),
                pl.BlockSpec(memory_space=pl.ANY),
                half_spec,
                half_spec,
                half_spec,
                pl.BlockSpec((count, experts), lambda j, c: (0, 0)),
            ],
            scratch_shapes=[
                pltpu.VMEM((count, width), bf16),
                pltpu.VMEM((count, width), f32),
                pltpu.VMEM((count, experts), f32),
                pltpu.VMEM((count, 1), f32),
                pltpu.VMEM((count, 1), f32),
                pltpu.SemaphoreType.DMA,
            ],
        ),
        out_shape=[
            jax.ShapeDtypeStruct(packed.shape, bf16),
            jax.ShapeDtypeStruct((count, width), bf16),
            halves,
            halves,
            halves,
            jax.ShapeDtypeStruct((count, experts), bf16),
        ],
        compiler_params=pltpu.CompilerParams(vmem_limit_bytes=60 * 1024 * 1024),
        cost_estimate=pl.CostEstimate(
            flops=8 * count * width * units, bytes_accessed=24 * 1024 * 1024, transcendentals=count * units
        ),
    )(core[None].astype(jnp.int32), mine, packed, plain_act_grad, gate_w, up_w, router)


PARTS = ((0, 384), (384, 768), (768, 1024))
OFFSETS = (0, 1408, 2816, 4096)


def part_sums(part, left, low, heads, grad, got):
    start, stop = PARTS[part]
    blocks = left.shape[0] // 32
    half = grad.shape[1] // 2
    main = dot(left, low).reshape(blocks, 32, low.shape[1])
    sides = [
        dot(heads, grad[:, h * half + start : h * half + stop]).reshape(blocks, 16, stop - start)
        for h in range(2)
    ]
    for g in got:
        main = main + g[:, :, : low.shape[1]].astype(jnp.float32)
        sides = [
            sides[h] + g[:, 16 * h : 16 * h + 16, low.shape[1] :].astype(jnp.float32)
            for h in range(2)
        ]
    return main, sides


def sent_body(count, *refs):
    lefts, lows, heads, grad = refs[:3], refs[3:6], refs[6:9], refs[9][...]
    got, outs = refs[10 : 10 + 3 * count], refs[10 + 3 * count :]
    for k in range(3):
        main, sides = part_sums(
            k, lefts[k][...], lows[k][...], heads[k][...], grad,
            [g[...] for g in got[k * count : (k + 1) * count]],
        )
        width = main.shape[2]
        outs[k][:, :, :width] = main.astype(jnp.bfloat16)
        for h in range(2):
            outs[k][:, 16 * h : 16 * h + 16, width:] = sides[h].astype(jnp.bfloat16)


def sent_pieces(step, lefts, lows, heads, grad, got):
    blocks = 1 << step
    chunk = min(blocks, 8)
    first = blocks // chunk
    count = len(got[0])
    ahead = lambda i: (first + i, 0)
    ahead3 = lambda i: (first + i, 0, 0)
    fixed = lambda i: (0, 0)
    columns = [OFFSETS[k + 1] - OFFSETS[k] for k in range(3)]
    return pl.pallas_call(
        functools.partial(sent_body, count),
        grid=(blocks // chunk,),
        in_specs=[pl.BlockSpec((chunk * 32, a.shape[1]), ahead) for a in lefts]
        + [pl.BlockSpec(a.shape, fixed) for a in lows]
        + [pl.BlockSpec((chunk * 16, a.shape[1]), ahead) for a in heads]
        + [pl.BlockSpec(grad.shape, fixed)]
        + [pl.BlockSpec((chunk, 32, columns[k]), ahead3) for k in range(3) for _ in range(count)],
        out_specs=[pl.BlockSpec((chunk, 32, c), lambda i: (i, 0, 0)) for c in columns],
        out_shape=[jax.ShapeDtypeStruct((blocks, 32, c), jnp.bfloat16) for c in columns],
        compiler_params=pltpu.CompilerParams(
            vmem_limit_bytes=(32 if step == 5 else 56) * 1024 * 1024
        ),
    )(*lefts, *lows, *heads, grad, *(g for k in range(3) for g in got[k]))


def near_body(place_ref, left_ref, *refs):
    lows, heads_ref, grad_ref, got, out_ref = refs[:3], refs[3], refs[4], refs[5:14], refs[14]
    for k in range(3):
        main, sides = part_sums(
            k, left_ref[...], lows[k][...], heads_ref[...], grad_ref[...],
            [g[...] for g in got[3 * k : 3 * k + 3]],
        )
        width, start, stop = main.shape[2], OFFSETS[k], OFFSETS[k + 1]
        for r in range(8):
            place = place_ref[0] ^ r
            out_ref[place, :, start : start + width] = main[r].astype(jnp.bfloat16)
            for h in range(2):
                out_ref[place, 16 * h : 16 * h + 16, start + width : stop] = sides[h][r].astype(
                    jnp.bfloat16
                )


def near_pieces(place, left, lows, heads, grad, got):
    return pl.pallas_call(
        near_body,
        grid_spec=pltpu.PrefetchScalarGridSpec(
            num_scalar_prefetch=1,
            grid=(1,),
            in_specs=[pl.BlockSpec((8 * 32, left.shape[1]), lambda i, c: (0, 0))]
            + [pl.BlockSpec(a.shape, lambda i, c: (0, 0)) for a in lows]
            + [
                pl.BlockSpec((8 * 16, heads.shape[1]), lambda i, c: (0, 0)),
                pl.BlockSpec(grad.shape, lambda i, c: (0, 0)),
            ]
            + [
                pl.BlockSpec((8, 32, g.shape[2]), lambda i, c: (0, 0, 0))
                for k in range(3)
                for g in got[k]
            ],
            out_specs=pl.BlockSpec((8, 32, OFFSETS[3]), lambda i, c: (0, 0, 0)),
        ),
        out_shape=jax.ShapeDtypeStruct((8, 32, OFFSETS[3]), jnp.bfloat16),
        compiler_params=pltpu.CompilerParams(vmem_limit_bytes=56 * 1024 * 1024),
    )(place[None].astype(jnp.int32), left, *lows, heads, grad, *(g for k in range(3) for g in got[k]))


def total_body(near_ref, *outs):
    out_ref = outs[3]
    half = out_ref.shape[1] // 2
    for k in range(3):
        start, stop = OFFSETS[k], OFFSETS[k + 1]
        total = near_ref[0, :, start:stop].astype(jnp.float32)
        for r in range(1, near_ref.shape[0]):
            total = total + near_ref[r, :, start:stop].astype(jnp.float32)
        outs[k][...] = total[:, :half]
        for h in range(2):
            out_ref[:, h * half + PARTS[k][0] : h * half + PARTS[k][1]] = total[
                16 * h : 16 * h + 16, half:
            ]


def near_total(near):
    rows, half = near.shape[1], 1024
    return pl.pallas_call(
        total_body,
        out_shape=[jax.ShapeDtypeStruct((rows, half), jnp.float32)] * 3
        + [jax.ShapeDtypeStruct((rows // 2, 2 * half), jnp.float32)],
        compiler_params=pltpu.CompilerParams(vmem_limit_bytes=56 * 1024 * 1024),
    )(near)


def exchange(rows):
    return lax.all_to_all(rows, "expert", split_axis=0, concat_axis=0, tiled=True)


def own_and_other(core_ref, total, own_ref, other_ref):
    count = own_ref.shape[0]
    own_ref[...] = total[pl.ds(pl.multiple_of(core_ref[0] * count, count), count), :]
    other_ref[...] = total[
        pl.ds(pl.multiple_of((1 - core_ref[0]) * count, count), count), :
    ].astype(other_ref.dtype)


def output_body(core_ref, heads_ref, weight_ref, inputs_ref, own_ref, other_ref, total):
    half = own_ref.shape[1]
    total[...] = dot(heads_ref[...], weight_ref[...].reshape(half, half))
    own_and_other(core_ref, total, own_ref, other_ref)
    own_ref[...] += inputs_ref[...].astype(jnp.float32)


def output_shares(heads, stacked, inputs, core):
    tokens, width = inputs.shape
    half = width // 2
    return pl.pallas_call(
        output_body,
        grid_spec=pltpu.PrefetchScalarGridSpec(
            num_scalar_prefetch=1,
            grid=(2,),
            in_specs=[
                pl.BlockSpec((2 * tokens, half), lambda h, c: (0, 0)),
                pl.BlockSpec((64, half // 64, half), lambda h, c: (0, h, 1)),
                pl.BlockSpec((tokens, half), lambda h, c: (0, h)),
            ],
            out_specs=[pl.BlockSpec((tokens, half), lambda h, c: (0, h))] * 2,
            scratch_shapes=[pltpu.VMEM((2 * tokens, half), jnp.float32)],
        ),
        out_shape=[
            jax.ShapeDtypeStruct((tokens, width), jnp.float32),
            jax.ShapeDtypeStruct((tokens, width), jnp.bfloat16),
        ],
        compiler_params=pltpu.CompilerParams(vmem_limit_bytes=56 * 1024 * 1024),
    )(core[None].astype(jnp.int32), heads, stacked, inputs)


def heads_body(grad_ref, weight_ref, out_ref, total):
    half = out_ref.shape[1]
    part = dot_nt(grad_ref[...], weight_ref[...].reshape(half, half))

    @pl.when(pl.program_id(0) == 0)
    def _():
        total[...] = part

    @pl.when(pl.program_id(0) == 1)
    def _():
        out_ref[...] = (total[...] + part).astype(jnp.bfloat16)


def heads_grad(grad, stacked):
    tokens, width = grad.shape
    half = width // 2
    return pl.pallas_call(
        heads_body,
        grid=(2,),
        in_specs=[
            pl.BlockSpec((tokens, half), lambda h: (0, h)),
            pl.BlockSpec((64, half // 64, half), lambda h: (0, h, 1)),
        ],
        out_specs=pl.BlockSpec((tokens, half), lambda h: (0, 0)),
        out_shape=jax.ShapeDtypeStruct((tokens, half), jnp.bfloat16),
        scratch_shapes=[pltpu.VMEM((tokens, half), jnp.float32)],
        compiler_params=pltpu.CompilerParams(vmem_limit_bytes=56 * 1024 * 1024),
    )(grad, stacked)


def share_body(
    core_ref, query_ref, key_ref, value_ref, scaled_ref, both_w_ref, value_w_ref,
    own_ref, other_ref, gain_ref, total,
):
    middle = both_w_ref.shape[1] // 2
    total[...] = (
        dot_nt(query_ref[...], both_w_ref[:, :middle])
        + dot_nt(key_ref[...], both_w_ref[:, middle:])
        + dot_nt(value_ref[...], value_w_ref[...])
    )
    own_and_other(core_ref, total, own_ref, other_ref)
    gain_ref[...] = jnp.sum(
        total[...] * scaled_ref[...].astype(jnp.float32), axis=0, keepdims=True
    )


def input_shares(lows, scaled, both_w, value_w, core):
    tokens, width = lows[0].shape[0] // 2, both_w.shape[0]
    half, tile = value_w.shape[1] // 2, width // 8
    return pl.pallas_call(
        share_body,
        grid_spec=pltpu.PrefetchScalarGridSpec(
            num_scalar_prefetch=1,
            grid=(8,),
            in_specs=[
                *(pl.BlockSpec(a.shape, lambda i, c: (0, 0)) for a in lows),
                pl.BlockSpec((2 * tokens, tile), lambda i, c: (0, i)),
                pl.BlockSpec((tile, width), lambda i, c: (i, 0)),
                pl.BlockSpec((tile, half), lambda i, c: (i, 0)),
            ],
            out_specs=[pl.BlockSpec((tokens, tile), lambda i, c: (0, i))] * 2
            + [pl.BlockSpec((1, tile), lambda i, c: (0, i))],
            scratch_shapes=[pltpu.VMEM((2 * tokens, tile), jnp.float32)],
        ),
        out_shape=[
            jax.ShapeDtypeStruct((tokens, width), jnp.float32),
            jax.ShapeDtypeStruct((tokens, width), jnp.bfloat16),
            jax.ShapeDtypeStruct((1, width), jnp.float32),
        ],
        compiler_params=pltpu.CompilerParams(vmem_limit_bytes=56 * 1024 * 1024),
        cost_estimate=pl.CostEstimate(
            flops=4 * 1000 * 1000 * 1000, bytes_accessed=16 * 1024 * 1024, transcendentals=0
        ),
    )(core[None].astype(jnp.int32), *lows, scaled, both_w, value_w)


def shards(
    block_entry_states,
    block_result_cotangent,
    token_assignments,
    packed_segment_sizes,
    admitted_route_quota,
    mixing_scale_factor,
    asker_projection,
    lookup_projection,
    content_projection,
    mixing_projection_back,
    asker_scale_factor,
    lookup_scale_factor,
    specialist_scale_factor,
    dispatcher_projection,
    specialist_switch_tensor,
    specialist_widen_tensor,
    specialist_shrink_tensor,
):
    bf16, f32 = jnp.bfloat16, jnp.float32
    tokens_dev = block_entry_states.shape[1]
    width = block_entry_states.shape[2]
    core = lax.axis_index("dp")
    me = lax.axis_index("expert")
    row_len = tokens_dev * 2
    heads_local = HEADS // 2
    head_width = width // HEADS
    half_width = width // 2
    score_scale = head_width ** (-0.5)
    experts = dispatcher_projection.shape[1]

    stacked_output = jnp.concatenate(
        [mixing_projection_back[:, :half_width], mixing_projection_back[:, half_width:]], axis=0
    )
    value_output = lax.all_gather(
        jnp.concatenate([content_projection, stacked_output], axis=1),
        "expert",
        axis=0,
        tiled=True,
    )
    stacked_output = value_output.reshape(64, width // 64, width)
    blocks = jnp.concatenate([asker_projection, lookup_projection], axis=1)
    for step in range(3):
        blocks = jnp.concatenate([blocks, permute_step(blocks, 0, step)], axis=0)
    cuts = (0, 768, 1408, 2048)
    pieces = [[blocks[:, cuts[k] : cuts[k + 1]]] for k in range(3)]
    for k in range(3):
        got = permute_step(pieces[k][0], k, 3)
        pieces[k] = [jnp.concatenate([pieces[k][0], got], axis=0)]
    for k in range(3):
        pieces[k].append(permute_step(pieces[k][0], k, 4))
    for k in range(3):
        pieces[k] += [permute_step(piece, k, 5) for piece in pieces[k]]
    orders = jnp.stack([relative_order(core, me, part) for part in range(3)])

    assigned = token_assignments[0]
    expert_iota = jnp.arange(experts, dtype=jnp.int32)
    chosen = jnp.any(assigned[:, :, None] == expert_iota[None, None, :], axis=1)
    token_iota = jnp.arange(tokens_dev, dtype=jnp.int32)
    earlier = (token_iota[:, None] > token_iota[None, :]).astype(bf16)
    rank = dot(earlier, chosen.astype(bf16))
    kept = chosen & (rank < admitted_route_quota.astype(f32)[None, :])
    sent_counts = jnp.sum(kept.astype(jnp.int32), axis=0, dtype=jnp.int32)
    line_iota = jnp.arange(experts * 8, dtype=jnp.int32)
    line = line_iota % 8
    spread = (expert_iota[:, None] == (line_iota // 8)[None, :]).astype(bf16)
    slot_of_line = dot(jnp.where(kept, rank, -1.0).astype(bf16), spread).astype(jnp.int32)
    main = (slot_of_line == line[None, :]).astype(bf16)
    spare_hit = slot_of_line == (8 + line // 2)[None, :]
    spare = jnp.concatenate(
        [spare_hit & (line % 2 == half)[None, :] for half in range(2)], axis=0
    ).astype(bf16)

    lengths = packed_segment_sizes[0]
    row_positions = jnp.arange(row_len, dtype=jnp.int32)
    doc_ids, doc_offset = doc_places(lengths, row_positions)
    allowed = (doc_ids[None, :] == doc_ids[:, None]) & (
        row_positions[None, :] <= row_positions[:, None]
    )
    cos_table, sin_table = rope_tables(doc_offset, head_width)
    head_shape = (row_len, heads_local, head_width)
    column_start = core * half_width
    query_half_gain = lax.dynamic_slice_in_dim(asker_scale_factor, column_start, half_width)
    key_half_gain = lax.dynamic_slice_in_dim(lookup_scale_factor, column_start, half_width)

    def whole_row(own):
        other = swap(own)
        return jnp.concatenate(
            [jnp.where(core == 0, own, other), jnp.where(core == 0, other, own)], axis=0
        )

    inputs = block_entry_states[0].astype(f32)
    factor_in = rms_factor(inputs)
    normed_in = (inputs * factor_in * mixing_scale_factor).astype(bf16)
    normed_t = whole_row(normed_in).T
    scaled_in = whole_row((inputs * factor_in).astype(bf16))
    normed_rel = reorder(normed_t, orders)

    def project(left, pieces):
        size = width // len(pieces)
        return sum(dot_tn(left[i * size : (i + 1) * size], p) for i, p in enumerate(pieces))

    both_proj = jnp.concatenate([project(normed_rel[k], pieces[k]) for k in range(3)], axis=1)
    query_proj, key_proj = both_proj[:, :half_width], both_proj[:, half_width:]
    value_low = dot_tn(normed_t, value_output[:, :half_width]).astype(bf16).reshape(head_shape)
    grad_top_low = block_result_cotangent[0]
    send_grads, *_ = lax.optimization_barrier(
        (to_experts(main, spare, grad_top_low), *(pieces[k][3] for k in range(3)))
    )
    arrived_grads = exchange(send_grads)
    query_sq, key_sq = lax.psum(
        (jnp.sum(query_proj * query_proj, axis=1), jnp.sum(key_proj * key_proj, axis=1)), "dp"
    )
    query_factor = lax.rsqrt(query_sq[:, None] / width + EPS)
    key_factor = lax.rsqrt(key_sq[:, None] / width + EPS)
    queries = rotate(
        (query_proj * query_factor * query_half_gain).reshape(head_shape), cos_table, sin_table
    ).astype(bf16)
    keys = rotate(
        (key_proj * key_factor * key_half_gain).reshape(head_shape), cos_table, sin_table
    ).astype(bf16)
    raw_scores = jnp.einsum("qhd,khd->hqk", queries, keys, preferred_element_type=f32) * score_scale
    attn_probs = softmax_rows(jnp.where(allowed[None], raw_scores, NEG))
    attn_low = attn_probs.astype(bf16)
    mixed_heads = (
        jnp.einsum("hqk,khd->qhd", attn_low, value_low, preferred_element_type=f32)
        .reshape(row_len, half_width)
        .astype(bf16)
    )
    hidden_own, share_other = output_shares(
        mixed_heads, stacked_output, block_entry_states[0], core
    )
    hidden = hidden_own + swap(share_other).astype(f32)
    factor_moe = rms_factor(hidden)
    normed_moe = (hidden * factor_moe * specialist_scale_factor).astype(bf16)

    arrived = exchange(to_experts(main, spare, normed_moe))
    *late_pieces, _ = lax.optimization_barrier((*pieces, normed_moe))
    both_w = collect(late_pieces, cuts, orders)
    mixed_rel = reorder(mixed_heads.T, orders)
    both_w, mixed_rel, arrived = lax.optimization_barrier((both_w, mixed_rel, arrived))
    gate_w, up_w, down_w = (
        specialist_switch_tensor[0],
        specialist_widen_tensor[0],
        specialist_shrink_tensor[0],
    )
    top_rows = unpack(arrived_grads)
    plain_act_grad = dot_nt(top_rows, down_w).astype(bf16)
    row_grad, rows_in, gate_pre_grad, up_pre_grad, gated_act, logit_grad = expert_rows(
        arrived, plain_act_grad, gate_w, up_w, dispatcher_projection, core, me
    )
    returned_grads = exchange(row_grad)

    own_counts = jnp.where(
        (jnp.arange(2)[:, None, None] == core) & (expert_iota[None, :, None] == me),
        sent_counts[None, None, :],
        0,
    ).astype(f32)
    early = half_of(
        jnp.concatenate(
            [dot_tn(logit_grad, rows_in), own_counts.reshape(2 * experts * experts // width, width)]
        ),
        core,
    )
    small_rows, small_cols = early.shape[0], half_width // 64
    extra = early.reshape(small_rows, 64, small_cols).transpose(1, 0, 2).reshape(64 * 8, -1)
    extra = jnp.pad(extra.astype(bf16), ((0, 0), (0, 256 - extra.shape[1])))
    unit_grads = [
        swap(dot_tn(left, right).astype(bf16))
        for left, right in (
            (rows_in, gate_pre_grad[1]),
            (rows_in, up_pre_grad[1]),
            (gated_act[1], top_rows),
        )
    ]
    send_out, returned_grads, unit_grads = lax.optimization_barrier(
        (expert_results(gated_act, down_w, extra, core), returned_grads, unit_grads)
    )
    returned = exchange(send_out)

    moe_in_grad = from_experts(main, spare, returned_grads, width)
    hidden_norm_grad, moe_gain_local = norm_back(
        moe_in_grad, hidden, factor_moe, specialist_scale_factor
    )
    hidden_grad = grad_top_low.astype(f32) + hidden_norm_grad
    grad_full = whole_row(hidden_grad.astype(bf16))
    mixed_grad = heads_grad(grad_full, stacked_output).reshape(head_shape)
    prob_grad_att = jnp.einsum("qhd,khd->hqk", mixed_grad, value_low, preferred_element_type=f32)
    score_grad = (
        attn_probs * (prob_grad_att - jnp.sum(attn_probs * prob_grad_att, axis=-1, keepdims=True))
    ).astype(bf16)
    value_grad = jnp.einsum("hqk,qhd->khd", attn_low, mixed_grad, preferred_element_type=f32)
    query_rot_grad = (
        jnp.einsum("hqk,khd->qhd", score_grad, keys, preferred_element_type=f32) * score_scale
    )
    key_rot_grad = (
        jnp.einsum("hqk,qhd->khd", score_grad, queries, preferred_element_type=f32) * score_scale
    )
    query_norm_grad = unrotate(query_rot_grad, cos_table, sin_table).reshape(row_len, half_width)
    key_norm_grad = unrotate(key_rot_grad, cos_table, sin_table).reshape(row_len, half_width)
    query_scaled = query_norm_grad * query_half_gain
    key_scaled = key_norm_grad * key_half_gain
    query_inner, key_inner = lax.psum(
        (jnp.sum(query_scaled * query_proj, axis=1), jnp.sum(key_scaled * key_proj, axis=1)), "dp"
    )
    query_low = (
        query_factor
        * (query_scaled - query_proj * query_factor * query_factor * (query_inner[:, None] / width))
    ).astype(bf16)
    key_low = (
        key_factor
        * (key_scaled - key_proj * key_factor * key_factor * (key_inner[:, None] / width))
    ).astype(bf16)
    value_proj_low = value_grad.reshape(row_len, half_width).astype(bf16)
    empty_gain = jnp.zeros((width,), f32)
    query_gain_local = lax.dynamic_update_slice_in_dim(
        empty_gain, jnp.sum(query_norm_grad * query_proj * query_factor, axis=0), column_start, 0
    )
    key_gain_local = lax.dynamic_update_slice_in_dim(
        empty_gain, jnp.sum(key_norm_grad * key_proj * key_factor, axis=0), column_start, 0
    )
    lows = (query_low, key_low, value_proj_low)

    got = [[], [], []]
    for step in (5, 4, 3):
        sent = sent_pieces(step, normed_rel, lows, mixed_rel, grad_full, got)
        if step == 5:
            sent, unit_grads, share_lows = lax.optimization_barrier((sent, unit_grads, lows))
        for k in range(3):
            got[k].append(permute_step(sent[k], k, step))
        if step == 5:
            gate_weight_grad = dot_tn(rows_in, gate_pre_grad[0]) + unit_grads[0].astype(f32)
            up_weight_grad = dot_tn(rows_in, up_pre_grad[0]) + unit_grads[1].astype(f32)
            down_weight_grad = dot_tn(gated_act[0], top_rows) + unit_grads[2].astype(f32)
            shares = input_shares(share_lows, scaled_in, both_w, value_output, core)
            attn_gain_local = shares[2][0]
            got, returned, gate_weight_grad, up_weight_grad, down_weight_grad, shares = (
                lax.optimization_barrier(
                    (got, returned, gate_weight_grad, up_weight_grad, down_weight_grad, shares[:2])
                )
            )
        if step == 4:
            block_output = hidden + from_experts(main, spare, returned, width)
            got, shares, block_output = lax.optimization_barrier((got, shares, block_output))
    near = lax.all_to_all(
        near_pieces(near_position(core, me), normed_rel[0], lows, mixed_rel[0], grad_full, got),
        BOTH,
        split_axis=0,
        concat_axis=0,
        tiled=True,
        axis_index_groups=near_groups(),
    )
    query_weight_grad, key_weight_grad, value_weight_grad, output_weight_grad = near_total(near)
    normed_in_grad = shares[0] + swap(shares[1]).astype(f32)
    input_norm_grad, _ = norm_back(
        normed_in_grad, inputs, factor_in, mixing_scale_factor
    )
    input_grad = hidden_grad + input_norm_grad

    gains = half_of(
        jnp.stack([attn_gain_local, query_gain_local, key_gain_local, moe_gain_local]), core
    )
    early = jnp.sum(
        returned[:, width * 3 // 2 : width * 3 // 2 + small_rows * small_cols // 8]
        .reshape(64, small_rows * small_cols)
        .astype(f32),
        axis=0,
    )
    small = jnp.concatenate([early, gains.reshape(-1)])
    small = jnp.pad(small, (0, 6144 - small.shape[0])).reshape(8, 768)
    small = lax.all_gather(small, "expert", axis=0, tiled=True).reshape(64, 6144)
    early = (
        small[:, : small_rows * small_cols]
        .reshape(64, small_rows, small_cols)
        .transpose(1, 0, 2)
        .reshape(small_rows, half_width)
    )
    gains = jnp.sum(
        small[:, small_rows * small_cols : small_rows * small_cols + 4 * half_width], axis=0
    ).reshape(4, half_width)
    totals = beside_other_half(jnp.concatenate([early, gains]), core)
    router_weight_grad, all_counts, gains = totals[:experts].T, totals[experts:-4], totals[-4:]
    got_counts = jnp.sum(
        jnp.where(
            (jnp.arange(2)[:, None, None] == core) & (expert_iota[None, None, :] == me),
            all_counts.reshape(2, experts, experts),
            0.0,
        ),
        axis=(0, 2),
    ).astype(jnp.int32)
    return (
        block_output[None],
        input_grad[None],
        gains[0],
        query_weight_grad,
        key_weight_grad,
        value_weight_grad,
        output_weight_grad,
        gains[1],
        gains[2],
        gains[3],
        router_weight_grad,
        gate_weight_grad[None],
        up_weight_grad[None],
        down_weight_grad[None],
        got_counts[None],
    )


def solution(mesh):
    placed = (
        P("expert", "dp", None),
        P("expert", "dp", None),
        P("expert", "dp", None),
        P("expert", None),
        P(),
        P(),
        P("expert", "dp"),
        P("expert", "dp"),
        P("expert", "dp"),
        P(("dp", "expert"), None),
        P(),
        P(),
        P(),
        P(),
        P("expert", None, None),
        P("expert", None, None),
        P("expert", None, None),
    )
    return jax.shard_map(
        shards,
        mesh=mesh,
        in_specs=placed,
        out_specs=(
            P("expert", "dp", None),
            P("expert", "dp", None),
            P(),
            P("expert", "dp"),
            P("expert", "dp"),
            P("expert", "dp"),
            P(("dp", "expert"), None),
            P(),
            P(),
            P(),
            P(),
            P("expert", None, "dp"),
            P("expert", None, "dp"),
            P("expert", "dp", None),
            P("expert", "dp"),
        ),
        check_vma=False,
    )
```

```python
import functools

import jax
import jax.numpy as jnp
from jax import lax
from jax.experimental import pallas as pl
from jax.experimental.pallas import tpu as pltpu
from jax.sharding import PartitionSpec as P

HEADS = 16
EPS = 1e-05
THETA = 10000.0
NEG = -1e30
BOTH = ("dp", "expert")
PARTS = ((0, 384), (384, 768), (768, 1024))
OFFSETS = (0, 1408, 2816, 4096)

FLIPS = ((1, 4, 16), (3, 12, 48))


def far_flip(core, part, step):
    return FLIPS[1 - core][(step + part) % 3]


def bits_of(chip, first, second):
    return sum(
        (((chip >> (2 * a)) & first) ^ ((chip >> (2 * a + 1)) & second)) << a for a in range(3)
    )


def near_position(core, chip):
    return bits_of(chip, 1, 1) if core == 0 else bits_of(chip, 0, 1)


def far_position(core, chip):
    return bits_of(chip, 0, 1) if core == 0 else bits_of(chip, 1, 1)


def groups_of(own, other):
    groups = []
    for core in range(2):
        for label in range(8):
            chips = [d for d in range(64) if other(core, d) == label]
            groups.append([64 * core + d for d in sorted(chips, key=lambda d: own(core, d))])
    return groups


def near_exchange(rows):
    return lax.all_to_all(
        rows, BOTH, split_axis=0, concat_axis=0, tiled=True,
        axis_index_groups=groups_of(near_position, far_position),
    )


def permute_step(value, part, step):
    pairs = []
    for core in range(2):
        flip = far_flip(core, part, step)
        pairs += [(64 * core + d, 64 * core + (d ^ flip)) for d in range(64)]
    return lax.ppermute(value, BOTH, pairs)


def relative_order(core, me, part):
    index = jnp.arange(64, dtype=jnp.int32)
    chips = []
    for c in range(2):
        low = (index & 7) ^ near_position(c, me)
        chip = me
        for b in range(3):
            chip = chip ^ (((low >> b) & 1) * FLIPS[c][b])
            chip = chip ^ (((index >> (3 + b)) & 1) * far_flip(c, part, 3 + b))
        chips.append(chip)
    return jnp.where(core == 0, chips[0], chips[1])


def reorder_body(order_ref, rows_ref, out_ref):
    for k in range(out_ref.shape[0]):
        for r in range(64):
            out_ref[k, r] = rows_ref[order_ref[k, r]]


def reorder(rows, orders):
    blocks = rows.reshape(64, rows.shape[0] // 64, rows.shape[1])
    count = orders.shape[0]
    out = pl.pallas_call(
        reorder_body,
        grid_spec=pltpu.PrefetchScalarGridSpec(
            num_scalar_prefetch=1,
            grid=(1,),
            in_specs=[pl.BlockSpec(blocks.shape, lambda i, o: (0, 0, 0))],
            out_specs=pl.BlockSpec((count, *blocks.shape), lambda i, o: (0, 0, 0, 0)),
        ),
        out_shape=jax.ShapeDtypeStruct((count, *blocks.shape), rows.dtype),
        compiler_params=pltpu.CompilerParams(vmem_limit_bytes=56 * 1024 * 1024),
    )(orders, blocks)
    return [out[k].reshape(rows.shape) for k in range(count)]


def place_blocks(source, block_rows, order_ref, k, first, out_ref, columns):
    for r in range(source.shape[0] // block_rows):
        rows = pl.ds(pl.multiple_of(order_ref[k, first + r] * block_rows, block_rows), block_rows)
        out_ref[rows, columns[0] : columns[1]] = source[r * block_rows : (r + 1) * block_rows, :]


def collect_body(order_ref, *refs):
    pieces, out_ref = refs[:-1], refs[-1]
    count = len(pieces) // 3
    for k in range(3):
        for i in range(count):
            place_blocks(
                pieces[k * count + i], 32, order_ref, k, i * 64 // count, out_ref, (1024 * k, 1024 * k + 1024)
            )


def collect(pieces, orders):
    flat = [piece for part in pieces for piece in part]
    return pl.pallas_call(
        collect_body,
        grid_spec=pltpu.PrefetchScalarGridSpec(
            num_scalar_prefetch=1,
            grid=(1,),
            in_specs=[pl.BlockSpec((a.shape[0], 1024), lambda i, o: (0, 0)) for a in flat],
            out_specs=pl.BlockSpec((64 * 32, 3 * 1024), lambda i, o: (0, 0)),
        ),
        out_shape=jax.ShapeDtypeStruct((64 * 32, 3 * 1024), jnp.bfloat16),
        compiler_params=pltpu.CompilerParams(vmem_limit_bytes=56 * 1024 * 1024),
    )(orders, *flat)


def half_of(rows, core):
    half = rows.shape[1] // 2
    own = lax.dynamic_slice_in_dim(rows, core * half, half, axis=1)
    return own + swap(lax.dynamic_slice_in_dim(rows, (1 - core) * half, half, axis=1))


def beside_other_half(own, core):
    other = swap(own)
    return jnp.concatenate(
        [jnp.where(core == 0, own, other), jnp.where(core == 0, other, own)], axis=1
    )


def swap(value):
    return lax.ppermute(value, "dp", [(0, 1), (1, 0)])


def dot(left, right):
    return jnp.dot(left, right, preferred_element_type=jnp.float32)


def dot_tn(left, right):
    return lax.dot_general(
        left, right, (((0,), (0,)), ((), ())), preferred_element_type=jnp.float32
    )


def dot_nt(left, right):
    return lax.dot_general(
        left, right, (((1,), (1,)), ((), ())), preferred_element_type=jnp.float32
    )


def rms_factor(values):
    return lax.rsqrt(jnp.mean(values * values, axis=-1, keepdims=True) + EPS)


def doc_places(lengths, places):
    ends = jnp.cumsum(lengths, dtype=jnp.int32)
    done = ends[None, :] <= places[:, None]
    doc_ids = jnp.sum(done.astype(jnp.int32), axis=1, dtype=jnp.int32)
    starts = jnp.sum(jnp.where(done, lengths[None, :], 0), axis=1, dtype=jnp.int32)
    return (doc_ids, places - starts)


def rope_tables(offsets, head_width):
    half_width = head_width // 2
    inverse = THETA ** (-jnp.arange(half_width, dtype=jnp.float32) * 2.0 / head_width)
    angles = offsets.astype(jnp.float32)[..., None] * inverse
    return (jnp.cos(angles)[..., None, :], jnp.sin(angles)[..., None, :])


def softmax_rows(values):
    exponent = jnp.exp(values - jnp.max(values, axis=-1, keepdims=True))
    return exponent / jnp.sum(exponent, axis=-1, keepdims=True)


def half_picker(count, half):
    rows = lax.broadcasted_iota(jnp.int32, (count // 2, count), 0)
    cols = lax.broadcasted_iota(jnp.int32, (count // 2, count), 1)
    return (cols == 2 * rows + half).astype(jnp.float32).astype(jnp.bfloat16)


def unpack_block(packed):
    count, width = packed.shape[0], packed.shape[1] * 2 // 3
    spare = packed[:, width:]
    rest = [dot(half_picker(count, h), spare).astype(jnp.bfloat16) for h in range(2)]
    return packed[:, :width], rest


def pack_block(rows, out_ref):
    count, width = out_ref.shape[0], rows.shape[1]
    half = width // 2
    out_ref[:, :width] = rows[:count]
    out_ref[:, width : width + half] = (
        dot_tn(half_picker(count, 0), rows[count:, :half])
        + dot_tn(half_picker(count, 1), rows[count:, half:])
    ).astype(jnp.bfloat16)


def unpack_body(packed_ref, rows_ref):
    main, rest = unpack_block(packed_ref[...])
    count, width = main.shape
    rows_ref[:count] = main
    rows_ref[count:, : width // 2] = rest[0]
    rows_ref[count:, width // 2 :] = rest[1]


def unpack(packed):
    count, width = packed.shape[0], packed.shape[1] * 2 // 3
    return pl.pallas_call(
        unpack_body,
        out_shape=jax.ShapeDtypeStruct((count * 3 // 2, width), jnp.bfloat16),
        compiler_params=pltpu.CompilerParams(vmem_limit_bytes=56 * 1024 * 1024),
    )(packed)


def send_body(main_ref, spare_ref, rows_ref, out_ref):
    width = rows_ref.shape[1]
    half, count = width // 2, rows_ref.shape[0]
    out_ref[:, :width] = dot_tn(main_ref[...], rows_ref[...]).astype(jnp.bfloat16)
    out_ref[:, width:] = (
        dot_tn(spare_ref[:count], rows_ref[:, :half])
        + dot_tn(spare_ref[count:], rows_ref[:, half:])
    ).astype(jnp.bfloat16)


def to_experts(main, spare, rows):
    tokens, lines = main.shape
    width, block = rows.shape[1], lines // 2
    return pl.pallas_call(
        send_body,
        grid=(2,),
        in_specs=[
            pl.BlockSpec((tokens, block), lambda i: (0, i)),
            pl.BlockSpec((2 * tokens, block), lambda i: (0, i)),
            pl.BlockSpec((tokens, width), lambda i: (0, 0)),
        ],
        out_specs=pl.BlockSpec((block, width * 3 // 2), lambda i: (i, 0)),
        out_shape=jax.ShapeDtypeStruct((lines, width * 3 // 2), jnp.bfloat16),
        compiler_params=pltpu.CompilerParams(vmem_limit_bytes=56 * 1024 * 1024),
    )(main, spare, rows)


def combine_body(main_ref, spare_ref, lines_ref, out_ref):
    tokens, width = out_ref.shape
    half = width // 2
    spare_lines = lines_ref[:, width : width + half]
    out_ref[:, :half] = dot(main_ref[...], lines_ref[:, :half]) + dot(
        spare_ref[:tokens], spare_lines
    )
    out_ref[:, half:] = dot(main_ref[...], lines_ref[:, half:width]) + dot(
        spare_ref[tokens:], spare_lines
    )


def from_experts(main, spare, lines, width):
    return pl.pallas_call(
        combine_body,
        out_shape=jax.ShapeDtypeStruct((main.shape[0], width), jnp.float32),
        compiler_params=pltpu.CompilerParams(vmem_limit_bytes=56 * 1024 * 1024),
    )(main, spare, lines)


def combine_back_body(
    main_ref, spare_ref, lines_ref, hidden_ref, factor_ref, gain_ref, top_ref,
    grad_ref, low_ref, gain_grad_ref, moe_ref,
):
    combine_body(main_ref, spare_ref, lines_ref, moe_ref)
    grad, hidden, factor = moe_ref[...], hidden_ref[...], factor_ref[...]
    scaled = grad * gain_ref[...]
    inner = jnp.mean(scaled * hidden, axis=-1, keepdims=True)
    normed = hidden * factor
    back = top_ref[...].astype(jnp.float32) + factor * (scaled - normed * (factor * inner))
    grad_ref[...] = back
    low_ref[...] = back.astype(jnp.bfloat16)
    gain_grad_ref[...] = jnp.sum(grad * normed, axis=0, keepdims=True)


def from_experts_back(main, spare, lines, hidden, factor, gain, top):
    tokens, width = hidden.shape
    return pl.pallas_call(
        combine_back_body,
        out_shape=[
            jax.ShapeDtypeStruct((tokens, width), jnp.float32),
            jax.ShapeDtypeStruct((tokens, width), jnp.bfloat16),
            jax.ShapeDtypeStruct((1, width), jnp.float32),
        ],
        scratch_shapes=[pltpu.VMEM((tokens, width), jnp.float32)],
        compiler_params=pltpu.CompilerParams(vmem_limit_bytes=56 * 1024 * 1024),
    )(main, spare, lines, hidden, factor, gain[None], top)


def row_body(core_ref, own_ref, other_ref, out_ref):
    count = own_ref.shape[0]
    out_ref[pl.ds(pl.multiple_of(core_ref[0] * count, count), count), :] = own_ref[...]
    out_ref[pl.ds(pl.multiple_of((1 - core_ref[0]) * count, count), count), :] = other_ref[...]


def whole_row(own, core):
    count, width = own.shape
    block = pl.BlockSpec((count, width), lambda i, c: (0, 0))
    return pl.pallas_call(
        row_body,
        grid_spec=pltpu.PrefetchScalarGridSpec(
            num_scalar_prefetch=1,
            grid=(1,),
            in_specs=[block] * 2,
            out_specs=pl.BlockSpec((2 * count, width), lambda i, c: (0, 0)),
        ),
        out_shape=jax.ShapeDtypeStruct((2 * count, width), own.dtype),
        compiler_params=pltpu.CompilerParams(vmem_limit_bytes=56 * 1024 * 1024),
    )(core[None].astype(jnp.int32), own, swap(own))


def out_body(core_ref, act_ref, own_ref, other_ref, extra_ref, out_ref):
    rows = dot(act_ref[0], own_ref[...]) + dot(act_ref[1], other_ref[...])
    pack_block(rows.astype(jnp.bfloat16), out_ref)
    out_ref[:, rows.shape[1] * 3 // 2 :] = extra_ref[...]


def expert_results(acts, down_w, extra, core):
    _, count, units = acts.shape
    width = down_w.shape[1]
    shape = (count * 2 // 3, width * 3 // 2 + extra.shape[1])
    return pl.pallas_call(
        out_body,
        grid_spec=pltpu.PrefetchScalarGridSpec(
            num_scalar_prefetch=1,
            grid=(1,),
            in_specs=[
                pl.BlockSpec((2, count, units), lambda i, c: (0, 0, 0)),
                pl.BlockSpec((units, width), lambda i, c: (c[0], 0)),
                pl.BlockSpec((units, width), lambda i, c: (1 - c[0], 0)),
                pl.BlockSpec(extra.shape, lambda i, c: (0, 0)),
            ],
            out_specs=pl.BlockSpec(shape, lambda i, c: (0, 0)),
        ),
        out_shape=jax.ShapeDtypeStruct(shape, jnp.bfloat16),
        compiler_params=pltpu.CompilerParams(vmem_limit_bytes=56 * 1024 * 1024),
        cost_estimate=pl.CostEstimate(
            flops=4 * count * width * units, bytes_accessed=12 * 1024 * 1024, transcendentals=0
        ),
    )(core[None].astype(jnp.int32), acts, down_w, down_w, extra)


def expert_body(
    core_ref, mine_ref, packed_ref, act_grad_ref, gate_w_ref, up_w_ref, router_ref,
    back_ref, x_out, gate_out_ref, up_out_ref, act_out_ref, logit_ref,
    x_ref, total, probs_ref, gate_ref, gate_grad_ref, sem,
):
    f32, bf16 = jnp.float32, jnp.bfloat16
    step = pl.program_id(0)
    x_copy = pltpu.make_async_copy(x_ref, x_out, sem)

    @pl.when(step == 0)
    def _():
        unpack_body(packed_ref, x_ref)
        x_copy.start()
        probs = softmax_rows(dot(x_ref[...], router_ref[...]))
        probs_ref[...] = probs
        gate_ref[...] = jnp.sum(probs * mine_ref[...], axis=1, keepdims=True)
        gate_grad_ref[...] = jnp.zeros_like(gate_grad_ref)
        total[...] = jnp.zeros_like(total)

    gate_w, up_w = gate_w_ref[...], up_w_ref[...]
    size = x_ref.shape[0] // 3
    for k in range(3):
        rows = pl.ds(k * size, size)
        x, gate = x_ref[rows, :], gate_ref[rows, :]
        gate_pre, up_pre = dot(x, gate_w), dot(x, up_w)
        plain = act_grad_ref[rows, :].astype(f32)
        sigmoid = 1.0 / (1.0 + jnp.exp(-gate_pre))
        silu = gate_pre * sigmoid
        act = silu * up_pre
        gate_grad = jnp.sum(act * plain, axis=1, keepdims=True)
        act_grad = gate * plain
        gate_pre_grad = (act_grad * up_pre * sigmoid * (1.0 + gate_pre * (1.0 - sigmoid))).astype(
            bf16
        )
        up_pre_grad = (act_grad * silu).astype(bf16)
        gate_out_ref[0, rows, :] = gate_pre_grad
        up_out_ref[0, rows, :] = up_pre_grad
        act_out_ref[0, rows, :] = (gate * act).astype(bf16)
        part = dot_nt(gate_pre_grad, gate_w) + dot_nt(up_pre_grad, up_w)

        gate_grad_ref[rows, :] += gate_grad
        total[rows, :] += part

    @pl.when(step == pl.num_programs(0) - 1)
    def _():
        logit = (gate_grad_ref[...] * gate_ref[...] * (mine_ref[...] - probs_ref[...])).astype(bf16)
        logit_ref[...] = logit
        pack_block((total[...] + dot_nt(logit, router_ref[...])).astype(bf16), back_ref)
        x_copy.wait()


def expert_rows(packed, plain_act_grad, gate_w, up_w, router, core, me):
    f32, bf16 = jnp.float32, jnp.bfloat16
    lines = packed.shape[0]
    width, units = gate_w.shape
    count, experts = lines * 3 // 2, router.shape[1]
    tile = units // 4
    mine = (jnp.arange(experts, dtype=jnp.int32) == me).astype(f32)[None, :]
    halves = jax.ShapeDtypeStruct((2, count, units // 2), bf16)
    half_spec = pl.BlockSpec((1, count, tile), lambda j, c: ((j // 2 + c[0]) % 2, 0, j % 2))
    return pl.pallas_call(
        expert_body,
        grid_spec=pltpu.PrefetchScalarGridSpec(
            num_scalar_prefetch=1,
            grid=(4,),
            in_specs=[
                pl.BlockSpec((1, experts), lambda j, c: (0, 0)),
                pl.BlockSpec(packed.shape, lambda j, c: (0, 0)),
                pl.BlockSpec((count, tile), lambda j, c: (0, j)),
                pl.BlockSpec((width, tile), lambda j, c: (0, j)),
                pl.BlockSpec((width, tile), lambda j, c: (0, j)),
                pl.BlockSpec((width, experts), lambda j, c: (0, 0)),
            ],
            out_specs=[
                pl.BlockSpec(packed.shape, lambda j, c: (0, 0)),
                pl.BlockSpec(memory_space=pl.ANY),
                half_spec,
                half_spec,
                half_spec,
                pl.BlockSpec((count, experts), lambda j, c: (0, 0)),
            ],
            scratch_shapes=[
                pltpu.VMEM((count, width), bf16),
                pltpu.VMEM((count, width), f32),
                pltpu.VMEM((count, experts), f32),
                pltpu.VMEM((count, 1), f32),
                pltpu.VMEM((count, 1), f32),
                pltpu.SemaphoreType.DMA,
            ],
        ),
        out_shape=[
            jax.ShapeDtypeStruct(packed.shape, bf16),
            jax.ShapeDtypeStruct((count, width), bf16),
            halves,
            halves,
            halves,
            jax.ShapeDtypeStruct((count, experts), bf16),
        ],
        compiler_params=pltpu.CompilerParams(vmem_limit_bytes=60 * 1024 * 1024),
        cost_estimate=pl.CostEstimate(
            flops=8 * count * width * units, bytes_accessed=24 * 1024 * 1024, transcendentals=count * units
        ),
    )(core[None].astype(jnp.int32), mine, packed, plain_act_grad, gate_w, up_w, router)


def part_sums(part, left, low, heads, grad, got):
    start, stop = PARTS[part]
    blocks = left.shape[0] // 32
    half = grad.shape[1] // 2
    main = dot(left, low).reshape(blocks, 32, low.shape[1])
    sides = [
        dot(heads, grad[:, h * half + start : h * half + stop]).reshape(blocks, 16, stop - start)
        for h in range(2)
    ]
    for g in got:
        main = main + g[:, :, : low.shape[1]].astype(jnp.float32)
        sides = [
            sides[h] + g[:, 16 * h : 16 * h + 16, low.shape[1] :].astype(jnp.float32)
            for h in range(2)
        ]
    return main, sides


def sent_body(count, *refs):
    lefts, lows, heads, grad = refs[:3], refs[3:6], refs[6:9], refs[9][...]
    got, outs = refs[10 : 10 + 3 * count], refs[10 + 3 * count :]
    for k in range(3):
        main, sides = part_sums(
            k, lefts[k][...], lows[k][...], heads[k][...], grad,
            [g[...] for g in got[k * count : (k + 1) * count]],
        )
        width = main.shape[2]
        outs[k][:, :, :width] = main.astype(jnp.bfloat16)
        for h in range(2):
            outs[k][:, 16 * h : 16 * h + 16, width:] = sides[h].astype(jnp.bfloat16)


def sent_pieces(step, lefts, lows, heads, grad, got):
    blocks = 1 << step
    chunk = min(blocks, 16)
    first = blocks // chunk
    count = len(got[0])
    ahead = lambda i: (first + i, 0)
    ahead3 = lambda i: (first + i, 0, 0)
    fixed = lambda i: (0, 0)
    columns = [OFFSETS[k + 1] - OFFSETS[k] for k in range(3)]
    return pl.pallas_call(
        functools.partial(sent_body, count),
        grid=(blocks // chunk,),
        in_specs=[pl.BlockSpec((chunk * 32, a.shape[1]), ahead) for a in lefts]
        + [pl.BlockSpec(a.shape, fixed) for a in lows]
        + [pl.BlockSpec((chunk * 16, a.shape[1]), ahead) for a in heads]
        + [pl.BlockSpec(grad.shape, fixed)]
        + [pl.BlockSpec((chunk, 32, columns[k]), ahead3) for k in range(3) for _ in range(count)],
        out_specs=[pl.BlockSpec((chunk, 32, c), lambda i: (i, 0, 0)) for c in columns],
        out_shape=[jax.ShapeDtypeStruct((blocks, 32, c), jnp.bfloat16) for c in columns],
        compiler_params=pltpu.CompilerParams(vmem_limit_bytes=56 * 1024 * 1024),
    )(*lefts, *lows, *heads, grad, *(g for k in range(3) for g in got[k]))


def near_body(left_ref, *refs):
    lows, heads_ref, grad_ref, got, out_ref = refs[:3], refs[3], refs[4], refs[5:14], refs[14]
    for k in range(3):
        main, sides = part_sums(
            k, left_ref[...], lows[k][...], heads_ref[...], grad_ref[...],
            [g[...] for g in got[3 * k : 3 * k + 3]],
        )
        width, start, stop = main.shape[2], OFFSETS[k], OFFSETS[k + 1]
        for r in range(8):
            out_ref[r, :, start : start + width] = main[r].astype(jnp.bfloat16)
            for h in range(2):
                out_ref[r, 16 * h : 16 * h + 16, start + width : stop] = sides[h][r].astype(
                    jnp.bfloat16
                )


def near_pieces(left, lows, heads, grad, got):
    fixed = lambda i: (0, 0)
    return pl.pallas_call(
        near_body,
        grid=(1,),
        in_specs=[pl.BlockSpec((8 * 32, left.shape[1]), fixed)]
        + [pl.BlockSpec(a.shape, fixed) for a in lows]
        + [pl.BlockSpec((8 * 16, heads.shape[1]), fixed), pl.BlockSpec(grad.shape, fixed)]
        + [
            pl.BlockSpec((8, 32, g.shape[2]), lambda i: (0, 0, 0))
            for k in range(3)
            for g in got[k]
        ],
        out_specs=pl.BlockSpec((8, 32, OFFSETS[3]), lambda i: (0, 0, 0)),
        out_shape=jax.ShapeDtypeStruct((8, 32, OFFSETS[3]), jnp.bfloat16),
        compiler_params=pltpu.CompilerParams(vmem_limit_bytes=56 * 1024 * 1024),
    )(left, *lows, heads, grad, *(g for k in range(3) for g in got[k]))


def total_body(near_ref, *outs):
    out_ref = outs[3]
    half = out_ref.shape[1] // 2
    for k in range(3):
        start, stop = OFFSETS[k], OFFSETS[k + 1]
        total = near_ref[0, :, start:stop].astype(jnp.float32)
        for r in range(1, near_ref.shape[0]):
            total = total + near_ref[r, :, start:stop].astype(jnp.float32)
        outs[k][...] = total[:, :half]
        for h in range(2):
            out_ref[:, h * half + PARTS[k][0] : h * half + PARTS[k][1]] = total[
                16 * h : 16 * h + 16, half:
            ]


def near_total(near):
    rows, half = near.shape[1], 1024
    return pl.pallas_call(
        total_body,
        out_shape=[jax.ShapeDtypeStruct((rows, half), jnp.float32)] * 3
        + [jax.ShapeDtypeStruct((rows // 2, 2 * half), jnp.float32)],
        compiler_params=pltpu.CompilerParams(vmem_limit_bytes=56 * 1024 * 1024),
    )(near)


def exchange(rows):
    return lax.all_to_all(rows, "expert", split_axis=0, concat_axis=0, tiled=True)


def own_and_other(core_ref, total, own_ref, other_ref):
    count = own_ref.shape[0]
    own_ref[...] = total[pl.ds(pl.multiple_of(core_ref[0] * count, count), count), :]
    other_ref[...] = total[
        pl.ds(pl.multiple_of((1 - core_ref[0]) * count, count), count), :
    ].astype(other_ref.dtype)


def output_body(core_ref, order_ref, heads_ref, inputs_ref, *refs):
    pieces, (own_ref, other_ref, stacked_out) = refs[:12], refs[12:15]
    scratch, stacked, total, sem, out_sem = refs[15:27], refs[27], refs[28], refs[29], refs[30]
    half = heads_ref.shape[1]
    copies = []
    for i in range(12):
        copies.append(
            pltpu.make_async_copy(pieces[i].at[:, half : pieces[i].shape[1]], scratch[i], sem.at[i])
        )
        copies[i].start()
    for i in range(12):
        copies[i].wait()
        place_blocks(scratch[i], 32, order_ref, i // 4, i % 4 * 16, stacked, PARTS[i // 4])
    copy_out = pltpu.make_async_copy(stacked, stacked_out, out_sem)
    copy_out.start()
    weights = stacked[...].reshape(64, 2, half // 64, half)
    for h in range(2):
        total[:, h * half : (h + 1) * half] = dot(
            heads_ref[...], weights[:, h].reshape(half, half)
        )
    own_and_other(core_ref, total, own_ref, other_ref)
    own_ref[...] += inputs_ref[...].astype(jnp.float32)
    copy_out.wait()


def output_shares(heads, pieces, orders, inputs, core):
    tokens, width = inputs.shape
    half = width // 2
    flat = [piece for part in pieces for piece in part]
    return pl.pallas_call(
        output_body,
        grid_spec=pltpu.PrefetchScalarGridSpec(
            num_scalar_prefetch=2,
            grid=(1,),
            in_specs=[
                pl.BlockSpec((2 * tokens, half), lambda i, c, o: (0, 0)),
                pl.BlockSpec((tokens, width), lambda i, c, o: (0, 0)),
            ]
            + [pl.BlockSpec(memory_space=pl.ANY)] * 12,
            out_specs=[pl.BlockSpec((tokens, width), lambda i, c, o: (0, 0))] * 2
            + [pl.BlockSpec(memory_space=pl.ANY)],
            scratch_shapes=[pltpu.VMEM((a.shape[0], a.shape[1] - half), jnp.bfloat16) for a in flat]
            + [
                pltpu.VMEM((width, half), jnp.bfloat16),
                pltpu.VMEM((2 * tokens, width), jnp.float32),
                pltpu.SemaphoreType.DMA((12,)),
                pltpu.SemaphoreType.DMA,
            ],
        ),
        out_shape=[
            jax.ShapeDtypeStruct((tokens, width), jnp.float32),
            jax.ShapeDtypeStruct((tokens, width), jnp.bfloat16),
            jax.ShapeDtypeStruct((width, half), jnp.bfloat16),
        ],
        compiler_params=pltpu.CompilerParams(vmem_limit_bytes=56 * 1024 * 1024),
    )(core[None].astype(jnp.int32), orders, heads, inputs, *flat)


def attend_body(
    query_ref, key_ref, value_ref, query_factor_ref, key_factor_ref, query_gain_ref, key_gain_ref,
    cos_ref, sin_ref, doc_ref, doc_row_ref, queries_ref, keys_ref, mixed_ref,
):
    bf16 = jnp.bfloat16
    length, head_width = cos_ref.shape
    cos, sin = cos_ref[...], sin_ref[...]

    def turned(x):
        return x * cos + pltpu.roll(x, head_width // 2, 1) * sin

    rows = lax.broadcasted_iota(jnp.int32, (length, length), 0)
    cols = lax.broadcasted_iota(jnp.int32, (length, length), 1)
    allowed = (doc_ref[...] == doc_row_ref[...]) & (cols <= rows)
    for head in range(query_ref.shape[1] // head_width):
        at = slice(head * head_width, (head + 1) * head_width)
        queries = turned(query_ref[:, at] * query_factor_ref[...] * query_gain_ref[:, at]).astype(bf16)
        keys = turned(key_ref[:, at] * key_factor_ref[...] * key_gain_ref[:, at]).astype(bf16)
        queries_ref[:, at] = queries
        keys_ref[:, at] = keys
        scores = jnp.where(allowed, dot_nt(queries, keys) * head_width ** (-0.5), NEG)
        mixed_ref[:, at] = dot(softmax_rows(scores).astype(bf16), value_ref[:, at]).astype(bf16)


def attend(query, key, value, factors, gains, cos, sin, docs):
    length, width = query.shape
    head_width = cos.shape[1]
    heads = 2
    by_head = pl.BlockSpec((length, heads * head_width), lambda h: (0, h))
    column = pl.BlockSpec((length, 1), lambda h: (0, 0))
    gain = pl.BlockSpec((1, heads * head_width), lambda h: (0, h))
    table = pl.BlockSpec((length, head_width), lambda h: (0, 0))
    return pl.pallas_call(
        attend_body,
        grid=(width // head_width // heads,),
        in_specs=[by_head] * 3 + [column] * 2 + [gain] * 2 + [table] * 2
        + [column, pl.BlockSpec((1, length), lambda h: (0, 0))],
        out_specs=[by_head] * 3,
        out_shape=[jax.ShapeDtypeStruct((length, width), jnp.bfloat16)] * 3,
        compiler_params=pltpu.CompilerParams(vmem_limit_bytes=56 * 1024 * 1024),
    )(query, key, value, *factors, *(g[None] for g in gains), cos, sin, docs[:, None], docs[None])


def attend_back_body(
    grad_ref, weight_ref, queries_ref, keys_ref, value_ref, probs_ref, query_ref, key_ref,
    query_factor_ref, key_factor_ref, query_gain_ref, key_gain_ref, cos_ref, sin_ref,
    query_out, key_out, value_out, query_inner, key_inner, query_gain_out, key_gain_out,
):
    bf16 = jnp.bfloat16
    head_width = cos_ref.shape[1]
    cos, sin = cos_ref[...], sin_ref[...]
    half, width = grad_ref.shape[1] // 2, query_ref.shape[1]
    weights = weight_ref[...].reshape(width // 16, 2, 16, half)
    all_mixed = sum(
        dot_nt(grad_ref[:, h * half : (h + 1) * half], weights[:, h].reshape(width, half))
        for h in range(2)
    ).astype(bf16)

    @pl.when(pl.program_id(0) == 0)
    def _():
        query_inner[...] = jnp.zeros_like(query_inner)
        key_inner[...] = jnp.zeros_like(key_inner)

    for head in range(width // head_width):
        at = slice(head * head_width, (head + 1) * head_width)
        mixed, probs = all_mixed[:, at], probs_ref[head]
        probs_grad = dot_nt(mixed, value_ref[:, at])
        inner = jnp.sum(probs * probs_grad, axis=-1, keepdims=True)
        score_grad = (probs * (probs_grad - inner)).astype(bf16)
        value_out[:, at] = dot_tn(probs.astype(bf16), mixed).astype(bf16)
        for grad, proj_ref, factor_ref, gain_ref, out_ref, inner_ref, gain_out in (
            (
                dot(score_grad, keys_ref[:, at]),
                query_ref, query_factor_ref, query_gain_ref, query_out, query_inner, query_gain_out,
            ),
            (
                dot_tn(score_grad, queries_ref[:, at]),
                key_ref, key_factor_ref, key_gain_ref, key_out, key_inner, key_gain_out,
            ),
        ):
            grad = grad * head_width ** (-0.5)
            grad = grad * cos - pltpu.roll(grad, head_width // 2, 1) * sin
            proj = proj_ref[:, at]
            gain_out[:, at] = jnp.sum(grad * proj * factor_ref[...], axis=0, keepdims=True)
            grad = grad * gain_ref[:, at]
            out_ref[:, at] = grad
            inner_ref[...] += jnp.sum(grad * proj, axis=1, keepdims=True)


def attend_back(grad, stacked, queries, keys, value, probs, projections, factors, gains, cos, sin):
    length, width = value.shape
    head_width = cos.shape[1]
    heads = 2
    by_head = pl.BlockSpec((length, heads * head_width), lambda h: (0, h))
    column = pl.BlockSpec((length, 1), lambda h: (0, 0))
    gain = pl.BlockSpec((1, heads * head_width), lambda h: (0, h))
    table = pl.BlockSpec((length, head_width), lambda h: (0, 0))
    f32 = jnp.float32
    return pl.pallas_call(
        attend_back_body,
        grid=(width // head_width // heads,),
        in_specs=[
            pl.BlockSpec(grad.shape, lambda h: (0, 0)),
            pl.BlockSpec((heads * head_width // 16, 32, width), lambda h: (h, 0, 0)),
            *[by_head] * 3,
            pl.BlockSpec((heads, length, length), lambda h: (h, 0, 0)),
            *[by_head] * 2,
            *[column] * 2,
            *[gain] * 2,
            *[table] * 2,
        ],
        out_specs=[by_head] * 3 + [column] * 2 + [gain] * 2,
        out_shape=[
            jax.ShapeDtypeStruct((length, width), f32),
            jax.ShapeDtypeStruct((length, width), f32),
            jax.ShapeDtypeStruct((length, width), jnp.bfloat16),
            jax.ShapeDtypeStruct((length, 1), f32),
            jax.ShapeDtypeStruct((length, 1), f32),
            jax.ShapeDtypeStruct((1, width), f32),
            jax.ShapeDtypeStruct((1, width), f32),
        ],
        compiler_params=pltpu.CompilerParams(vmem_limit_bytes=56 * 1024 * 1024),
    )(grad, stacked, queries, keys, value, probs, *projections, *factors, *(g[None] for g in gains), cos, sin)


def share_body(
    core_ref, query_ref, key_ref, value_ref, scaled_ref, weights_ref,
    own_ref, other_ref, gain_ref, total,
):
    total[...] = sum(
        dot_nt(low_ref[...], weights_ref[:, 1024 * k : 1024 * k + 1024])
        for k, low_ref in enumerate((query_ref, key_ref, value_ref))
    )
    own_and_other(core_ref, total, own_ref, other_ref)
    gain_ref[...] = jnp.sum(
        total[...] * scaled_ref[...].astype(jnp.float32), axis=0, keepdims=True
    )


def input_shares(lows, scaled, weights, core):
    tokens, width = lows[0].shape[0] // 2, weights.shape[0]
    tile = width // 8
    return pl.pallas_call(
        share_body,
        grid_spec=pltpu.PrefetchScalarGridSpec(
            num_scalar_prefetch=1,
            grid=(8,),
            in_specs=[
                *(pl.BlockSpec(a.shape, lambda i, c: (0, 0)) for a in lows),
                pl.BlockSpec((2 * tokens, tile), lambda i, c: (0, i)),
                pl.BlockSpec((tile, weights.shape[1]), lambda i, c: (i, 0)),
            ],
            out_specs=[pl.BlockSpec((tokens, tile), lambda i, c: (0, i))] * 2
            + [pl.BlockSpec((1, tile), lambda i, c: (0, i))],
            scratch_shapes=[pltpu.VMEM((2 * tokens, tile), jnp.float32)],
        ),
        out_shape=[
            jax.ShapeDtypeStruct((tokens, width), jnp.float32),
            jax.ShapeDtypeStruct((tokens, width), jnp.bfloat16),
            jax.ShapeDtypeStruct((1, width), jnp.float32),
        ],
        compiler_params=pltpu.CompilerParams(vmem_limit_bytes=56 * 1024 * 1024),
        cost_estimate=pl.CostEstimate(
            flops=4 * 1000 * 1000 * 1000, bytes_accessed=16 * 1024 * 1024, transcendentals=0
        ),
    )(core[None].astype(jnp.int32), *lows, scaled, weights)


def shards(
    block_entry_states,
    block_result_cotangent,
    token_assignments,
    packed_segment_sizes,
    admitted_route_quota,
    mixing_scale_factor,
    asker_projection,
    lookup_projection,
    content_projection,
    mixing_projection_back,
    asker_scale_factor,
    lookup_scale_factor,
    specialist_scale_factor,
    dispatcher_projection,
    specialist_switch_tensor,
    specialist_widen_tensor,
    specialist_shrink_tensor,
):
    bf16, f32 = jnp.bfloat16, jnp.float32
    tokens_dev = block_entry_states.shape[1]
    width = block_entry_states.shape[2]
    core = lax.axis_index("dp")
    me = lax.axis_index("expert")
    row_len = tokens_dev * 2
    heads_local = HEADS // 2
    head_width = width // HEADS
    half_width = width // 2
    score_scale = head_width ** (-0.5)
    experts = dispatcher_projection.shape[1]

    stacked = jnp.concatenate(
        [mixing_projection_back[:, :half_width], mixing_projection_back[:, half_width:]], axis=0
    )
    block = jnp.concatenate(
        [
            a
            for k, w in enumerate((asker_projection, lookup_projection, content_projection))
            for a in (w, stacked[:, PARTS[k][0] : PARTS[k][1]])
        ],
        axis=1,
    )
    blocks = near_exchange(jnp.broadcast_to(block[None], (8, *block.shape)))
    orders = jnp.stack([relative_order(core, me, part) for part in range(3)])

    assigned = token_assignments[0]
    expert_iota = jnp.arange(experts, dtype=jnp.int32)
    chosen = jnp.any(assigned[:, :, None] == expert_iota[None, None, :], axis=1)
    token_iota = jnp.arange(tokens_dev, dtype=jnp.int32)
    earlier = (token_iota[:, None] > token_iota[None, :]).astype(bf16)
    rank = dot(earlier, chosen.astype(bf16))
    kept = chosen & (rank < admitted_route_quota.astype(f32)[None, :])
    sent_counts = jnp.sum(kept.astype(jnp.int32), axis=0, dtype=jnp.int32)
    line_iota = jnp.arange(experts * 8, dtype=jnp.int32)
    line = line_iota % 8
    spread = (expert_iota[:, None] == (line_iota // 8)[None, :]).astype(bf16)
    slot_of_line = dot(jnp.where(kept, rank, -1.0).astype(bf16), spread).astype(jnp.int32)
    main = (slot_of_line == line[None, :]).astype(bf16)
    spare_hit = slot_of_line == (8 + line // 2)[None, :]
    spare = jnp.concatenate(
        [spare_hit & (line % 2 == half)[None, :] for half in range(2)], axis=0
    ).astype(bf16)

    lengths = packed_segment_sizes[0]
    row_positions = jnp.arange(row_len, dtype=jnp.int32)
    doc_ids, doc_offset = doc_places(lengths, row_positions)
    allowed = (doc_ids[None, :] == doc_ids[:, None]) & (
        row_positions[None, :] <= row_positions[:, None]
    )
    cos_table, sin_table = rope_tables(doc_offset, head_width)
    head_shape = (row_len, heads_local, head_width)
    column_start = core * half_width
    query_half_gain = lax.dynamic_slice_in_dim(asker_scale_factor, column_start, half_width)
    key_half_gain = lax.dynamic_slice_in_dim(lookup_scale_factor, column_start, half_width)

    inputs = block_entry_states[0].astype(f32)
    factor_in = rms_factor(inputs)
    normed_in = (inputs * factor_in * mixing_scale_factor).astype(bf16)
    normed_t = whole_row(normed_in, core).T
    normed_rel = reorder(normed_t, orders)
    grad_top_low = block_result_cotangent[0]
    send_grads = to_experts(main, spare, grad_top_low)
    both_cos = jnp.concatenate([cos_table, cos_table], axis=-1)[:, 0]
    both_sin = jnp.concatenate([-sin_table, sin_table], axis=-1)[:, 0]
    blocks, normed_rel, send_grads, both_cos, both_sin = lax.optimization_barrier(
        (blocks, normed_rel, send_grads, both_cos, both_sin)
    )
    blocks = blocks.reshape(8 * block.shape[0], block.shape[1])
    pieces = [[blocks[:, OFFSETS[k] : OFFSETS[k + 1]]] for k in range(3)]
    for k in range(3):
        got = permute_step(pieces[k][0], k, 3)
        pieces[k] = [jnp.concatenate([pieces[k][0], got], axis=0)]
    for k in range(3):
        pieces[k].append(permute_step(pieces[k][0], k, 4))
    for k in range(3):
        pieces[k] += [permute_step(piece, k, 5) for piece in pieces[k]]

    def project(left, pieces):
        size = width // len(pieces)
        return sum(
            dot_tn(left[i * size : (i + 1) * size], p[:, :half_width])
            for i, p in enumerate(pieces)
        )

    query_proj, key_proj, value_proj = (project(normed_rel[k], pieces[k]) for k in range(3))
    value_flat = value_proj.astype(bf16)
    send_grads, *_ = lax.optimization_barrier((send_grads, *(pieces[k][3] for k in range(3))))
    arrived_grads = exchange(send_grads)
    query_sq, key_sq = lax.psum(
        (jnp.sum(query_proj * query_proj, axis=1), jnp.sum(key_proj * key_proj, axis=1)), "dp"
    )
    query_factor = lax.rsqrt(query_sq[:, None] / width + EPS)
    key_factor = lax.rsqrt(key_sq[:, None] / width + EPS)
    queries, keys, mixed_heads = attend(
        query_proj, key_proj, value_flat, (query_factor, key_factor),
        (query_half_gain, key_half_gain), both_cos, both_sin, doc_ids,
    )
    hidden_own, share_other, stacked_output = output_shares(
        mixed_heads, pieces, orders, block_entry_states[0], core
    )
    stacked_output = stacked_output.reshape(64, width // 64, half_width)
    hidden = hidden_own + swap(share_other).astype(f32)
    factor_moe = rms_factor(hidden)
    normed_moe = (hidden * factor_moe * specialist_scale_factor).astype(bf16)

    arrived = exchange(to_experts(main, spare, normed_moe))
    *late_pieces, queries, keys, scaled_own, _ = lax.optimization_barrier(
        (*pieces, queries, keys, (inputs * factor_in).astype(bf16), normed_moe)
    )
    scaled_in = whole_row(scaled_own, core)
    weights = collect(late_pieces, orders)
    mixed_rel = reorder(mixed_heads.T, orders)
    raw_scores = (
        jnp.einsum(
            "qhd,khd->hqk",
            queries.reshape(head_shape),
            keys.reshape(head_shape),
            preferred_element_type=f32,
        )
        * score_scale
    )
    attn_probs = softmax_rows(jnp.where(allowed[None], raw_scores, NEG))
    weights, mixed_rel, attn_probs, scaled_in, arrived = lax.optimization_barrier(
        (weights, mixed_rel, attn_probs, scaled_in, arrived)
    )
    gate_w, up_w, down_w = (
        specialist_switch_tensor[0],
        specialist_widen_tensor[0],
        specialist_shrink_tensor[0],
    )
    top_rows = unpack(arrived_grads)
    plain_act_grad = dot_nt(top_rows, down_w).astype(bf16)
    row_grad, rows_in, gate_pre_grad, up_pre_grad, gated_act, logit_grad = expert_rows(
        arrived, plain_act_grad, gate_w, up_w, dispatcher_projection, core, me
    )
    returned_grads = exchange(row_grad)

    own_counts = jnp.where(
        (jnp.arange(2)[:, None, None] == core) & (expert_iota[None, :, None] == me),
        sent_counts[None, None, :],
        0,
    ).astype(f32)
    early = half_of(
        jnp.concatenate(
            [dot_tn(logit_grad, rows_in), own_counts.reshape(2 * experts * experts // width, width)]
        ),
        core,
    )
    small_rows, small_cols = early.shape[0], half_width // 64
    extra = early.reshape(small_rows, 64, small_cols).transpose(1, 0, 2)
    extra = extra.reshape(64 * 8, -1)
    extra = jnp.pad(extra.astype(bf16), ((0, 0), (0, 256 - extra.shape[1])))
    unit_grads = [
        swap(dot_tn(left, right).astype(bf16))
        for left, right in (
            (rows_in, gate_pre_grad[1]),
            (rows_in, up_pre_grad[1]),
            (gated_act[1], top_rows),
        )
    ]
    send_out, returned_grads, unit_grads = lax.optimization_barrier(
        (expert_results(gated_act, down_w, extra, core), returned_grads, unit_grads)
    )
    returned = exchange(send_out)

    hidden_grad, hidden_low, moe_gain_local = from_experts_back(
        main, spare, returned_grads, hidden, factor_moe, specialist_scale_factor, grad_top_low
    )
    grad_full = whole_row(hidden_low, core)
    query_scaled, key_scaled, value_proj_low, query_inner, key_inner, query_gain, key_gain = (
        attend_back(
            grad_full, stacked_output, queries, keys, value_flat, attn_probs,
            (query_proj, key_proj), (query_factor, key_factor),
            (query_half_gain, key_half_gain), both_cos, both_sin,
        )
    )
    query_inner, key_inner = lax.psum((query_inner[:, 0], key_inner[:, 0]), "dp")
    query_low = (
        query_factor
        * (query_scaled - query_proj * query_factor * query_factor * (query_inner[:, None] / width))
    ).astype(bf16)
    key_low = (
        key_factor
        * (key_scaled - key_proj * key_factor * key_factor * (key_inner[:, None] / width))
    ).astype(bf16)
    empty_gain = jnp.zeros((width,), f32)
    query_gain_local = lax.dynamic_update_slice_in_dim(empty_gain, query_gain[0], column_start, 0)
    key_gain_local = lax.dynamic_update_slice_in_dim(empty_gain, key_gain[0], column_start, 0)
    lows = (query_low, key_low, value_proj_low)

    got = [[], [], []]
    for step in (5, 4, 3):
        sent = sent_pieces(step, normed_rel, lows, mixed_rel, grad_full, got)
        if step == 5:
            sent, unit_grads, share_lows = lax.optimization_barrier((sent, unit_grads, lows))
        for k in range(3):
            got[k].append(permute_step(sent[k], k, step))
        if step == 5:
            gate_weight_grad = dot_tn(rows_in, gate_pre_grad[0]) + unit_grads[0].astype(f32)
            up_weight_grad = dot_tn(rows_in, up_pre_grad[0]) + unit_grads[1].astype(f32)
            down_weight_grad = dot_tn(gated_act[0], top_rows) + unit_grads[2].astype(f32)
            shares = input_shares(share_lows, scaled_in, weights, core)
            attn_gain_local = shares[2][0]
            gains = half_of(
                jnp.stack([attn_gain_local, query_gain_local, key_gain_local, moe_gain_local[0]]), core
            )
            early = jnp.sum(
                returned[:, width * 3 // 2 : width * 3 // 2 + small_rows * small_cols // 8]
                .reshape(64, small_rows * small_cols)
                .astype(f32),
                axis=0,
            )
            count = early.shape[0]
            small = jnp.concatenate([early, gains.reshape(-1)]).astype(bf16)
            small = jnp.pad(small, (0, 6144 - small.shape[0])).reshape(1, 8, 768)
            small = exchange(jnp.broadcast_to(small, (64, 8, 768)).reshape(512, 768))
            got, returned, gate_weight_grad, up_weight_grad, down_weight_grad, shares, small = (
                lax.optimization_barrier(
                    (
                        got,
                        returned,
                        gate_weight_grad,
                        up_weight_grad,
                        down_weight_grad,
                        shares[:2],
                        small,
                    )
                )
            )
        if step == 4:
            block_output = hidden + from_experts(main, spare, returned, width)
            got, shares, block_output = lax.optimization_barrier((got, shares, block_output))
    near = near_exchange(near_pieces(normed_rel[0], lows, mixed_rel[0], grad_full, got))
    query_weight_grad, key_weight_grad, value_weight_grad, output_weight_grad = near_total(near)
    normed_in_grad = shares[0] + swap(shares[1]).astype(f32)
    scaled = normed_in_grad * mixing_scale_factor
    input_norm_grad = factor_in * (
        scaled
        - inputs * factor_in * factor_in * jnp.mean(scaled * inputs, axis=-1, keepdims=True)
    )
    input_grad = hidden_grad + input_norm_grad

    small = small.reshape(64, 6144).astype(f32)
    early = (
        small[:, :count]
        .reshape(64, small_rows, small_cols)
        .transpose(1, 0, 2)
        .reshape(small_rows, half_width)
    )
    gains = jnp.sum(small[:, count : count + 4 * half_width], axis=0).reshape(4, half_width)
    totals = beside_other_half(jnp.concatenate([early, gains]), core)
    router_weight_grad, all_counts, gains = totals[:experts].T, totals[experts:-4], totals[-4:]
    got_counts = jnp.sum(
        jnp.where(
            (jnp.arange(2)[:, None, None] == core) & (expert_iota[None, None, :] == me),
            all_counts.reshape(2, experts, experts),
            0.0,
        ),
        axis=(0, 2),
    ).astype(jnp.int32)
    return (
        block_output[None],
        input_grad[None],
        gains[0],
        query_weight_grad,
        key_weight_grad,
        value_weight_grad,
        output_weight_grad,
        gains[1],
        gains[2],
        gains[3],
        router_weight_grad,
        gate_weight_grad[None],
        up_weight_grad[None],
        down_weight_grad[None],
        got_counts[None],
    )


def solution(mesh):
    placed = (
        P("expert", "dp", None),
        P("expert", "dp", None),
        P("expert", "dp", None),
        P("expert", None),
        P(),
        P(),
        P("expert", "dp"),
        P("expert", "dp"),
        P("expert", "dp"),
        P(("dp", "expert"), None),
        P(),
        P(),
        P(),
        P(),
        P("expert", None, None),
        P("expert", None, None),
        P("expert", None, None),
    )
    return jax.shard_map(
        shards,
        mesh=mesh,
        in_specs=placed,
        out_specs=(
            P("expert", "dp", None),
            P("expert", "dp", None),
            P(),
            P("expert", "dp"),
            P("expert", "dp"),
            P("expert", "dp"),
            P(("dp", "expert"), None),
            P(),
            P(),
            P(),
            P(),
            P("expert", None, "dp"),
            P("expert", None, "dp"),
            P("expert", "dp", None),
            P("expert", "dp"),
        ),
        check_vma=False,
    )
```

```python
import functools

import jax
import jax.numpy as jnp
from jax import lax
from jax.experimental import pallas as pl
from jax.experimental.pallas import tpu as pltpu
from jax.sharding import PartitionSpec as P

HEADS = 16
EPS = 1e-05
THETA = 10000.0
NEG = -1e30
BOTH = ("dp", "expert")
PARTS = ((0, 384), (384, 768), (768, 1024))
OFFSETS = (0, 1408, 2816, 4096)

FLIPS = ((1, 4, 16), (3, 12, 48))


def far_flip(core, part, step):
    return FLIPS[1 - core][(step + part) % 3]


def bits_of(chip, first, second):
    return sum(
        (((chip >> (2 * a)) & first) ^ ((chip >> (2 * a + 1)) & second)) << a for a in range(3)
    )


def near_position(core, chip):
    return bits_of(chip, 1, 1) if core == 0 else bits_of(chip, 0, 1)


def far_position(core, chip):
    return bits_of(chip, 0, 1) if core == 0 else bits_of(chip, 1, 1)


def groups_of(own, other):
    groups = []
    for core in range(2):
        for label in range(8):
            chips = [d for d in range(64) if other(core, d) == label]
            groups.append([64 * core + d for d in sorted(chips, key=lambda d: own(core, d))])
    return groups


def near_exchange(rows):
    return lax.all_to_all(
        rows, BOTH, split_axis=0, concat_axis=0, tiled=True,
        axis_index_groups=groups_of(near_position, far_position),
    )


def permute_step(value, part, step):
    pairs = []
    for core in range(2):
        flip = far_flip(core, part, step)
        pairs += [(64 * core + d, 64 * core + (d ^ flip)) for d in range(64)]
    return lax.ppermute(value, BOTH, pairs)


def relative_order(core, me, part):
    index = jnp.arange(64, dtype=jnp.int32)
    chips = []
    for c in range(2):
        low = (index & 7) ^ near_position(c, me)
        chip = me
        for b in range(3):
            chip = chip ^ (((low >> b) & 1) * FLIPS[c][b])
            chip = chip ^ (((index >> (3 + b)) & 1) * far_flip(c, part, 3 + b))
        chips.append(chip)
    return jnp.where(core == 0, chips[0], chips[1])


def reorder_body(order_ref, rows_ref, out_ref):
    for k in range(out_ref.shape[0]):
        for r in range(64):
            out_ref[k, r] = rows_ref[order_ref[k, r]]


def reorder(rows, orders):
    blocks = rows.reshape(64, rows.shape[0] // 64, rows.shape[1])
    count = orders.shape[0]
    out = pl.pallas_call(
        reorder_body,
        grid_spec=pltpu.PrefetchScalarGridSpec(
            num_scalar_prefetch=1,
            grid=(1,),
            in_specs=[pl.BlockSpec(blocks.shape, lambda i, o: (0, 0, 0))],
            out_specs=pl.BlockSpec((count, *blocks.shape), lambda i, o: (0, 0, 0, 0)),
        ),
        out_shape=jax.ShapeDtypeStruct((count, *blocks.shape), rows.dtype),
        compiler_params=pltpu.CompilerParams(vmem_limit_bytes=56 * 1024 * 1024),
    )(orders, blocks)
    return [out[k].reshape(rows.shape) for k in range(count)]


def place_blocks(source, order_ref, k, first, out_ref, columns):
    for r in range(source.shape[0] // 32):
        rows = pl.ds(pl.multiple_of(order_ref[k, first + r] * 32, 32), 32)
        out_ref[rows, columns[0] : columns[1]] = source[r * 32 : (r + 1) * 32, :]


def collect_body(order_ref, *refs):
    pieces, out_ref = refs[:-1], refs[-1]
    count = len(pieces) // 3
    for k in range(3):
        for i in range(count):
            place_blocks(
                pieces[k * count + i], order_ref, k, i * 64 // count, out_ref, (1024 * k, 1024 * k + 1024)
            )


def collect(pieces, orders):
    flat = [piece for part in pieces for piece in part]
    return pl.pallas_call(
        collect_body,
        grid_spec=pltpu.PrefetchScalarGridSpec(
            num_scalar_prefetch=1,
            grid=(1,),
            in_specs=[pl.BlockSpec((a.shape[0], 1024), lambda i, o: (0, 0)) for a in flat],
            out_specs=pl.BlockSpec((64 * 32, 3 * 1024), lambda i, o: (0, 0)),
        ),
        out_shape=jax.ShapeDtypeStruct((64 * 32, 3 * 1024), jnp.bfloat16),
        compiler_params=pltpu.CompilerParams(vmem_limit_bytes=56 * 1024 * 1024),
    )(orders, *flat)


def half_of(rows, core):
    half = rows.shape[1] // 2
    own = lax.dynamic_slice_in_dim(rows, core * half, half, axis=1)
    return own + swap(lax.dynamic_slice_in_dim(rows, (1 - core) * half, half, axis=1))


def beside_other_half(own, core):
    other = swap(own)
    return jnp.concatenate(
        [jnp.where(core == 0, own, other), jnp.where(core == 0, other, own)], axis=1
    )


def swap(value):
    return lax.ppermute(value, "dp", [(0, 1), (1, 0)])


def dot(left, right):
    return jnp.dot(left, right, preferred_element_type=jnp.float32)


def dot_tn(left, right):
    return lax.dot_general(
        left, right, (((0,), (0,)), ((), ())), preferred_element_type=jnp.float32
    )


def dot_nt(left, right):
    return lax.dot_general(
        left, right, (((1,), (1,)), ((), ())), preferred_element_type=jnp.float32
    )


def rms_factor(values):
    return lax.rsqrt(jnp.mean(values * values, axis=-1, keepdims=True) + EPS)


def doc_places(lengths, places):
    ends = jnp.cumsum(lengths, dtype=jnp.int32)
    done = ends[None, :] <= places[:, None]
    doc_ids = jnp.sum(done.astype(jnp.int32), axis=1, dtype=jnp.int32)
    starts = jnp.sum(jnp.where(done, lengths[None, :], 0), axis=1, dtype=jnp.int32)
    return (doc_ids, places - starts)


def rope_tables(offsets, head_width):
    half_width = head_width // 2
    inverse = THETA ** (-jnp.arange(half_width, dtype=jnp.float32) * 2.0 / head_width)
    angles = offsets.astype(jnp.float32)[..., None] * inverse
    return (jnp.cos(angles)[..., None, :], jnp.sin(angles)[..., None, :])


def softmax_rows(values):
    exponent = jnp.exp(values - jnp.max(values, axis=-1, keepdims=True))
    return exponent / jnp.sum(exponent, axis=-1, keepdims=True)


def half_picker(count, half):
    rows = lax.broadcasted_iota(jnp.int32, (count // 2, count), 0)
    cols = lax.broadcasted_iota(jnp.int32, (count // 2, count), 1)
    return (cols == 2 * rows + half).astype(jnp.float32).astype(jnp.bfloat16)


def unpack_block(packed):
    count, width = packed.shape[0], packed.shape[1] * 2 // 3
    spare = packed[:, width:]
    rest = [dot(half_picker(count, h), spare).astype(jnp.bfloat16) for h in range(2)]
    return packed[:, :width], rest


def pack_block(rows, out_ref):
    count, width = out_ref.shape[0], rows.shape[1]
    half = width // 2
    out_ref[:, :width] = rows[:count]
    out_ref[:, width : width + half] = (
        dot_tn(half_picker(count, 0), rows[count:, :half])
        + dot_tn(half_picker(count, 1), rows[count:, half:])
    ).astype(jnp.bfloat16)


def unpack_body(packed_ref, rows_ref):
    main, rest = unpack_block(packed_ref[...])
    count, width = main.shape
    rows_ref[:count] = main
    rows_ref[count:, : width // 2] = rest[0]
    rows_ref[count:, width // 2 :] = rest[1]


def unpack(packed):
    count, width = packed.shape[0], packed.shape[1] * 2 // 3
    return pl.pallas_call(
        unpack_body,
        out_shape=jax.ShapeDtypeStruct((count * 3 // 2, width), jnp.bfloat16),
        compiler_params=pltpu.CompilerParams(vmem_limit_bytes=56 * 1024 * 1024),
    )(packed)


def send_body(main_ref, spare_ref, rows_ref, out_ref):
    width = rows_ref.shape[1]
    half, count = width // 2, rows_ref.shape[0]
    out_ref[:, :width] = dot_tn(main_ref[...], rows_ref[...]).astype(jnp.bfloat16)
    out_ref[:, width:] = (
        dot_tn(spare_ref[:count], rows_ref[:, :half])
        + dot_tn(spare_ref[count:], rows_ref[:, half:])
    ).astype(jnp.bfloat16)


def to_experts(main, spare, rows):
    tokens, lines = main.shape
    width, block = rows.shape[1], lines // 2
    return pl.pallas_call(
        send_body,
        grid=(2,),
        in_specs=[
            pl.BlockSpec((tokens, block), lambda i: (0, i)),
            pl.BlockSpec((2 * tokens, block), lambda i: (0, i)),
            pl.BlockSpec((tokens, width), lambda i: (0, 0)),
        ],
        out_specs=pl.BlockSpec((block, width * 3 // 2), lambda i: (i, 0)),
        out_shape=jax.ShapeDtypeStruct((lines, width * 3 // 2), jnp.bfloat16),
        compiler_params=pltpu.CompilerParams(vmem_limit_bytes=56 * 1024 * 1024),
    )(main, spare, rows)


def send_normed_body(
    main_ref, spare_ref, own_ref, other_ref, gain_ref, out_ref, hidden_ref, factor_ref, normed
):
    @pl.when(pl.program_id(0) == 0)
    def _():
        hidden = own_ref[...] + other_ref[...].astype(jnp.float32)
        factor = rms_factor(hidden)
        hidden_ref[...] = hidden
        factor_ref[...] = factor
        normed[...] = (hidden * factor * gain_ref[...]).astype(jnp.bfloat16)

    send_body(main_ref, spare_ref, normed, out_ref)


def normed_to_experts(main, spare, own, other, gain):
    tokens, lines = main.shape
    width, block = own.shape[1], lines // 2
    whole = pl.BlockSpec((tokens, width), lambda i: (0, 0))
    return pl.pallas_call(
        send_normed_body,
        grid=(2,),
        in_specs=[
            pl.BlockSpec((tokens, block), lambda i: (0, i)),
            pl.BlockSpec((2 * tokens, block), lambda i: (0, i)),
            whole,
            whole,
            pl.BlockSpec((1, width), lambda i: (0, 0)),
        ],
        out_specs=[
            pl.BlockSpec((block, width * 3 // 2), lambda i: (i, 0)),
            whole,
            pl.BlockSpec((tokens, 1), lambda i: (0, 0)),
        ],
        out_shape=[
            jax.ShapeDtypeStruct((lines, width * 3 // 2), jnp.bfloat16),
            jax.ShapeDtypeStruct((tokens, width), jnp.float32),
            jax.ShapeDtypeStruct((tokens, 1), jnp.float32),
        ],
        scratch_shapes=[pltpu.VMEM((tokens, width), jnp.bfloat16)],
        compiler_params=pltpu.CompilerParams(vmem_limit_bytes=56 * 1024 * 1024),
    )(main, spare, own, other, gain[None])


def combine_body(main_ref, spare_ref, lines_ref, out_ref):
    tokens, width = out_ref.shape
    half = width // 2
    spare_lines = lines_ref[:, width : width + half]
    out_ref[:, :half] = dot(main_ref[...], lines_ref[:, :half]) + dot(
        spare_ref[:tokens], spare_lines
    )
    out_ref[:, half:] = dot(main_ref[...], lines_ref[:, half:width]) + dot(
        spare_ref[tokens:], spare_lines
    )


def from_experts(main, spare, lines, width):
    return pl.pallas_call(
        combine_body,
        out_shape=jax.ShapeDtypeStruct((main.shape[0], width), jnp.float32),
        compiler_params=pltpu.CompilerParams(vmem_limit_bytes=56 * 1024 * 1024),
    )(main, spare, lines)


def combine_back_body(
    main_ref, spare_ref, lines_ref, hidden_ref, factor_ref, gain_ref, top_ref,
    grad_ref, low_ref, gain_grad_ref, moe_ref,
):
    combine_body(main_ref, spare_ref, lines_ref, moe_ref)
    grad, hidden, factor = moe_ref[...], hidden_ref[...], factor_ref[...]
    scaled = grad * gain_ref[...]
    inner = jnp.mean(scaled * hidden, axis=-1, keepdims=True)
    normed = hidden * factor
    back = top_ref[...].astype(jnp.float32) + factor * (scaled - normed * (factor * inner))
    grad_ref[...] = back
    low_ref[...] = back.astype(jnp.bfloat16)
    gain_grad_ref[...] = jnp.sum(grad * normed, axis=0, keepdims=True)


def from_experts_back(main, spare, lines, hidden, factor, gain, top):
    tokens, width = hidden.shape
    return pl.pallas_call(
        combine_back_body,
        out_shape=[
            jax.ShapeDtypeStruct((tokens, width), jnp.float32),
            jax.ShapeDtypeStruct((tokens, width), jnp.bfloat16),
            jax.ShapeDtypeStruct((1, width), jnp.float32),
        ],
        scratch_shapes=[pltpu.VMEM((tokens, width), jnp.float32)],
        compiler_params=pltpu.CompilerParams(vmem_limit_bytes=56 * 1024 * 1024),
    )(main, spare, lines, hidden, factor, gain[None], top)


def row_body(core_ref, own_ref, other_ref, out_ref):
    count = own_ref.shape[0]
    out_ref[pl.ds(pl.multiple_of(core_ref[0] * count, count), count), :] = own_ref[...]
    out_ref[pl.ds(pl.multiple_of((1 - core_ref[0]) * count, count), count), :] = other_ref[...]


def whole_row(own, core):
    count, width = own.shape
    block = pl.BlockSpec((count, width), lambda i, c: (0, 0))
    return pl.pallas_call(
        row_body,
        grid_spec=pltpu.PrefetchScalarGridSpec(
            num_scalar_prefetch=1,
            grid=(1,),
            in_specs=[block] * 2,
            out_specs=pl.BlockSpec((2 * count, width), lambda i, c: (0, 0)),
        ),
        out_shape=jax.ShapeDtypeStruct((2 * count, width), own.dtype),
        compiler_params=pltpu.CompilerParams(vmem_limit_bytes=56 * 1024 * 1024),
    )(core[None].astype(jnp.int32), own, swap(own))


def out_body(core_ref, act_ref, own_ref, other_ref, extra_ref, out_ref):
    rows = dot(act_ref[0], own_ref[...]) + dot(act_ref[1], other_ref[...])
    pack_block(rows.astype(jnp.bfloat16), out_ref)
    out_ref[:, rows.shape[1] * 3 // 2 :] = extra_ref[...]


def expert_results(acts, down_w, extra, core):
    _, count, units = acts.shape
    width = down_w.shape[1]
    shape = (count * 2 // 3, width * 3 // 2 + extra.shape[1])
    return pl.pallas_call(
        out_body,
        grid_spec=pltpu.PrefetchScalarGridSpec(
            num_scalar_prefetch=1,
            grid=(1,),
            in_specs=[
                pl.BlockSpec((2, count, units), lambda i, c: (0, 0, 0)),
                pl.BlockSpec((units, width), lambda i, c: (c[0], 0)),
                pl.BlockSpec((units, width), lambda i, c: (1 - c[0], 0)),
                pl.BlockSpec(extra.shape, lambda i, c: (0, 0)),
            ],
            out_specs=pl.BlockSpec(shape, lambda i, c: (0, 0)),
        ),
        out_shape=jax.ShapeDtypeStruct(shape, jnp.bfloat16),
        compiler_params=pltpu.CompilerParams(vmem_limit_bytes=56 * 1024 * 1024),
        cost_estimate=pl.CostEstimate(
            flops=4 * count * width * units, bytes_accessed=12 * 1024 * 1024, transcendentals=0
        ),
    )(core[None].astype(jnp.int32), acts, down_w, down_w, extra)


def as_column(row):
    return jnp.broadcast_to(row, (8, row.shape[1])).T[:, :1]


def as_row(column):
    return jnp.broadcast_to(column, (column.shape[0], 128)).T[:1, :]


def expert_body(
    core_ref, mine_ref, packed_ref, act_grad_ref, gate_w_ref, up_w_ref, router_ref,
    back_ref, x_out, gate_out_ref, up_out_ref, act_out_ref, logit_ref,
    x_ref, total, probs_ref, gate_ref, gate_grad_ref, sem,
):
    f32, bf16 = jnp.float32, jnp.bfloat16
    step = pl.program_id(0)
    x_copy = pltpu.make_async_copy(x_ref, x_out, sem)

    @pl.when(step == 0)
    def _():
        unpack_body(packed_ref, x_ref)
        x_copy.start()
        probs = softmax_rows(dot(x_ref[...], router_ref[...]))
        probs_ref[...] = probs
        gate_ref[...] = jnp.sum(probs * mine_ref[...], axis=1, keepdims=True)
        gate_grad_ref[...] = jnp.zeros_like(gate_grad_ref)
        total[...] = jnp.zeros_like(total)

    gate_w, up_w = gate_w_ref[...], up_w_ref[...]
    size = x_ref.shape[0] // 3
    for k in range(3):
        rows = pl.ds(k * size, size)
        x, gate = x_ref[rows, :], gate_ref[rows, :]
        gate_pre, up_pre = dot(x, gate_w), dot(x, up_w)
        plain = act_grad_ref[rows, :].astype(f32)
        sigmoid = 1.0 / (1.0 + jnp.exp(-gate_pre))
        silu = gate_pre * sigmoid
        act = silu * up_pre
        gate_grad = jnp.sum(act * plain, axis=1, keepdims=True)
        act_grad = gate * plain
        gate_pre_grad = (act_grad * up_pre * sigmoid * (1.0 + gate_pre * (1.0 - sigmoid))).astype(
            bf16
        )
        up_pre_grad = (act_grad * silu).astype(bf16)
        gate_out_ref[0, rows, :] = gate_pre_grad
        up_out_ref[0, rows, :] = up_pre_grad
        act_out_ref[0, rows, :] = (gate * act).astype(bf16)
        part = dot_nt(gate_pre_grad, gate_w) + dot_nt(up_pre_grad, up_w)

        gate_grad_ref[rows, :] += gate_grad
        total[rows, :] += part

    @pl.when(step == pl.num_programs(0) - 1)
    def _():
        logit = (gate_grad_ref[...] * gate_ref[...] * (mine_ref[...] - probs_ref[...])).astype(bf16)
        logit_ref[...] = logit
        pack_block((total[...] + dot_nt(logit, router_ref[...])).astype(bf16), back_ref)
        x_copy.wait()


def expert_rows(packed, plain_act_grad, gate_w, up_w, router, core, me):
    f32, bf16 = jnp.float32, jnp.bfloat16
    lines = packed.shape[0]
    width, units = gate_w.shape
    count, experts = lines * 3 // 2, router.shape[1]
    tile = units // 4
    mine = (jnp.arange(experts, dtype=jnp.int32) == me).astype(f32)[None, :]
    halves = jax.ShapeDtypeStruct((2, count, units // 2), bf16)
    half_spec = pl.BlockSpec((1, count, tile), lambda j, c: ((j // 2 + c[0]) % 2, 0, j % 2))
    return pl.pallas_call(
        expert_body,
        grid_spec=pltpu.PrefetchScalarGridSpec(
            num_scalar_prefetch=1,
            grid=(4,),
            in_specs=[
                pl.BlockSpec((1, experts), lambda j, c: (0, 0)),
                pl.BlockSpec(packed.shape, lambda j, c: (0, 0)),
                pl.BlockSpec((count, tile), lambda j, c: (0, j)),
                pl.BlockSpec((width, tile), lambda j, c: (0, j)),
                pl.BlockSpec((width, tile), lambda j, c: (0, j)),
                pl.BlockSpec((width, experts), lambda j, c: (0, 0)),
            ],
            out_specs=[
                pl.BlockSpec(packed.shape, lambda j, c: (0, 0)),
                pl.BlockSpec(memory_space=pl.ANY),
                half_spec,
                half_spec,
                half_spec,
                pl.BlockSpec((count, experts), lambda j, c: (0, 0)),
            ],
            scratch_shapes=[
                pltpu.VMEM((count, width), bf16),
                pltpu.VMEM((count, width), f32),
                pltpu.VMEM((count, experts), f32),
                pltpu.VMEM((count, 1), f32),
                pltpu.VMEM((count, 1), f32),
                pltpu.SemaphoreType.DMA,
            ],
        ),
        out_shape=[
            jax.ShapeDtypeStruct(packed.shape, bf16),
            jax.ShapeDtypeStruct((count, width), bf16),
            halves,
            halves,
            halves,
            jax.ShapeDtypeStruct((count, experts), bf16),
        ],
        compiler_params=pltpu.CompilerParams(vmem_limit_bytes=60 * 1024 * 1024),
        cost_estimate=pl.CostEstimate(
            flops=8 * count * width * units, bytes_accessed=24 * 1024 * 1024, transcendentals=count * units
        ),
    )(core[None].astype(jnp.int32), mine, packed, plain_act_grad, gate_w, up_w, router)


def part_sums(part, left, low, heads, grad, got):
    start, stop = PARTS[part]
    blocks = left.shape[0] // 32
    half = grad.shape[1] // 2
    main = dot(left, low).reshape(blocks, 32, low.shape[1])
    sides = [
        dot(heads, grad[:, h * half + start : h * half + stop]).reshape(blocks, 16, stop - start)
        for h in range(2)
    ]
    for g in got:
        main = main + g[:, :, : low.shape[1]].astype(jnp.float32)
        sides = [
            sides[h] + g[:, 16 * h : 16 * h + 16, low.shape[1] :].astype(jnp.float32)
            for h in range(2)
        ]
    return main, sides


def store_piece(part, left_ref, low, heads_ref, grad, got, out_ref):
    main, sides = part_sums(part, left_ref[...], low, heads_ref[...], grad, [g[...] for g in got])
    width = main.shape[2]
    out_ref[:, :, :width] = main.astype(jnp.bfloat16)
    for h in range(2):
        out_ref[:, 16 * h : 16 * h + 16, width:] = sides[h].astype(jnp.bfloat16)


def sent_body(parts, count, *refs):
    n = len(parts)
    lefts, lows, heads, grad = refs[:n], refs[n : 2 * n], refs[2 * n : 3 * n], refs[3 * n][...]
    got, outs = refs[3 * n + 1 : 3 * n + 1 + n * count], refs[3 * n + 1 + n * count :]
    for i, k in enumerate(parts):
        part_got = got[i * count : (i + 1) * count]
        store_piece(k, lefts[i], lows[i][...], heads[i], grad, part_got, outs[i])


def piece_specs(step, parts, lefts, heads, grad, count):
    blocks = 1 << step
    chunk = 16 if blocks == 32 else 8
    first = blocks // chunk
    ahead = lambda i: (first + i, 0)
    ahead3 = lambda i: (first + i, 0, 0)
    columns = [OFFSETS[k + 1] - OFFSETS[k] for k in parts]
    return (
        blocks // chunk,
        [pl.BlockSpec((chunk * 32, lefts[0].shape[1]), ahead) for _ in parts],
        [pl.BlockSpec((chunk * 16, heads[0].shape[1]), ahead) for _ in parts]
        + [pl.BlockSpec(grad.shape, lambda i: (0, 0))]
        + [pl.BlockSpec((chunk, 32, c), ahead3) for c in columns for _ in range(count)],
        [pl.BlockSpec((chunk, 32, c), lambda i: (i, 0, 0)) for c in columns],
        [jax.ShapeDtypeStruct((blocks, 32, c), jnp.bfloat16) for c in columns],
    )


def sent_pieces(step, parts, lefts, lows, heads, grad, got):
    count = len(got[0])
    steps, left_specs, other_specs, out_specs, out_shape = piece_specs(
        step, parts, lefts, heads, grad, count
    )
    return pl.pallas_call(
        functools.partial(sent_body, parts, count),
        grid=(steps,),
        in_specs=left_specs + [pl.BlockSpec(a.shape, lambda i: (0, 0)) for a in lows] + other_specs,
        out_specs=out_specs,
        out_shape=out_shape,
        compiler_params=pltpu.CompilerParams(vmem_limit_bytes=56 * 1024 * 1024),
    )(
        *(lefts[k] for k in parts),
        *lows,
        *(heads[k] for k in parts),
        grad,
        *(g for k in parts for g in got[k]),
    )


def first_body(
    scaled_query, scaled_key, query_proj, key_proj, query_sq, key_sq, query_inner, key_inner,
    value_low, left0, left1, left2, heads0, heads1, heads2, grad_ref,
    query_low, key_low, out0, out1, out2,
):
    @pl.when(pl.program_id(0) == 0)
    def _():
        for scaled, proj, squares, inner, low in (
            (scaled_query, query_proj, query_sq, query_inner, query_low),
            (scaled_key, key_proj, key_sq, key_inner, key_low),
        ):
            row = factor_of(squares[...])
            factor = as_column(row)
            share = as_column(row * row * (inner[...] / 2048))
            low[...] = (factor * (scaled[...] - proj[...] * share)).astype(jnp.bfloat16)

    grad = grad_ref[...]
    store_piece(0, left0, query_low[...], heads0, grad, [], out0)
    store_piece(1, left1, key_low[...], heads1, grad, [], out1)
    store_piece(2, left2, value_low[...], heads2, grad, [], out2)


def first_pieces(scaled, projections, squares, inners, value_low, lefts, heads, grad):
    steps, left_specs, other_specs, out_specs, out_shape = piece_specs(
        5, (0, 1, 2), lefts, heads, grad, 0
    )
    whole = pl.BlockSpec(scaled[0].shape, lambda i: (0, 0))
    row = pl.BlockSpec((1, scaled[0].shape[0]), lambda i: (0, 0))
    low = jax.ShapeDtypeStruct(scaled[0].shape, jnp.bfloat16)
    return pl.pallas_call(
        first_body,
        grid=(steps,),
        in_specs=[whole] * 4 + [row] * 4 + [whole] + left_specs + other_specs,
        out_specs=[whole] * 2 + out_specs,
        out_shape=[low] * 2 + out_shape,
        compiler_params=pltpu.CompilerParams(vmem_limit_bytes=56 * 1024 * 1024),
    )(
        *scaled,
        *projections,
        *(q[None] for q in squares),
        *(q[None] for q in inners),
        value_low,
        *lefts,
        *heads,
        grad,
    )


def near_body(left_ref, *refs):
    lows, heads_ref, grad_ref, got, out_ref = refs[:3], refs[3], refs[4], refs[5:14], refs[14]
    for k in range(3):
        main, sides = part_sums(
            k, left_ref[...], lows[k][...], heads_ref[...], grad_ref[...],
            [g[...] for g in got[3 * k : 3 * k + 3]],
        )
        width, start, stop = main.shape[2], OFFSETS[k], OFFSETS[k + 1]
        for r in range(8):
            out_ref[r, :, start : start + width] = main[r].astype(jnp.bfloat16)
            for h in range(2):
                out_ref[r, 16 * h : 16 * h + 16, start + width : stop] = sides[h][r].astype(
                    jnp.bfloat16
                )


def near_pieces(left, lows, heads, grad, got):
    fixed = lambda i: (0, 0)
    return pl.pallas_call(
        near_body,
        grid=(1,),
        in_specs=[pl.BlockSpec((8 * 32, left.shape[1]), fixed)]
        + [pl.BlockSpec(a.shape, fixed) for a in lows]
        + [pl.BlockSpec((8 * 16, heads.shape[1]), fixed), pl.BlockSpec(grad.shape, fixed)]
        + [
            pl.BlockSpec((8, 32, g.shape[2]), lambda i: (0, 0, 0))
            for k in range(3)
            for g in got[k]
        ],
        out_specs=pl.BlockSpec((8, 32, OFFSETS[3]), lambda i: (0, 0, 0)),
        out_shape=jax.ShapeDtypeStruct((8, 32, OFFSETS[3]), jnp.bfloat16),
        compiler_params=pltpu.CompilerParams(vmem_limit_bytes=56 * 1024 * 1024),
    )(left, *lows, heads, grad, *(g for k in range(3) for g in got[k]))


def total_body(near_ref, *outs):
    out_ref = outs[3]
    half = out_ref.shape[1] // 2
    for k in range(3):
        start, stop = OFFSETS[k], OFFSETS[k + 1]
        total = near_ref[0, :, start:stop].astype(jnp.float32)
        for r in range(1, near_ref.shape[0]):
            total = total + near_ref[r, :, start:stop].astype(jnp.float32)
        outs[k][...] = total[:, :half]
        for h in range(2):
            out_ref[:, h * half + PARTS[k][0] : h * half + PARTS[k][1]] = total[
                16 * h : 16 * h + 16, half:
            ]


def near_total(near):
    rows, half = near.shape[1], 1024
    return pl.pallas_call(
        total_body,
        out_shape=[jax.ShapeDtypeStruct((rows, half), jnp.float32)] * 3
        + [jax.ShapeDtypeStruct((rows // 2, 2 * half), jnp.float32)],
        compiler_params=pltpu.CompilerParams(vmem_limit_bytes=56 * 1024 * 1024),
    )(near)


def exchange(rows):
    return lax.all_to_all(rows, "expert", split_axis=0, concat_axis=0, tiled=True)


def own_and_other(core_ref, total, own_ref, other_ref):
    count = own_ref.shape[0]
    own_ref[...] = total[pl.ds(pl.multiple_of(core_ref[0] * count, count), count), :]
    other_ref[...] = total[
        pl.ds(pl.multiple_of((1 - core_ref[0]) * count, count), count), :
    ].astype(other_ref.dtype)


def output_body(core_ref, order_ref, heads_ref, inputs_ref, *refs):
    pieces, (own_ref, other_ref, stacked_out) = refs[:12], refs[12:15]
    scratch, stacked, total, sem, out_sem = refs[15:27], refs[27], refs[28], refs[29], refs[30]
    half = heads_ref.shape[1]
    copies = []
    for i in range(12):
        copies.append(
            pltpu.make_async_copy(pieces[i].at[:, half : pieces[i].shape[1]], scratch[i], sem.at[i])
        )
        copies[i].start()
    for i in range(12):
        copies[i].wait()
        k, first = i // 4, i % 4 * 16
        for r in range(16):
            rows = pl.ds(pl.multiple_of(order_ref[k, first + r] * 16, 16), 16)
            for h in range(2):
                stacked[h, rows, PARTS[k][0] : PARTS[k][1]] = scratch[i][
                    r * 32 + h * 16 : r * 32 + h * 16 + 16, :
                ]
    copy_out = pltpu.make_async_copy(stacked, stacked_out, out_sem)
    copy_out.start()
    for h in range(2):
        total[:, h * half : (h + 1) * half] = dot(heads_ref[...], stacked[h])
    own_and_other(core_ref, total, own_ref, other_ref)
    own_ref[...] += inputs_ref[...].astype(jnp.float32)
    copy_out.wait()


def output_shares(heads, pieces, orders, inputs, core):
    tokens, width = inputs.shape
    half = width // 2
    flat = [piece for part in pieces for piece in part]
    return pl.pallas_call(
        output_body,
        grid_spec=pltpu.PrefetchScalarGridSpec(
            num_scalar_prefetch=2,
            grid=(1,),
            in_specs=[
                pl.BlockSpec((2 * tokens, half), lambda i, c, o: (0, 0)),
                pl.BlockSpec((tokens, width), lambda i, c, o: (0, 0)),
            ]
            + [pl.BlockSpec(memory_space=pl.ANY)] * 12,
            out_specs=[pl.BlockSpec((tokens, width), lambda i, c, o: (0, 0))] * 2
            + [pl.BlockSpec(memory_space=pl.ANY)],
            scratch_shapes=[pltpu.VMEM((a.shape[0], a.shape[1] - half), jnp.bfloat16) for a in flat]
            + [
                pltpu.VMEM((2, half, half), jnp.bfloat16),
                pltpu.VMEM((2 * tokens, width), jnp.float32),
                pltpu.SemaphoreType.DMA((12,)),
                pltpu.SemaphoreType.DMA,
            ],
        ),
        out_shape=[
            jax.ShapeDtypeStruct((tokens, width), jnp.float32),
            jax.ShapeDtypeStruct((tokens, width), jnp.bfloat16),
            jax.ShapeDtypeStruct((2, half, half), jnp.bfloat16),
        ],
        compiler_params=pltpu.CompilerParams(vmem_limit_bytes=56 * 1024 * 1024),
    )(core[None].astype(jnp.int32), orders, heads, inputs, *flat)


def factor_of(squares):
    return lax.rsqrt(squares / 2048 + EPS)


def attend_body(
    query_ref, key_ref, value_ref, query_sq_ref, key_sq_ref, query_gain_ref, key_gain_ref,
    cos_ref, sin_ref, doc_ref, doc_row_ref, queries_ref, keys_ref, mixed_ref,
    query_factor_ref, key_factor_ref,
):
    bf16 = jnp.bfloat16
    length, head_width = cos_ref.shape
    cos, sin = cos_ref[...], sin_ref[...]

    @pl.when(pl.program_id(0) == 0)
    def _():
        query_factor_ref[...] = as_column(factor_of(query_sq_ref[...]))
        key_factor_ref[...] = as_column(factor_of(key_sq_ref[...]))

    def turned(x):
        return x * cos + pltpu.roll(x, head_width // 2, 1) * sin

    rows = lax.broadcasted_iota(jnp.int32, (length, length), 0)
    cols = lax.broadcasted_iota(jnp.int32, (length, length), 1)
    allowed = (doc_ref[...] == doc_row_ref[...]) & (cols <= rows)
    for head in range(query_ref.shape[1] // head_width):
        at = slice(head * head_width, (head + 1) * head_width)
        queries = turned(query_ref[:, at] * query_factor_ref[...] * query_gain_ref[:, at]).astype(bf16)
        keys = turned(key_ref[:, at] * key_factor_ref[...] * key_gain_ref[:, at]).astype(bf16)
        queries_ref[:, at] = queries
        keys_ref[:, at] = keys
        scores = jnp.where(allowed, dot_nt(queries, keys) * head_width ** (-0.5), NEG)
        mixed_ref[:, at] = dot(softmax_rows(scores).astype(bf16), value_ref[:, at]).astype(bf16)


def attend(query, key, value, squares, gains, cos, sin, docs):
    length, width = query.shape
    head_width = cos.shape[1]
    heads = 2
    by_head = pl.BlockSpec((length, heads * head_width), lambda h: (0, h))
    column = pl.BlockSpec((length, 1), lambda h: (0, 0))
    row = pl.BlockSpec((1, length), lambda h: (0, 0))
    gain = pl.BlockSpec((1, heads * head_width), lambda h: (0, h))
    table = pl.BlockSpec((length, head_width), lambda h: (0, 0))
    return pl.pallas_call(
        attend_body,
        grid=(width // head_width // heads,),
        in_specs=[by_head] * 3 + [row] * 2 + [gain] * 2 + [table] * 2 + [column, row],
        out_specs=[by_head] * 3,
        out_shape=[jax.ShapeDtypeStruct((length, width), jnp.bfloat16)] * 3,
        scratch_shapes=[pltpu.VMEM((length, 1), jnp.float32)] * 2,
        compiler_params=pltpu.CompilerParams(vmem_limit_bytes=56 * 1024 * 1024),
    )(query, key, value, *(q[None] for q in squares), *(g[None] for g in gains), cos, sin, docs[:, None], docs[None])


def attend_back_body(
    core_ref, own_ref, other_ref, weight_ref, queries_ref, keys_ref, value_ref, probs_ref,
    query_ref, key_ref, query_sq_ref, key_sq_ref, query_gain_ref, key_gain_ref, cos_ref, sin_ref,
    query_out, key_out, value_out, query_inner_row, key_inner_row, query_gain_out, key_gain_out,
    grad_ref, query_factor_ref, key_factor_ref, query_inner, key_inner,
):
    bf16 = jnp.bfloat16
    head_width = cos_ref.shape[1]
    cos, sin = cos_ref[...], sin_ref[...]
    half, width = grad_ref.shape[1] // 2, query_ref.shape[1]
    @pl.when(pl.program_id(0) == 0)
    def _():
        row_body(core_ref, own_ref, other_ref, grad_ref)
        query_factor_ref[...] = as_column(factor_of(query_sq_ref[...]))
        key_factor_ref[...] = as_column(factor_of(key_sq_ref[...]))
        query_inner[...] = jnp.zeros_like(query_inner)
        key_inner[...] = jnp.zeros_like(key_inner)

    all_mixed = sum(
        dot_nt(grad_ref[:, h * half : (h + 1) * half], weight_ref[h]) for h in range(2)
    ).astype(bf16)

    for head in range(width // head_width):
        at = slice(head * head_width, (head + 1) * head_width)
        mixed, probs = all_mixed[:, at], probs_ref[head]
        probs_grad = dot_nt(mixed, value_ref[:, at])
        inner = jnp.sum(probs * probs_grad, axis=-1, keepdims=True)
        score_grad = (probs * (probs_grad - inner)).astype(bf16)
        value_out[:, at] = dot_tn(probs.astype(bf16), mixed).astype(bf16)
        for grad, proj_ref, factor_ref, gain_ref, out_ref, inner_ref, gain_out in (
            (
                dot(score_grad, keys_ref[:, at]),
                query_ref, query_factor_ref, query_gain_ref, query_out, query_inner, query_gain_out,
            ),
            (
                dot_tn(score_grad, queries_ref[:, at]),
                key_ref, key_factor_ref, key_gain_ref, key_out, key_inner, key_gain_out,
            ),
        ):
            grad = grad * head_width ** (-0.5)
            grad = grad * cos - pltpu.roll(grad, head_width // 2, 1) * sin
            proj = proj_ref[:, at]
            gain_out[:, at] = jnp.sum(grad * proj * factor_ref[...], axis=0, keepdims=True)
            grad = grad * gain_ref[:, at]
            out_ref[:, at] = grad
            inner_ref[...] += jnp.sum(grad * proj, axis=1, keepdims=True)

    @pl.when(pl.program_id(0) == pl.num_programs(0) - 1)
    def _():
        query_inner_row[...] = as_row(query_inner[...])
        key_inner_row[...] = as_row(key_inner[...])


def attend_back(own, other, core, stacked, queries, keys, value, probs, projections, squares, gains, cos, sin):
    length, width = value.shape
    head_width = cos.shape[1]
    heads = 2
    by_head = pl.BlockSpec((length, heads * head_width), lambda h, c: (0, h))
    row = pl.BlockSpec((1, length), lambda h, c: (0, 0))
    gain = pl.BlockSpec((1, heads * head_width), lambda h, c: (0, h))
    table = pl.BlockSpec((length, head_width), lambda h, c: (0, 0))
    f32 = jnp.float32
    return pl.pallas_call(
        attend_back_body,
        grid_spec=pltpu.PrefetchScalarGridSpec(
            num_scalar_prefetch=1,
            grid=(width // head_width // heads,),
            in_specs=[
            pl.BlockSpec(own.shape, lambda h, c: (0, 0)),
            pl.BlockSpec(own.shape, lambda h, c: (0, 0)),
            pl.BlockSpec((2, heads * head_width, width), lambda h, c: (0, h, 0)),
            *[by_head] * 3,
            pl.BlockSpec((heads, length, length), lambda h, c: (h, 0, 0)),
            *[by_head] * 2,
            *[row] * 2,
            *[gain] * 2,
            *[table] * 2,
        ],
        out_specs=[by_head] * 3 + [row] * 2 + [gain] * 2
        + [pl.BlockSpec((length, own.shape[1]), lambda h, c: (0, 0))],
            scratch_shapes=[pltpu.VMEM((length, 1), f32)] * 4,
        ),
        out_shape=[
            jax.ShapeDtypeStruct((length, width), f32),
            jax.ShapeDtypeStruct((length, width), f32),
            jax.ShapeDtypeStruct((length, width), jnp.bfloat16),
            jax.ShapeDtypeStruct((1, length), f32),
            jax.ShapeDtypeStruct((1, length), f32),
            jax.ShapeDtypeStruct((1, width), f32),
            jax.ShapeDtypeStruct((1, width), f32),
            jax.ShapeDtypeStruct((length, own.shape[1]), jnp.bfloat16),
        ],
        compiler_params=pltpu.CompilerParams(vmem_limit_bytes=56 * 1024 * 1024),
    )(core[None].astype(jnp.int32), own, other, stacked, queries, keys, value, probs, *projections, *(q[None] for q in squares), *(g[None] for g in gains), cos, sin)


def share_body(
    core_ref, query_ref, key_ref, value_ref, scaled_ref, weights_ref,
    own_ref, other_ref, gain_ref, total,
):
    total[...] = sum(
        dot_nt(low_ref[...], weights_ref[:, 1024 * k : 1024 * k + 1024])
        for k, low_ref in enumerate((query_ref, key_ref, value_ref))
    )
    own_and_other(core_ref, total, own_ref, other_ref)
    gain_ref[...] = jnp.sum(
        total[...] * scaled_ref[...].astype(jnp.float32), axis=0, keepdims=True
    )


def input_shares(lows, scaled, weights, core):
    tokens, width = lows[0].shape[0] // 2, weights.shape[0]
    tile = width // 8
    return pl.pallas_call(
        share_body,
        grid_spec=pltpu.PrefetchScalarGridSpec(
            num_scalar_prefetch=1,
            grid=(8,),
            in_specs=[
                *(pl.BlockSpec(a.shape, lambda i, c: (0, 0)) for a in lows),
                pl.BlockSpec((2 * tokens, tile), lambda i, c: (0, i)),
                pl.BlockSpec((tile, weights.shape[1]), lambda i, c: (i, 0)),
            ],
            out_specs=[pl.BlockSpec((tokens, tile), lambda i, c: (0, i))] * 2
            + [pl.BlockSpec((1, tile), lambda i, c: (0, i))],
            scratch_shapes=[pltpu.VMEM((2 * tokens, tile), jnp.float32)],
        ),
        out_shape=[
            jax.ShapeDtypeStruct((tokens, width), jnp.float32),
            jax.ShapeDtypeStruct((tokens, width), jnp.bfloat16),
            jax.ShapeDtypeStruct((1, width), jnp.float32),
        ],
        compiler_params=pltpu.CompilerParams(vmem_limit_bytes=56 * 1024 * 1024),
        cost_estimate=pl.CostEstimate(
            flops=4 * 1000 * 1000 * 1000, bytes_accessed=16 * 1024 * 1024, transcendentals=0
        ),
    )(core[None].astype(jnp.int32), *lows, scaled, weights)


def shards(
    block_entry_states,
    block_result_cotangent,
    token_assignments,
    packed_segment_sizes,
    admitted_route_quota,
    mixing_scale_factor,
    asker_projection,
    lookup_projection,
    content_projection,
    mixing_projection_back,
    asker_scale_factor,
    lookup_scale_factor,
    specialist_scale_factor,
    dispatcher_projection,
    specialist_switch_tensor,
    specialist_widen_tensor,
    specialist_shrink_tensor,
):
    bf16, f32 = jnp.bfloat16, jnp.float32
    tokens_dev = block_entry_states.shape[1]
    width = block_entry_states.shape[2]
    core = lax.axis_index("dp")
    me = lax.axis_index("expert")
    row_len = tokens_dev * 2
    heads_local = HEADS // 2
    head_width = width // HEADS
    half_width = width // 2
    score_scale = head_width ** (-0.5)
    experts = dispatcher_projection.shape[1]

    stacked = jnp.concatenate(
        [mixing_projection_back[:, :half_width], mixing_projection_back[:, half_width:]], axis=0
    )
    block = jnp.concatenate(
        [
            a
            for k, w in enumerate((asker_projection, lookup_projection, content_projection))
            for a in (w, stacked[:, PARTS[k][0] : PARTS[k][1]])
        ],
        axis=1,
    )
    blocks = near_exchange(jnp.broadcast_to(block[None], (8, *block.shape)))
    orders = jnp.stack([relative_order(core, me, part) for part in range(3)])

    assigned = token_assignments[0]
    expert_iota = jnp.arange(experts, dtype=jnp.int32)
    chosen = jnp.any(assigned[:, :, None] == expert_iota[None, None, :], axis=1)
    token_iota = jnp.arange(tokens_dev, dtype=jnp.int32)
    earlier = (token_iota[:, None] > token_iota[None, :]).astype(bf16)
    rank = dot(earlier, chosen.astype(bf16))
    kept = chosen & (rank < admitted_route_quota.astype(f32)[None, :])
    sent_counts = jnp.sum(kept.astype(jnp.int32), axis=0, dtype=jnp.int32)
    line_iota = jnp.arange(experts * 8, dtype=jnp.int32)
    line = line_iota % 8
    spread = (expert_iota[:, None] == (line_iota // 8)[None, :]).astype(bf16)
    slot_of_line = dot(jnp.where(kept, rank, -1.0).astype(bf16), spread).astype(jnp.int32)
    main = (slot_of_line == line[None, :]).astype(bf16)
    spare_hit = slot_of_line == (8 + line // 2)[None, :]
    spare = jnp.concatenate(
        [spare_hit & (line % 2 == half)[None, :] for half in range(2)], axis=0
    ).astype(bf16)

    lengths = packed_segment_sizes[0]
    row_positions = jnp.arange(row_len, dtype=jnp.int32)
    doc_ids, doc_offset = doc_places(lengths, row_positions)
    allowed = (doc_ids[None, :] == doc_ids[:, None]) & (
        row_positions[None, :] <= row_positions[:, None]
    )
    cos_table, sin_table = rope_tables(doc_offset, head_width)
    head_shape = (row_len, heads_local, head_width)
    column_start = core * half_width
    query_half_gain = lax.dynamic_slice_in_dim(asker_scale_factor, column_start, half_width)
    key_half_gain = lax.dynamic_slice_in_dim(lookup_scale_factor, column_start, half_width)

    inputs = block_entry_states[0].astype(f32)
    factor_in = rms_factor(inputs)
    normed_in = (inputs * factor_in * mixing_scale_factor).astype(bf16)
    normed_t = whole_row(normed_in, core).T
    normed_rel = reorder(normed_t, orders)
    grad_top_low = block_result_cotangent[0]
    send_grads = to_experts(main, spare, grad_top_low)
    both_cos = jnp.concatenate([cos_table, cos_table], axis=-1)[:, 0]
    both_sin = jnp.concatenate([-sin_table, sin_table], axis=-1)[:, 0]
    blocks, normed_rel, send_grads, both_cos, both_sin = lax.optimization_barrier(
        (blocks, normed_rel, send_grads, both_cos, both_sin)
    )
    blocks = blocks.reshape(8 * block.shape[0], block.shape[1])
    pieces = [[blocks[:, OFFSETS[k] : OFFSETS[k + 1]]] for k in range(3)]
    for k in range(3):
        got = permute_step(pieces[k][0], k, 3)
        pieces[k] = [jnp.concatenate([pieces[k][0], got], axis=0)]
    for k in range(3):
        pieces[k].append(permute_step(pieces[k][0], k, 4))
    for k in range(3):
        pieces[k] += [permute_step(piece, k, 5) for piece in pieces[k]]

    def product(k, i):
        size = width // 4
        return dot_tn(normed_rel[k][i * size : (i + 1) * size], pieces[k][i][:, :half_width])

    partial = [sum(product(k, i) for i in range(3)) for k in range(3)]
    send_grads, *_ = lax.optimization_barrier(
        (send_grads, *partial, *(pieces[k][3] for k in range(3)))
    )
    arrived_grads = exchange(send_grads)
    query_proj, key_proj, value_proj = (partial[k] + product(k, 3) for k in range(3))
    value_flat = value_proj.astype(bf16)
    query_sq, key_sq = lax.psum(
        (jnp.sum(query_proj * query_proj, axis=1), jnp.sum(key_proj * key_proj, axis=1)), "dp"
    )
    queries, keys, mixed_heads = attend(
        query_proj, key_proj, value_flat, (query_sq, key_sq),
        (query_half_gain, key_half_gain), both_cos, both_sin, doc_ids,
    )
    hidden_own, share_other, stacked_output = output_shares(
        mixed_heads, pieces, orders, block_entry_states[0], core
    )
    send_rows, hidden, factor_moe = normed_to_experts(
        main, spare, hidden_own, swap(share_other), specialist_scale_factor
    )

    arrived = exchange(send_rows)
    *late_pieces, queries, keys, scaled_own, _ = lax.optimization_barrier(
        (*pieces, queries, keys, (inputs * factor_in).astype(bf16), send_rows)
    )
    scaled_in = whole_row(scaled_own, core)
    weights = collect(late_pieces, orders)
    mixed_rel = reorder(mixed_heads.T, orders)
    raw_scores = (
        jnp.einsum(
            "qhd,khd->hqk",
            queries.reshape(head_shape),
            keys.reshape(head_shape),
            preferred_element_type=f32,
        )
        * score_scale
    )
    attn_probs = softmax_rows(jnp.where(allowed[None], raw_scores, NEG))
    weights, mixed_rel, attn_probs, scaled_in, arrived = lax.optimization_barrier(
        (weights, mixed_rel, attn_probs, scaled_in, arrived)
    )
    gate_w, up_w, down_w = (
        specialist_switch_tensor[0],
        specialist_widen_tensor[0],
        specialist_shrink_tensor[0],
    )
    top_rows = unpack(arrived_grads)
    plain_act_grad = dot_nt(top_rows, down_w).astype(bf16)
    row_grad, rows_in, gate_pre_grad, up_pre_grad, gated_act, logit_grad = expert_rows(
        arrived, plain_act_grad, gate_w, up_w, dispatcher_projection, core, me
    )
    returned_grads = exchange(row_grad)

    own_counts = jnp.where(
        (jnp.arange(2)[:, None, None] == core) & (expert_iota[None, :, None] == me),
        sent_counts[None, None, :],
        0,
    ).astype(f32)
    early = half_of(
        jnp.concatenate(
            [dot_tn(logit_grad, rows_in), own_counts.reshape(2 * experts * experts // width, width)]
        ),
        core,
    )
    small_rows, small_cols = early.shape[0], half_width // 64
    extra = early.reshape(small_rows, 64, small_cols).transpose(1, 0, 2)
    extra = extra.reshape(64 * 8, -1)
    extra = jnp.pad(extra.astype(bf16), ((0, 0), (0, 256 - extra.shape[1])))
    unit_grads = [
        swap(dot_tn(left, right).astype(bf16))
        for left, right in (
            (rows_in, gate_pre_grad[1]),
            (rows_in, up_pre_grad[1]),
            (gated_act[1], top_rows),
        )
    ]
    send_out, returned_grads, unit_grads = lax.optimization_barrier(
        (expert_results(gated_act, down_w, extra, core), returned_grads, unit_grads)
    )
    hidden_grad, hidden_low, moe_gain_local = from_experts_back(
        main, spare, returned_grads, hidden, factor_moe, specialist_scale_factor, grad_top_low
    )
    returned = exchange(send_out)
    (
        query_scaled, key_scaled, value_proj_low, query_inner, key_inner, query_gain, key_gain,
        grad_full,
    ) = attend_back(
        hidden_low, swap(hidden_low), core, stacked_output, queries, keys, value_flat, attn_probs,
        (query_proj, key_proj), (query_sq, key_sq),
        (query_half_gain, key_half_gain), both_cos, both_sin,
    )
    got = [[], [], []]
    query_inner, key_inner = lax.psum((query_inner[0], key_inner[0]), "dp")
    query_low, key_low, *sent = first_pieces(
        (query_scaled, key_scaled), (query_proj, key_proj), (query_sq, key_sq),
        (query_inner, key_inner), value_proj_low, normed_rel, mixed_rel, grad_full,
    )
    empty_gain = jnp.zeros((width,), f32)
    query_gain_local = lax.dynamic_update_slice_in_dim(empty_gain, query_gain[0], column_start, 0)
    key_gain_local = lax.dynamic_update_slice_in_dim(empty_gain, key_gain[0], column_start, 0)
    lows = (query_low, key_low, value_proj_low)

    for step in (5, 4, 3):
        if step < 5:
            sent = sent_pieces(step, (0, 1, 2), normed_rel, lows, mixed_rel, grad_full, got)
        else:
            sent, unit_grads, share_lows, own_units = lax.optimization_barrier(
                (sent, unit_grads, lows, (gate_pre_grad, up_pre_grad, gated_act))
            )
        for k in range(3):
            got[k].append(permute_step(sent[k], k, step))
        if step == 5:
            gate_weight_grad = dot_tn(rows_in, own_units[0][0]) + unit_grads[0].astype(f32)
            shares = input_shares(share_lows, scaled_in, weights, core)
            attn_gain_local = shares[2][0]
            gains = half_of(
                jnp.stack([attn_gain_local, query_gain_local, key_gain_local, moe_gain_local[0]]), core
            )
            early = jnp.sum(
                returned[:, width * 3 // 2 : width * 3 // 2 + small_rows * small_cols // 8]
                .reshape(64, small_rows * small_cols)
                .astype(f32),
                axis=0,
            )
            count = early.shape[0]
            small = jnp.concatenate([early, gains.reshape(-1)]).astype(bf16)
            small = jnp.pad(small, (0, 6144 - small.shape[0])).reshape(1, 8, 768)
            small = jnp.broadcast_to(small, (64, 8, 768)).reshape(512, 768)
            got, returned, gate_weight_grad, shares, small = (
                lax.optimization_barrier(
                    (
                        got,
                        returned,
                        gate_weight_grad,
                        shares[:2],
                        small,
                    )
                )
            )
            small = exchange(small)
        if step == 4:
            block_output = hidden + from_experts(main, spare, returned, width)
            down_weight_grad = dot_tn(own_units[2][0], top_rows) + unit_grads[2].astype(f32)
            got, shares, block_output, down_weight_grad = lax.optimization_barrier(
                (got, shares, block_output, down_weight_grad)
            )
    up_weight_grad = dot_tn(rows_in, own_units[1][0]) + unit_grads[1].astype(f32)
    got, up_weight_grad, small = lax.optimization_barrier((got, up_weight_grad, small))
    near = near_exchange(near_pieces(normed_rel[0], lows, mixed_rel[0], grad_full, got))
    query_weight_grad, key_weight_grad, value_weight_grad, output_weight_grad = near_total(near)
    normed_in_grad = shares[0] + swap(shares[1]).astype(f32)
    scaled = normed_in_grad * mixing_scale_factor
    input_norm_grad = factor_in * (
        scaled
        - inputs * factor_in * factor_in * jnp.mean(scaled * inputs, axis=-1, keepdims=True)
    )
    input_grad = hidden_grad + input_norm_grad

    small = small.reshape(64, 6144).astype(f32)
    early = (
        small[:, :count]
        .reshape(64, small_rows, small_cols)
        .transpose(1, 0, 2)
        .reshape(small_rows, half_width)
    )
    gains = jnp.sum(small[:, count : count + 4 * half_width], axis=0).reshape(4, half_width)
    totals = beside_other_half(jnp.concatenate([early, gains]), core)
    router_weight_grad, all_counts, gains = totals[:experts].T, totals[experts:-4], totals[-4:]
    got_counts = jnp.sum(
        jnp.where(
            (jnp.arange(2)[:, None, None] == core) & (expert_iota[None, None, :] == me),
            all_counts.reshape(2, experts, experts),
            0.0,
        ),
        axis=(0, 2),
    ).astype(jnp.int32)
    return (
        block_output[None],
        input_grad[None],
        gains[0],
        query_weight_grad,
        key_weight_grad,
        value_weight_grad,
        output_weight_grad,
        gains[1],
        gains[2],
        gains[3],
        router_weight_grad,
        gate_weight_grad[None],
        up_weight_grad[None],
        down_weight_grad[None],
        got_counts[None],
    )


def solution(mesh):
    placed = (
        P("expert", "dp", None),
        P("expert", "dp", None),
        P("expert", "dp", None),
        P("expert", None),
        P(),
        P(),
        P("expert", "dp"),
        P("expert", "dp"),
        P("expert", "dp"),
        P(("dp", "expert"), None),
        P(),
        P(),
        P(),
        P(),
        P("expert", None, None),
        P("expert", None, None),
        P("expert", None, None),
    )
    return jax.shard_map(
        shards,
        mesh=mesh,
        in_specs=placed,
        out_specs=(
            P("expert", "dp", None),
            P("expert", "dp", None),
            P(),
            P("expert", "dp"),
            P("expert", "dp"),
            P("expert", "dp"),
            P(("dp", "expert"), None),
            P(),
            P(),
            P(),
            P(),
            P("expert", None, "dp"),
            P("expert", None, "dp"),
            P("expert", "dp", None),
            P("expert", "dp"),
        ),
        check_vma=False,
    )
```

```python
import functools

import jax
import jax.numpy as jnp
from jax import lax
from jax.experimental import pallas as pl
from jax.experimental.pallas import tpu as pltpu
from jax.sharding import PartitionSpec as P

HEADS = 16
EPS = 1e-05
THETA = 10000.0
NEG = -1e30
BOTH = ("dp", "expert")
PARTS = ((0, 384), (384, 768), (768, 1024))
OFFSETS = (0, 1408, 2816, 4096)

FLIPS = ((1, 4, 16), (3, 12, 48))


def far_flip(core, part, step):
    return FLIPS[1 - core][(step + part) % 3]


def bits_of(chip, first, second):
    return sum(
        (((chip >> (2 * a)) & first) ^ ((chip >> (2 * a + 1)) & second)) << a for a in range(3)
    )


def near_position(core, chip):
    return bits_of(chip, 1, 1) if core == 0 else bits_of(chip, 0, 1)


def far_position(core, chip):
    return bits_of(chip, 0, 1) if core == 0 else bits_of(chip, 1, 1)


def groups_of(own, other):
    groups = []
    for core in range(2):
        for label in range(8):
            chips = [d for d in range(64) if other(core, d) == label]
            groups.append([64 * core + d for d in sorted(chips, key=lambda d: own(core, d))])
    return groups


def near_exchange(rows):
    return lax.all_to_all(
        rows, BOTH, split_axis=0, concat_axis=0, tiled=True,
        axis_index_groups=groups_of(near_position, far_position),
    )


def permute_step(value, part, step):
    pairs = []
    for core in range(2):
        flip = far_flip(core, part, step)
        pairs += [(64 * core + d, 64 * core + (d ^ flip)) for d in range(64)]
    return lax.ppermute(value, BOTH, pairs)


def relative_order(core, me, part):
    index = jnp.arange(64, dtype=jnp.int32)
    chips = []
    for c in range(2):
        low = (index & 7) ^ near_position(c, me)
        chip = me
        for b in range(3):
            chip = chip ^ (((low >> b) & 1) * FLIPS[c][b])
            chip = chip ^ (((index >> (3 + b)) & 1) * far_flip(c, part, 3 + b))
        chips.append(chip)
    return jnp.where(core == 0, chips[0], chips[1])


def reorder_body(order_ref, rows_ref, out_ref):
    for k in range(out_ref.shape[0]):
        for r in range(64):
            out_ref[k, r] = rows_ref[order_ref[k, r]]


def reorder(rows, orders):
    blocks = rows.reshape(64, rows.shape[0] // 64, rows.shape[1])
    count = orders.shape[0]
    out = pl.pallas_call(
        reorder_body,
        grid_spec=pltpu.PrefetchScalarGridSpec(
            num_scalar_prefetch=1,
            grid=(1,),
            in_specs=[pl.BlockSpec(blocks.shape, lambda i, o: (0, 0, 0))],
            out_specs=pl.BlockSpec((count, *blocks.shape), lambda i, o: (0, 0, 0, 0)),
        ),
        out_shape=jax.ShapeDtypeStruct((count, *blocks.shape), rows.dtype),
        compiler_params=pltpu.CompilerParams(vmem_limit_bytes=56 * 1024 * 1024),
    )(orders, blocks)
    return [out[k].reshape(rows.shape) for k in range(count)]


def place_blocks(source, order_ref, k, first, out_ref, columns):
    for r in range(source.shape[0] // 32):
        rows = pl.ds(pl.multiple_of(order_ref[k, first + r] * 32, 32), 32)
        out_ref[rows, columns[0] : columns[1]] = source[r * 32 : (r + 1) * 32, :]


def collect_body(order_ref, *refs):
    pieces, out_ref = refs[:-1], refs[-1]
    count = len(pieces) // 3
    for k in range(3):
        for i in range(count):
            place_blocks(
                pieces[k * count + i], order_ref, k, i * 64 // count, out_ref, (1024 * k, 1024 * k + 1024)
            )


def collect(pieces, orders):
    flat = [piece for part in pieces for piece in part]
    return pl.pallas_call(
        collect_body,
        grid_spec=pltpu.PrefetchScalarGridSpec(
            num_scalar_prefetch=1,
            grid=(1,),
            in_specs=[pl.BlockSpec((a.shape[0], 1024), lambda i, o: (0, 0)) for a in flat],
            out_specs=pl.BlockSpec((64 * 32, 3 * 1024), lambda i, o: (0, 0)),
        ),
        out_shape=jax.ShapeDtypeStruct((64 * 32, 3 * 1024), jnp.bfloat16),
        compiler_params=pltpu.CompilerParams(vmem_limit_bytes=56 * 1024 * 1024),
    )(orders, *flat)


def half_of(rows, core):
    half = rows.shape[1] // 2
    own = lax.dynamic_slice_in_dim(rows, core * half, half, axis=1)
    return own + swap(lax.dynamic_slice_in_dim(rows, (1 - core) * half, half, axis=1))


def beside_other_half(own, core):
    other = swap(own)
    return jnp.concatenate(
        [jnp.where(core == 0, own, other), jnp.where(core == 0, other, own)], axis=1
    )


def swap(value):
    return lax.ppermute(value, "dp", [(0, 1), (1, 0)])


def dot(left, right):
    return jnp.dot(left, right, preferred_element_type=jnp.float32)


def dot_tn(left, right):
    return lax.dot_general(
        left, right, (((0,), (0,)), ((), ())), preferred_element_type=jnp.float32
    )


def dot_nt(left, right):
    return lax.dot_general(
        left, right, (((1,), (1,)), ((), ())), preferred_element_type=jnp.float32
    )


def rms_factor(values):
    return lax.rsqrt(jnp.mean(values * values, axis=-1, keepdims=True) + EPS)


def doc_places(lengths, places):
    ends = jnp.cumsum(lengths, dtype=jnp.int32)
    done = ends[None, :] <= places[:, None]
    doc_ids = jnp.sum(done.astype(jnp.int32), axis=1, dtype=jnp.int32)
    starts = jnp.sum(jnp.where(done, lengths[None, :], 0), axis=1, dtype=jnp.int32)
    return (doc_ids, places - starts)


def rope_tables(offsets, head_width):
    half_width = head_width // 2
    inverse = THETA ** (-jnp.arange(half_width, dtype=jnp.float32) * 2.0 / head_width)
    angles = offsets.astype(jnp.float32)[..., None] * inverse
    return (jnp.cos(angles)[..., None, :], jnp.sin(angles)[..., None, :])


def softmax_rows(values):
    exponent = jnp.exp(values - jnp.max(values, axis=-1, keepdims=True))
    return exponent / jnp.sum(exponent, axis=-1, keepdims=True)


def half_picker(count, half):
    rows = lax.broadcasted_iota(jnp.int32, (count // 2, count), 0)
    cols = lax.broadcasted_iota(jnp.int32, (count // 2, count), 1)
    return (cols == 2 * rows + half).astype(jnp.float32).astype(jnp.bfloat16)


def unpack_block(packed):
    count, width = packed.shape[0], packed.shape[1] * 2 // 3
    spare = packed[:, width:]
    rest = [dot(half_picker(count, h), spare).astype(jnp.bfloat16) for h in range(2)]
    return packed[:, :width], rest


def pack_block(rows, out_ref):
    count, width = out_ref.shape[0], rows.shape[1]
    half = width // 2
    out_ref[:, :width] = rows[:count]
    out_ref[:, width : width + half] = (
        dot_tn(half_picker(count, 0), rows[count:, :half])
        + dot_tn(half_picker(count, 1), rows[count:, half:])
    ).astype(jnp.bfloat16)


def unpack_body(packed_ref, rows_ref):
    main, rest = unpack_block(packed_ref[...])
    count, width = main.shape
    rows_ref[:count] = main
    rows_ref[count:, : width // 2] = rest[0]
    rows_ref[count:, width // 2 :] = rest[1]


def unpack(packed):
    count, width = packed.shape[0], packed.shape[1] * 2 // 3
    return pl.pallas_call(
        unpack_body,
        out_shape=jax.ShapeDtypeStruct((count * 3 // 2, width), jnp.bfloat16),
        compiler_params=pltpu.CompilerParams(vmem_limit_bytes=56 * 1024 * 1024),
    )(packed)


def send_body(main_ref, spare_ref, rows_ref, out_ref):
    width = rows_ref.shape[1]
    half, count = width // 2, rows_ref.shape[0]
    out_ref[:, :width] = dot_tn(main_ref[...], rows_ref[...]).astype(jnp.bfloat16)
    out_ref[:, width:] = (
        dot_tn(spare_ref[:count], rows_ref[:, :half])
        + dot_tn(spare_ref[count:], rows_ref[:, half:])
    ).astype(jnp.bfloat16)


def to_experts(main, spare, rows):
    tokens, lines = main.shape
    width, block = rows.shape[1], lines // 2
    return pl.pallas_call(
        send_body,
        grid=(2,),
        in_specs=[
            pl.BlockSpec((tokens, block), lambda i: (0, i)),
            pl.BlockSpec((2 * tokens, block), lambda i: (0, i)),
            pl.BlockSpec((tokens, width), lambda i: (0, 0)),
        ],
        out_specs=pl.BlockSpec((block, width * 3 // 2), lambda i: (i, 0)),
        out_shape=jax.ShapeDtypeStruct((lines, width * 3 // 2), jnp.bfloat16),
        compiler_params=pltpu.CompilerParams(vmem_limit_bytes=56 * 1024 * 1024),
    )(main, spare, rows)


def send_normed_body(
    main_ref, spare_ref, own_ref, other_ref, gain_ref, out_ref, hidden_ref, factor_ref, normed
):
    @pl.when(pl.program_id(0) == 0)
    def _():
        hidden = own_ref[...] + other_ref[...].astype(jnp.float32)
        factor = rms_factor(hidden)
        hidden_ref[...] = hidden
        factor_ref[...] = factor
        normed[...] = (hidden * factor * gain_ref[...]).astype(jnp.bfloat16)

    send_body(main_ref, spare_ref, normed, out_ref)


def normed_to_experts(main, spare, own, other, gain):
    tokens, lines = main.shape
    width, block = own.shape[1], lines // 2
    whole = pl.BlockSpec((tokens, width), lambda i: (0, 0))
    return pl.pallas_call(
        send_normed_body,
        grid=(2,),
        in_specs=[
            pl.BlockSpec((tokens, block), lambda i: (0, i)),
            pl.BlockSpec((2 * tokens, block), lambda i: (0, i)),
            whole,
            whole,
            pl.BlockSpec((1, width), lambda i: (0, 0)),
        ],
        out_specs=[
            pl.BlockSpec((block, width * 3 // 2), lambda i: (i, 0)),
            whole,
            pl.BlockSpec((tokens, 1), lambda i: (0, 0)),
        ],
        out_shape=[
            jax.ShapeDtypeStruct((lines, width * 3 // 2), jnp.bfloat16),
            jax.ShapeDtypeStruct((tokens, width), jnp.float32),
            jax.ShapeDtypeStruct((tokens, 1), jnp.float32),
        ],
        scratch_shapes=[pltpu.VMEM((tokens, width), jnp.bfloat16)],
        compiler_params=pltpu.CompilerParams(vmem_limit_bytes=56 * 1024 * 1024),
    )(main, spare, own, other, gain[None])


def combine_body(main_ref, spare_ref, lines_ref, out_ref):
    tokens, width = out_ref.shape
    half = width // 2
    spare_lines = lines_ref[:, width : width + half]
    out_ref[:, :half] = dot(main_ref[...], lines_ref[:, :half]) + dot(
        spare_ref[:tokens], spare_lines
    )
    out_ref[:, half:] = dot(main_ref[...], lines_ref[:, half:width]) + dot(
        spare_ref[tokens:], spare_lines
    )


def from_experts(main, spare, lines, width):
    return pl.pallas_call(
        combine_body,
        out_shape=jax.ShapeDtypeStruct((main.shape[0], width), jnp.float32),
        compiler_params=pltpu.CompilerParams(vmem_limit_bytes=56 * 1024 * 1024),
    )(main, spare, lines)


def combine_back_body(
    main_ref, spare_ref, lines_ref, hidden_ref, factor_ref, gain_ref, top_ref,
    grad_ref, low_ref, gain_grad_ref, moe_ref,
):
    combine_body(main_ref, spare_ref, lines_ref, moe_ref)
    grad, hidden, factor = moe_ref[...], hidden_ref[...], factor_ref[...]
    scaled = grad * gain_ref[...]
    inner = jnp.mean(scaled * hidden, axis=-1, keepdims=True)
    normed = hidden * factor
    back = top_ref[...].astype(jnp.float32) + factor * (scaled - normed * (factor * inner))
    grad_ref[...] = back
    low_ref[...] = back.astype(jnp.bfloat16)
    gain_grad_ref[...] = jnp.sum(grad * normed, axis=0, keepdims=True)


def from_experts_back(main, spare, lines, hidden, factor, gain, top):
    tokens, width = hidden.shape
    return pl.pallas_call(
        combine_back_body,
        out_shape=[
            jax.ShapeDtypeStruct((tokens, width), jnp.float32),
            jax.ShapeDtypeStruct((tokens, width), jnp.bfloat16),
            jax.ShapeDtypeStruct((1, width), jnp.float32),
        ],
        scratch_shapes=[pltpu.VMEM((tokens, width), jnp.float32)],
        compiler_params=pltpu.CompilerParams(vmem_limit_bytes=56 * 1024 * 1024),
    )(main, spare, lines, hidden, factor, gain[None], top)


def row_body(core_ref, own_ref, other_ref, out_ref):
    count = own_ref.shape[0]
    out_ref[pl.ds(pl.multiple_of(core_ref[0] * count, count), count), :] = own_ref[...]
    out_ref[pl.ds(pl.multiple_of((1 - core_ref[0]) * count, count), count), :] = other_ref[...]


def whole_row(own, core):
    count, width = own.shape
    block = pl.BlockSpec((count, width), lambda i, c: (0, 0))
    return pl.pallas_call(
        row_body,
        grid_spec=pltpu.PrefetchScalarGridSpec(
            num_scalar_prefetch=1,
            grid=(1,),
            in_specs=[block] * 2,
            out_specs=pl.BlockSpec((2 * count, width), lambda i, c: (0, 0)),
        ),
        out_shape=jax.ShapeDtypeStruct((2 * count, width), own.dtype),
        compiler_params=pltpu.CompilerParams(vmem_limit_bytes=56 * 1024 * 1024),
    )(core[None].astype(jnp.int32), own, swap(own))


def out_body(core_ref, act_ref, own_ref, other_ref, extra_ref, out_ref):
    rows = dot(act_ref[0], own_ref[...]) + dot(act_ref[1], other_ref[...])
    pack_block(rows.astype(jnp.bfloat16), out_ref)
    out_ref[:, rows.shape[1] * 3 // 2 :] = extra_ref[...]


def expert_results(acts, down_w, extra, core):
    _, count, units = acts.shape
    width = down_w.shape[1]
    shape = (count * 2 // 3, width * 3 // 2 + extra.shape[1])
    return pl.pallas_call(
        out_body,
        grid_spec=pltpu.PrefetchScalarGridSpec(
            num_scalar_prefetch=1,
            grid=(1,),
            in_specs=[
                pl.BlockSpec((2, count, units), lambda i, c: (0, 0, 0)),
                pl.BlockSpec((units, width), lambda i, c: (c[0], 0)),
                pl.BlockSpec((units, width), lambda i, c: (1 - c[0], 0)),
                pl.BlockSpec(extra.shape, lambda i, c: (0, 0)),
            ],
            out_specs=pl.BlockSpec(shape, lambda i, c: (0, 0)),
        ),
        out_shape=jax.ShapeDtypeStruct(shape, jnp.bfloat16),
        compiler_params=pltpu.CompilerParams(vmem_limit_bytes=56 * 1024 * 1024),
        cost_estimate=pl.CostEstimate(
            flops=4 * count * width * units, bytes_accessed=12 * 1024 * 1024, transcendentals=0
        ),
    )(core[None].astype(jnp.int32), acts, down_w, down_w, extra)


def as_column(row):
    return jnp.broadcast_to(row, (8, row.shape[1])).T[:, :1]


def as_row(column):
    return jnp.broadcast_to(column, (column.shape[0], 128)).T[:1, :]


def expert_body(
    core_ref, mine_ref, packed_ref, act_grad_ref, gate_w_ref, up_w_ref, router_ref,
    back_ref, x_out, gate_out_ref, up_out_ref, act_out_ref, logit_ref,
    x_ref, total, probs_ref, gate_ref, gate_grad_ref, sem,
):
    f32, bf16 = jnp.float32, jnp.bfloat16
    step = pl.program_id(0)
    x_copy = pltpu.make_async_copy(x_ref, x_out, sem)

    @pl.when(step == 0)
    def _():
        unpack_body(packed_ref, x_ref)
        x_copy.start()
        probs = softmax_rows(dot(x_ref[...], router_ref[...]))
        probs_ref[...] = probs
        gate_ref[...] = jnp.sum(probs * mine_ref[...], axis=1, keepdims=True)
        gate_grad_ref[...] = jnp.zeros_like(gate_grad_ref)
        total[...] = jnp.zeros_like(total)

    gate_w, up_w = gate_w_ref[...], up_w_ref[...]
    size = x_ref.shape[0] // 3
    for k in range(3):
        rows = pl.ds(k * size, size)
        x, gate = x_ref[rows, :], gate_ref[rows, :]
        gate_pre, up_pre = dot(x, gate_w), dot(x, up_w)
        plain = act_grad_ref[rows, :].astype(f32)
        sigmoid = 1.0 / (1.0 + jnp.exp(-gate_pre))
        silu = gate_pre * sigmoid
        act = silu * up_pre
        gate_grad = jnp.sum(act * plain, axis=1, keepdims=True)
        act_grad = gate * plain
        gate_pre_grad = (act_grad * up_pre * sigmoid * (1.0 + gate_pre * (1.0 - sigmoid))).astype(
            bf16
        )
        up_pre_grad = (act_grad * silu).astype(bf16)
        gate_out_ref[0, rows, :] = gate_pre_grad
        up_out_ref[0, rows, :] = up_pre_grad
        act_out_ref[0, rows, :] = (gate * act).astype(bf16)
        part = dot_nt(gate_pre_grad, gate_w) + dot_nt(up_pre_grad, up_w)

        gate_grad_ref[rows, :] += gate_grad
        total[rows, :] += part

    @pl.when(step == pl.num_programs(0) - 1)
    def _():
        logit = (gate_grad_ref[...] * gate_ref[...] * (mine_ref[...] - probs_ref[...])).astype(bf16)
        logit_ref[...] = logit
        pack_block((total[...] + dot_nt(logit, router_ref[...])).astype(bf16), back_ref)
        x_copy.wait()


def expert_rows(packed, plain_act_grad, gate_w, up_w, router, core, me):
    f32, bf16 = jnp.float32, jnp.bfloat16
    lines = packed.shape[0]
    width, units = gate_w.shape
    count, experts = lines * 3 // 2, router.shape[1]
    tile = units // 4
    mine = (jnp.arange(experts, dtype=jnp.int32) == me).astype(f32)[None, :]
    halves = jax.ShapeDtypeStruct((2, count, units // 2), bf16)
    half_spec = pl.BlockSpec((1, count, tile), lambda j, c: ((j // 2 + c[0]) % 2, 0, j % 2))
    return pl.pallas_call(
        expert_body,
        grid_spec=pltpu.PrefetchScalarGridSpec(
            num_scalar_prefetch=1,
            grid=(4,),
            in_specs=[
                pl.BlockSpec((1, experts), lambda j, c: (0, 0)),
                pl.BlockSpec(packed.shape, lambda j, c: (0, 0)),
                pl.BlockSpec((count, tile), lambda j, c: (0, j)),
                pl.BlockSpec((width, tile), lambda j, c: (0, j)),
                pl.BlockSpec((width, tile), lambda j, c: (0, j)),
                pl.BlockSpec((width, experts), lambda j, c: (0, 0)),
            ],
            out_specs=[
                pl.BlockSpec(packed.shape, lambda j, c: (0, 0)),
                pl.BlockSpec(memory_space=pl.ANY),
                half_spec,
                half_spec,
                half_spec,
                pl.BlockSpec((count, experts), lambda j, c: (0, 0)),
            ],
            scratch_shapes=[
                pltpu.VMEM((count, width), bf16),
                pltpu.VMEM((count, width), f32),
                pltpu.VMEM((count, experts), f32),
                pltpu.VMEM((count, 1), f32),
                pltpu.VMEM((count, 1), f32),
                pltpu.SemaphoreType.DMA,
            ],
        ),
        out_shape=[
            jax.ShapeDtypeStruct(packed.shape, bf16),
            jax.ShapeDtypeStruct((count, width), bf16),
            halves,
            halves,
            halves,
            jax.ShapeDtypeStruct((count, experts), bf16),
        ],
        compiler_params=pltpu.CompilerParams(vmem_limit_bytes=60 * 1024 * 1024),
        cost_estimate=pl.CostEstimate(
            flops=8 * count * width * units, bytes_accessed=24 * 1024 * 1024, transcendentals=count * units
        ),
    )(core[None].astype(jnp.int32), mine, packed, plain_act_grad, gate_w, up_w, router)


def part_sums(part, left, low, heads, grad, got):
    start, stop = PARTS[part]
    blocks = left.shape[0] // 32
    half = grad.shape[1] // 2
    main = dot(left, low).reshape(blocks, 32, low.shape[1])
    sides = [
        dot(heads, grad[:, h * half + start : h * half + stop]).reshape(blocks, 16, stop - start)
        for h in range(2)
    ]
    for g in got:
        main = main + g[:, :, : low.shape[1]].astype(jnp.float32)
        sides = [
            sides[h] + g[:, 16 * h : 16 * h + 16, low.shape[1] :].astype(jnp.float32)
            for h in range(2)
        ]
    return main, sides


def store_piece(part, left_ref, low, heads_ref, grad, got, out_ref):
    main, sides = part_sums(part, left_ref[...], low, heads_ref[...], grad, [g[...] for g in got])
    width = main.shape[2]
    out_ref[:, :, :width] = main.astype(jnp.bfloat16)
    for h in range(2):
        out_ref[:, 16 * h : 16 * h + 16, width:] = sides[h].astype(jnp.bfloat16)


def sent_body(parts, count, *refs):
    n = len(parts)
    lefts, lows, heads, grad = refs[:n], refs[n : 2 * n], refs[2 * n : 3 * n], refs[3 * n][...]
    got, outs = refs[3 * n + 1 : 3 * n + 1 + n * count], refs[3 * n + 1 + n * count :]
    for i, k in enumerate(parts):
        part_got = got[i * count : (i + 1) * count]
        store_piece(k, lefts[i], lows[i][...], heads[i], grad, part_got, outs[i])


def piece_specs(step, parts, lefts, heads, grad, count):
    blocks = 1 << step
    chunk = 16 if blocks == 32 else 8
    first = blocks // chunk
    ahead = lambda i: (first + i, 0)
    ahead3 = lambda i: (first + i, 0, 0)
    columns = [OFFSETS[k + 1] - OFFSETS[k] for k in parts]
    return (
        blocks // chunk,
        [pl.BlockSpec((chunk * 32, lefts[0].shape[1]), ahead) for _ in parts],
        [pl.BlockSpec((chunk * 16, heads[0].shape[1]), ahead) for _ in parts]
        + [pl.BlockSpec(grad.shape, lambda i: (0, 0))]
        + [pl.BlockSpec((chunk, 32, c), ahead3) for c in columns for _ in range(count)],
        [pl.BlockSpec((chunk, 32, c), lambda i: (i, 0, 0)) for c in columns],
        [jax.ShapeDtypeStruct((blocks, 32, c), jnp.bfloat16) for c in columns],
    )


def sent_pieces(step, parts, lefts, lows, heads, grad, got):
    count = len(got[0])
    steps, left_specs, other_specs, out_specs, out_shape = piece_specs(
        step, parts, lefts, heads, grad, count
    )
    return pl.pallas_call(
        functools.partial(sent_body, parts, count),
        grid=(steps,),
        in_specs=left_specs + [pl.BlockSpec(a.shape, lambda i: (0, 0)) for a in lows] + other_specs,
        out_specs=out_specs,
        out_shape=out_shape,
        compiler_params=pltpu.CompilerParams(vmem_limit_bytes=56 * 1024 * 1024),
    )(
        *(lefts[k] for k in parts),
        *lows,
        *(heads[k] for k in parts),
        grad,
        *(g for k in parts for g in got[k]),
    )


def first_body(
    scaled_query, scaled_key, query_proj, key_proj, query_sq, key_sq, query_inner, key_inner,
    value_low, left0, left1, left2, heads0, heads1, heads2, grad_ref,
    query_low, key_low, out0, out1, out2,
):
    @pl.when(pl.program_id(0) == 0)
    def _():
        for scaled, proj, squares, inner, low in (
            (scaled_query, query_proj, query_sq, query_inner, query_low),
            (scaled_key, key_proj, key_sq, key_inner, key_low),
        ):
            row = factor_of(squares[...])
            factor = as_column(row)
            share = as_column(row * row * (inner[...] / 2048))
            low[...] = (factor * (scaled[...] - proj[...] * share)).astype(jnp.bfloat16)

    grad = grad_ref[...]
    store_piece(0, left0, query_low[...], heads0, grad, [], out0)
    store_piece(1, left1, key_low[...], heads1, grad, [], out1)
    store_piece(2, left2, value_low[...], heads2, grad, [], out2)


def first_pieces(scaled, projections, squares, inners, value_low, lefts, heads, grad):
    steps, left_specs, other_specs, out_specs, out_shape = piece_specs(
        5, (0, 1, 2), lefts, heads, grad, 0
    )
    whole = pl.BlockSpec(scaled[0].shape, lambda i: (0, 0))
    row = pl.BlockSpec((1, scaled[0].shape[0]), lambda i: (0, 0))
    low = jax.ShapeDtypeStruct(scaled[0].shape, jnp.bfloat16)
    return pl.pallas_call(
        first_body,
        grid=(steps,),
        in_specs=[whole] * 4 + [row] * 4 + [whole] + left_specs + other_specs,
        out_specs=[whole] * 2 + out_specs,
        out_shape=[low] * 2 + out_shape,
        compiler_params=pltpu.CompilerParams(vmem_limit_bytes=56 * 1024 * 1024),
    )(
        *scaled,
        *projections,
        *(q[None] for q in squares),
        *(q[None] for q in inners),
        value_low,
        *lefts,
        *heads,
        grad,
    )


def near_body(left_ref, *refs):
    lows, heads_ref, grad_ref, got, out_ref = refs[:3], refs[3], refs[4], refs[5:14], refs[14]
    for k in range(3):
        main, sides = part_sums(
            k, left_ref[...], lows[k][...], heads_ref[...], grad_ref[...],
            [g[...] for g in got[3 * k : 3 * k + 3]],
        )
        width, start, stop = main.shape[2], OFFSETS[k], OFFSETS[k + 1]
        for r in range(8):
            out_ref[r, :, start : start + width] = main[r].astype(jnp.bfloat16)
            for h in range(2):
                out_ref[r, 16 * h : 16 * h + 16, start + width : stop] = sides[h][r].astype(
                    jnp.bfloat16
                )


def near_pieces(left, lows, heads, grad, got):
    fixed = lambda i: (0, 0)
    return pl.pallas_call(
        near_body,
        grid=(1,),
        in_specs=[pl.BlockSpec((8 * 32, left.shape[1]), fixed)]
        + [pl.BlockSpec(a.shape, fixed) for a in lows]
        + [pl.BlockSpec((8 * 16, heads.shape[1]), fixed), pl.BlockSpec(grad.shape, fixed)]
        + [
            pl.BlockSpec((8, 32, g.shape[2]), lambda i: (0, 0, 0))
            for k in range(3)
            for g in got[k]
        ],
        out_specs=pl.BlockSpec((8, 32, OFFSETS[3]), lambda i: (0, 0, 0)),
        out_shape=jax.ShapeDtypeStruct((8, 32, OFFSETS[3]), jnp.bfloat16),
        compiler_params=pltpu.CompilerParams(vmem_limit_bytes=56 * 1024 * 1024),
    )(left, *lows, heads, grad, *(g for k in range(3) for g in got[k]))


def total_body(near_ref, *outs):
    out_ref = outs[3]
    half = out_ref.shape[1] // 2
    for k in range(3):
        start, stop = OFFSETS[k], OFFSETS[k + 1]
        total = near_ref[0, :, start:stop].astype(jnp.float32)
        for r in range(1, near_ref.shape[0]):
            total = total + near_ref[r, :, start:stop].astype(jnp.float32)
        outs[k][...] = total[:, :half]
        for h in range(2):
            out_ref[:, h * half + PARTS[k][0] : h * half + PARTS[k][1]] = total[
                16 * h : 16 * h + 16, half:
            ]


def near_total(near):
    rows, half = near.shape[1], 1024
    return pl.pallas_call(
        total_body,
        out_shape=[jax.ShapeDtypeStruct((rows, half), jnp.float32)] * 3
        + [jax.ShapeDtypeStruct((rows // 2, 2 * half), jnp.float32)],
        compiler_params=pltpu.CompilerParams(vmem_limit_bytes=56 * 1024 * 1024),
    )(near)


def exchange(rows):
    return lax.all_to_all(rows, "expert", split_axis=0, concat_axis=0, tiled=True)


def own_and_other(core_ref, total, own_ref, other_ref):
    count = own_ref.shape[0]
    own_ref[...] = total[pl.ds(pl.multiple_of(core_ref[0] * count, count), count), :]
    other_ref[...] = total[
        pl.ds(pl.multiple_of((1 - core_ref[0]) * count, count), count), :
    ].astype(other_ref.dtype)


def output_body(core_ref, order_ref, heads_ref, inputs_ref, *refs):
    pieces, (own_ref, other_ref, stacked_out) = refs[:12], refs[12:15]
    scratch, stacked, total, sem, out_sem = refs[15:27], refs[27], refs[28], refs[29], refs[30]
    half = heads_ref.shape[1]
    copies = []
    for i in range(12):
        copies.append(
            pltpu.make_async_copy(pieces[i].at[:, half : pieces[i].shape[1]], scratch[i], sem.at[i])
        )
        copies[i].start()
    for i in range(12):
        copies[i].wait()
        k, first = i // 4, i % 4 * 16
        for r in range(16):
            rows = pl.ds(pl.multiple_of(order_ref[k, first + r] * 16, 16), 16)
            for h in range(2):
                stacked[h, rows, PARTS[k][0] : PARTS[k][1]] = scratch[i][
                    r * 32 + h * 16 : r * 32 + h * 16 + 16, :
                ]
    copy_out = pltpu.make_async_copy(stacked, stacked_out, out_sem)
    copy_out.start()
    for h in range(2):
        total[:, h * half : (h + 1) * half] = dot(heads_ref[...], stacked[h])
    own_and_other(core_ref, total, own_ref, other_ref)
    own_ref[...] += inputs_ref[...].astype(jnp.float32)
    copy_out.wait()


def output_shares(heads, pieces, orders, inputs, core):
    tokens, width = inputs.shape
    half = width // 2
    flat = [piece for part in pieces for piece in part]
    return pl.pallas_call(
        output_body,
        grid_spec=pltpu.PrefetchScalarGridSpec(
            num_scalar_prefetch=2,
            grid=(1,),
            in_specs=[
                pl.BlockSpec((2 * tokens, half), lambda i, c, o: (0, 0)),
                pl.BlockSpec((tokens, width), lambda i, c, o: (0, 0)),
            ]
            + [pl.BlockSpec(memory_space=pl.ANY)] * 12,
            out_specs=[pl.BlockSpec((tokens, width), lambda i, c, o: (0, 0))] * 2
            + [pl.BlockSpec(memory_space=pl.ANY)],
            scratch_shapes=[pltpu.VMEM((a.shape[0], a.shape[1] - half), jnp.bfloat16) for a in flat]
            + [
                pltpu.VMEM((2, half, half), jnp.bfloat16),
                pltpu.VMEM((2 * tokens, width), jnp.float32),
                pltpu.SemaphoreType.DMA((12,)),
                pltpu.SemaphoreType.DMA,
            ],
        ),
        out_shape=[
            jax.ShapeDtypeStruct((tokens, width), jnp.float32),
            jax.ShapeDtypeStruct((tokens, width), jnp.bfloat16),
            jax.ShapeDtypeStruct((2, half, half), jnp.bfloat16),
        ],
        compiler_params=pltpu.CompilerParams(vmem_limit_bytes=56 * 1024 * 1024),
    )(core[None].astype(jnp.int32), orders, heads, inputs, *flat)


def factor_of(squares):
    return lax.rsqrt(squares / 2048 + EPS)


def attend_body(
    query_ref, key_ref, value_ref, query_sq_ref, key_sq_ref, query_gain_ref, key_gain_ref,
    cos_ref, sin_ref, doc_ref, doc_row_ref, queries_ref, keys_ref, mixed_ref,
    query_factor_ref, key_factor_ref,
):
    bf16 = jnp.bfloat16
    length, head_width = cos_ref.shape
    cos, sin = cos_ref[...], sin_ref[...]

    @pl.when(pl.program_id(0) == 0)
    def _():
        query_factor_ref[...] = as_column(factor_of(query_sq_ref[...]))
        key_factor_ref[...] = as_column(factor_of(key_sq_ref[...]))

    def turned(x):
        return x * cos + pltpu.roll(x, head_width // 2, 1) * sin

    rows = lax.broadcasted_iota(jnp.int32, (length, length), 0)
    cols = lax.broadcasted_iota(jnp.int32, (length, length), 1)
    allowed = (doc_ref[...] == doc_row_ref[...]) & (cols <= rows)
    for head in range(query_ref.shape[1] // head_width):
        at = slice(head * head_width, (head + 1) * head_width)
        queries = turned(query_ref[:, at] * query_factor_ref[...] * query_gain_ref[:, at]).astype(bf16)
        keys = turned(key_ref[:, at] * key_factor_ref[...] * key_gain_ref[:, at]).astype(bf16)
        queries_ref[:, at] = queries
        keys_ref[:, at] = keys
        scores = jnp.where(allowed, dot_nt(queries, keys) * head_width ** (-0.5), NEG)
        mixed_ref[:, at] = dot(softmax_rows(scores).astype(bf16), value_ref[:, at]).astype(bf16)


def attend(query, key, value, squares, gains, cos, sin, docs):
    length, width = query.shape
    head_width = cos.shape[1]
    heads = 2
    by_head = pl.BlockSpec((length, heads * head_width), lambda h: (0, h))
    column = pl.BlockSpec((length, 1), lambda h: (0, 0))
    row = pl.BlockSpec((1, length), lambda h: (0, 0))
    gain = pl.BlockSpec((1, heads * head_width), lambda h: (0, h))
    table = pl.BlockSpec((length, head_width), lambda h: (0, 0))
    return pl.pallas_call(
        attend_body,
        grid=(width // head_width // heads,),
        in_specs=[by_head] * 3 + [row] * 2 + [gain] * 2 + [table] * 2 + [column, row],
        out_specs=[by_head] * 3,
        out_shape=[jax.ShapeDtypeStruct((length, width), jnp.bfloat16)] * 3,
        scratch_shapes=[pltpu.VMEM((length, 1), jnp.float32)] * 2,
        compiler_params=pltpu.CompilerParams(vmem_limit_bytes=56 * 1024 * 1024),
    )(query, key, value, *(q[None] for q in squares), *(g[None] for g in gains), cos, sin, docs[:, None], docs[None])


def attend_back_body(
    core_ref, own_ref, other_ref, weight_ref, queries_ref, keys_ref, value_ref, probs_ref,
    query_ref, key_ref, query_sq_ref, key_sq_ref, query_gain_ref, key_gain_ref, cos_ref, sin_ref,
    query_out, key_out, value_out, query_inner_row, key_inner_row, query_gain_out, key_gain_out,
    grad_ref, query_factor_ref, key_factor_ref, query_inner, key_inner,
):
    bf16 = jnp.bfloat16
    head_width = cos_ref.shape[1]
    cos, sin = cos_ref[...], sin_ref[...]
    half, width = grad_ref.shape[1] // 2, query_ref.shape[1]
    @pl.when(pl.program_id(0) == 0)
    def _():
        row_body(core_ref, own_ref, other_ref, grad_ref)
        query_factor_ref[...] = as_column(factor_of(query_sq_ref[...]))
        key_factor_ref[...] = as_column(factor_of(key_sq_ref[...]))
        query_inner[...] = jnp.zeros_like(query_inner)
        key_inner[...] = jnp.zeros_like(key_inner)

    all_mixed = sum(
        dot_nt(grad_ref[:, h * half : (h + 1) * half], weight_ref[h]) for h in range(2)
    ).astype(bf16)

    for head in range(width // head_width):
        at = slice(head * head_width, (head + 1) * head_width)
        mixed, probs = all_mixed[:, at], probs_ref[head]
        probs_grad = dot_nt(mixed, value_ref[:, at])
        inner = jnp.sum(probs * probs_grad, axis=-1, keepdims=True)
        score_grad = (probs * (probs_grad - inner)).astype(bf16)
        value_out[:, at] = dot_tn(probs.astype(bf16), mixed).astype(bf16)
        for grad, proj_ref, factor_ref, gain_ref, out_ref, inner_ref, gain_out in (
            (
                dot(score_grad, keys_ref[:, at]),
                query_ref, query_factor_ref, query_gain_ref, query_out, query_inner, query_gain_out,
            ),
            (
                dot_tn(score_grad, queries_ref[:, at]),
                key_ref, key_factor_ref, key_gain_ref, key_out, key_inner, key_gain_out,
            ),
        ):
            grad = grad * head_width ** (-0.5)
            grad = grad * cos - pltpu.roll(grad, head_width // 2, 1) * sin
            proj = proj_ref[:, at]
            gain_out[:, at] = jnp.sum(grad * proj * factor_ref[...], axis=0, keepdims=True)
            grad = grad * gain_ref[:, at]
            out_ref[:, at] = grad
            inner_ref[...] += jnp.sum(grad * proj, axis=1, keepdims=True)

    @pl.when(pl.program_id(0) == pl.num_programs(0) - 1)
    def _():
        query_inner_row[...] = as_row(query_inner[...])
        key_inner_row[...] = as_row(key_inner[...])


def attend_back(own, other, core, stacked, queries, keys, value, probs, projections, squares, gains, cos, sin):
    length, width = value.shape
    head_width = cos.shape[1]
    heads = 2
    by_head = pl.BlockSpec((length, heads * head_width), lambda h, c: (0, h))
    row = pl.BlockSpec((1, length), lambda h, c: (0, 0))
    gain = pl.BlockSpec((1, heads * head_width), lambda h, c: (0, h))
    table = pl.BlockSpec((length, head_width), lambda h, c: (0, 0))
    f32 = jnp.float32
    return pl.pallas_call(
        attend_back_body,
        grid_spec=pltpu.PrefetchScalarGridSpec(
            num_scalar_prefetch=1,
            grid=(width // head_width // heads,),
            in_specs=[
            pl.BlockSpec(own.shape, lambda h, c: (0, 0)),
            pl.BlockSpec(own.shape, lambda h, c: (0, 0)),
            pl.BlockSpec((2, heads * head_width, width), lambda h, c: (0, h, 0)),
            *[by_head] * 3,
            pl.BlockSpec((heads, length, length), lambda h, c: (h, 0, 0)),
            *[by_head] * 2,
            *[row] * 2,
            *[gain] * 2,
            *[table] * 2,
        ],
        out_specs=[by_head] * 3 + [row] * 2 + [gain] * 2
        + [pl.BlockSpec((length, own.shape[1]), lambda h, c: (0, 0))],
            scratch_shapes=[pltpu.VMEM((length, 1), f32)] * 4,
        ),
        out_shape=[
            jax.ShapeDtypeStruct((length, width), f32),
            jax.ShapeDtypeStruct((length, width), f32),
            jax.ShapeDtypeStruct((length, width), jnp.bfloat16),
            jax.ShapeDtypeStruct((1, length), f32),
            jax.ShapeDtypeStruct((1, length), f32),
            jax.ShapeDtypeStruct((1, width), f32),
            jax.ShapeDtypeStruct((1, width), f32),
            jax.ShapeDtypeStruct((length, own.shape[1]), jnp.bfloat16),
        ],
        compiler_params=pltpu.CompilerParams(vmem_limit_bytes=56 * 1024 * 1024),
    )(core[None].astype(jnp.int32), own, other, stacked, queries, keys, value, probs, *projections, *(q[None] for q in squares), *(g[None] for g in gains), cos, sin)


def share_body(
    core_ref, query_ref, key_ref, value_ref, scaled_ref, weights_ref,
    own_ref, other_ref, gain_ref, total,
):
    total[...] = sum(
        dot_nt(low_ref[...], weights_ref[:, 1024 * k : 1024 * k + 1024])
        for k, low_ref in enumerate((query_ref, key_ref, value_ref))
    )
    own_and_other(core_ref, total, own_ref, other_ref)
    gain_ref[...] = jnp.sum(
        total[...] * scaled_ref[...].astype(jnp.float32), axis=0, keepdims=True
    )


def input_shares(lows, scaled, weights, core):
    tokens, width = lows[0].shape[0] // 2, weights.shape[0]
    tile = width // 8
    return pl.pallas_call(
        share_body,
        grid_spec=pltpu.PrefetchScalarGridSpec(
            num_scalar_prefetch=1,
            grid=(8,),
            in_specs=[
                *(pl.BlockSpec(a.shape, lambda i, c: (0, 0)) for a in lows),
                pl.BlockSpec((2 * tokens, tile), lambda i, c: (0, i)),
                pl.BlockSpec((tile, weights.shape[1]), lambda i, c: (i, 0)),
            ],
            out_specs=[pl.BlockSpec((tokens, tile), lambda i, c: (0, i))] * 2
            + [pl.BlockSpec((1, tile), lambda i, c: (0, i))],
            scratch_shapes=[pltpu.VMEM((2 * tokens, tile), jnp.float32)],
        ),
        out_shape=[
            jax.ShapeDtypeStruct((tokens, width), jnp.float32),
            jax.ShapeDtypeStruct((tokens, width), jnp.bfloat16),
            jax.ShapeDtypeStruct((1, width), jnp.float32),
        ],
        compiler_params=pltpu.CompilerParams(vmem_limit_bytes=56 * 1024 * 1024),
        cost_estimate=pl.CostEstimate(
            flops=4 * 1000 * 1000 * 1000, bytes_accessed=16 * 1024 * 1024, transcendentals=0
        ),
    )(core[None].astype(jnp.int32), *lows, scaled, weights)


def shards(
    block_entry_states,
    block_result_cotangent,
    token_assignments,
    packed_segment_sizes,
    admitted_route_quota,
    mixing_scale_factor,
    asker_projection,
    lookup_projection,
    content_projection,
    mixing_projection_back,
    asker_scale_factor,
    lookup_scale_factor,
    specialist_scale_factor,
    dispatcher_projection,
    specialist_switch_tensor,
    specialist_widen_tensor,
    specialist_shrink_tensor,
):
    bf16, f32 = jnp.bfloat16, jnp.float32
    tokens_dev = block_entry_states.shape[1]
    width = block_entry_states.shape[2]
    core = lax.axis_index("dp")
    me = lax.axis_index("expert")
    row_len = tokens_dev * 2
    heads_local = HEADS // 2
    head_width = width // HEADS
    half_width = width // 2
    score_scale = head_width ** (-0.5)
    experts = dispatcher_projection.shape[1]

    stacked = jnp.concatenate(
        [mixing_projection_back[:, :half_width], mixing_projection_back[:, half_width:]], axis=0
    )
    block = jnp.concatenate(
        [
            a
            for k, w in enumerate((asker_projection, lookup_projection, content_projection))
            for a in (w, stacked[:, PARTS[k][0] : PARTS[k][1]])
        ],
        axis=1,
    )
    blocks = near_exchange(jnp.broadcast_to(block[None], (8, *block.shape)))
    orders = jnp.stack([relative_order(core, me, part) for part in range(3)])

    assigned = token_assignments[0]
    expert_iota = jnp.arange(experts, dtype=jnp.int32)
    chosen = jnp.any(assigned[:, :, None] == expert_iota[None, None, :], axis=1)
    token_iota = jnp.arange(tokens_dev, dtype=jnp.int32)
    earlier = (token_iota[:, None] > token_iota[None, :]).astype(bf16)
    rank = dot(earlier, chosen.astype(bf16))
    kept = chosen & (rank < admitted_route_quota.astype(f32)[None, :])
    sent_counts = jnp.sum(kept.astype(jnp.int32), axis=0, dtype=jnp.int32)
    line_iota = jnp.arange(experts * 8, dtype=jnp.int32)
    line = line_iota % 8
    spread = (expert_iota[:, None] == (line_iota // 8)[None, :]).astype(bf16)
    slot_of_line = dot(jnp.where(kept, rank, -1.0).astype(bf16), spread).astype(jnp.int32)
    main = (slot_of_line == line[None, :]).astype(bf16)
    spare_hit = slot_of_line == (8 + line // 2)[None, :]
    spare = jnp.concatenate(
        [spare_hit & (line % 2 == half)[None, :] for half in range(2)], axis=0
    ).astype(bf16)

    lengths = packed_segment_sizes[0]
    row_positions = jnp.arange(row_len, dtype=jnp.int32)
    doc_ids, doc_offset = doc_places(lengths, row_positions)
    allowed = (doc_ids[None, :] == doc_ids[:, None]) & (
        row_positions[None, :] <= row_positions[:, None]
    )
    cos_table, sin_table = rope_tables(doc_offset, head_width)
    head_shape = (row_len, heads_local, head_width)
    column_start = core * half_width
    query_half_gain = lax.dynamic_slice_in_dim(asker_scale_factor, column_start, half_width)
    key_half_gain = lax.dynamic_slice_in_dim(lookup_scale_factor, column_start, half_width)

    inputs = block_entry_states[0].astype(f32)
    factor_in = rms_factor(inputs)
    normed_in = (inputs * factor_in * mixing_scale_factor).astype(bf16)
    normed_t = whole_row(normed_in, core).T
    normed_rel = reorder(normed_t, orders)
    grad_top_low = block_result_cotangent[0]
    send_grads = to_experts(main, spare, grad_top_low)
    both_cos = jnp.concatenate([cos_table, cos_table], axis=-1)[:, 0]
    both_sin = jnp.concatenate([-sin_table, sin_table], axis=-1)[:, 0]
    blocks, normed_rel, send_grads, both_cos, both_sin = lax.optimization_barrier(
        (blocks, normed_rel, send_grads, both_cos, both_sin)
    )
    blocks = blocks.reshape(8 * block.shape[0], block.shape[1])
    pieces = [[blocks[:, OFFSETS[k] : OFFSETS[k + 1]]] for k in range(3)]
    for k in range(3):
        got = permute_step(pieces[k][0], k, 3)
        pieces[k] = [jnp.concatenate([pieces[k][0], got], axis=0)]
    for k in range(3):
        pieces[k].append(permute_step(pieces[k][0], k, 4))
    for k in range(3):
        pieces[k] += [permute_step(piece, k, 5) for piece in pieces[k]]

    def product(k, i):
        size = width // 4
        return dot_tn(normed_rel[k][i * size : (i + 1) * size], pieces[k][i][:, :half_width])

    partial = [sum(product(k, i) for i in range(3)) for k in range(3)]
    send_grads, *_ = lax.optimization_barrier(
        (send_grads, *partial, *(pieces[k][3] for k in range(3)))
    )
    arrived_grads = exchange(send_grads)
    query_proj, key_proj, value_proj = (partial[k] + product(k, 3) for k in range(3))
    value_flat = value_proj.astype(bf16)
    query_sq, key_sq = lax.psum(
        (jnp.sum(query_proj * query_proj, axis=1), jnp.sum(key_proj * key_proj, axis=1)), "dp"
    )
    queries, keys, mixed_heads = attend(
        query_proj, key_proj, value_flat, (query_sq, key_sq),
        (query_half_gain, key_half_gain), both_cos, both_sin, doc_ids,
    )
    hidden_own, share_other, stacked_output = output_shares(
        mixed_heads, pieces, orders, block_entry_states[0], core
    )
    send_rows, hidden, factor_moe = normed_to_experts(
        main, spare, hidden_own, swap(share_other), specialist_scale_factor
    )

    arrived = exchange(send_rows)
    *late_pieces, queries, keys, scaled_own, _ = lax.optimization_barrier(
        (*pieces, queries, keys, (inputs * factor_in).astype(bf16), send_rows)
    )
    scaled_in = whole_row(scaled_own, core)
    weights = collect(late_pieces, orders)
    mixed_rel = reorder(mixed_heads.T, orders)
    raw_scores = (
        jnp.einsum(
            "qhd,khd->hqk",
            queries.reshape(head_shape),
            keys.reshape(head_shape),
            preferred_element_type=f32,
        )
        * score_scale
    )
    attn_probs = softmax_rows(jnp.where(allowed[None], raw_scores, NEG))
    weights, mixed_rel, attn_probs, scaled_in, arrived = lax.optimization_barrier(
        (weights, mixed_rel, attn_probs, scaled_in, arrived)
    )
    gate_w, up_w, down_w = (
        specialist_switch_tensor[0],
        specialist_widen_tensor[0],
        specialist_shrink_tensor[0],
    )
    top_rows = unpack(arrived_grads)
    plain_act_grad = dot_nt(top_rows, down_w).astype(bf16)
    row_grad, rows_in, gate_pre_grad, up_pre_grad, gated_act, logit_grad = expert_rows(
        arrived, plain_act_grad, gate_w, up_w, dispatcher_projection, core, me
    )
    returned_grads = exchange(row_grad)

    own_counts = jnp.where(
        (jnp.arange(2)[:, None, None] == core) & (expert_iota[None, :, None] == me),
        sent_counts[None, None, :],
        0,
    ).astype(f32)
    early = half_of(
        jnp.concatenate(
            [dot_tn(logit_grad, rows_in), own_counts.reshape(2 * experts * experts // width, width)]
        ),
        core,
    )
    small_rows, small_cols = early.shape[0], half_width // 64
    extra = early.reshape(small_rows, 64, small_cols).transpose(1, 0, 2)
    extra = extra.reshape(64 * 8, -1)
    extra = jnp.pad(extra.astype(bf16), ((0, 0), (0, 256 - extra.shape[1])))
    unit_grads = [
        swap(dot_tn(left, right).astype(bf16))
        for left, right in (
            (rows_in, gate_pre_grad[1]),
            (rows_in, up_pre_grad[1]),
            (gated_act[1], top_rows),
        )
    ]
    send_out, returned_grads, unit_grads, down_own = lax.optimization_barrier(
        (
            expert_results(gated_act, down_w, extra, core),
            returned_grads,
            unit_grads,
            dot_tn(gated_act[0], top_rows),
        )
    )
    hidden_grad, hidden_low, moe_gain_local = from_experts_back(
        main, spare, returned_grads, hidden, factor_moe, specialist_scale_factor, grad_top_low
    )
    returned = exchange(send_out)
    (
        query_scaled, key_scaled, value_proj_low, query_inner, key_inner, query_gain, key_gain,
        grad_full,
    ) = attend_back(
        hidden_low, swap(hidden_low), core, stacked_output, queries, keys, value_flat, attn_probs,
        (query_proj, key_proj), (query_sq, key_sq),
        (query_half_gain, key_half_gain), both_cos, both_sin,
    )
    got = [[], [], []]
    query_inner, key_inner = lax.psum((query_inner[0], key_inner[0]), "dp")
    query_low, key_low, *sent = first_pieces(
        (query_scaled, key_scaled), (query_proj, key_proj), (query_sq, key_sq),
        (query_inner, key_inner), value_proj_low, normed_rel, mixed_rel, grad_full,
    )
    empty_gain = jnp.zeros((width,), f32)
    query_gain_local = lax.dynamic_update_slice_in_dim(empty_gain, query_gain[0], column_start, 0)
    key_gain_local = lax.dynamic_update_slice_in_dim(empty_gain, key_gain[0], column_start, 0)
    lows = (query_low, key_low, value_proj_low)

    for step in (5, 4, 3):
        if step < 5:
            sent = sent_pieces(step, (0, 1, 2), normed_rel, lows, mixed_rel, grad_full, got)
        else:
            sent, unit_grads, share_lows, own_units = lax.optimization_barrier(
                (sent, unit_grads, lows, (gate_pre_grad, up_pre_grad))
            )
        for k in range(3):
            got[k].append(permute_step(sent[k], k, step))
        if step == 5:
            gate_weight_grad = dot_tn(rows_in, own_units[0][0]) + unit_grads[0].astype(f32)
            shares = input_shares(share_lows, scaled_in, weights, core)
            attn_gain_local = shares[2][0]
            gains = half_of(
                jnp.stack([attn_gain_local, query_gain_local, key_gain_local, moe_gain_local[0]]), core
            )
            early = jnp.sum(
                returned[:, width * 3 // 2 : width * 3 // 2 + small_rows * small_cols // 8]
                .reshape(64, small_rows * small_cols)
                .astype(f32),
                axis=0,
            )
            count = early.shape[0]
            small = jnp.concatenate([early, gains.reshape(-1)]).astype(bf16)
            small = jnp.pad(small, (0, 6144 - small.shape[0])).reshape(1, 8, 768)
            small = jnp.broadcast_to(small, (64, 8, 768)).reshape(512, 768)
            got, returned, gate_weight_grad, shares, small = (
                lax.optimization_barrier(
                    (
                        got,
                        returned,
                        gate_weight_grad,
                        shares[:2],
                        small,
                    )
                )
            )
            small = exchange(small)
        if step == 4:
            block_output = hidden + from_experts(main, spare, returned, width)
            down_weight_grad = down_own + unit_grads[2].astype(f32)
            got, shares, block_output, down_weight_grad = lax.optimization_barrier(
                (got, shares, block_output, down_weight_grad)
            )
    up_weight_grad = dot_tn(rows_in, own_units[1][0]) + unit_grads[1].astype(f32)
    got, up_weight_grad, small = lax.optimization_barrier((got, up_weight_grad, small))
    near = near_exchange(near_pieces(normed_rel[0], lows, mixed_rel[0], grad_full, got))
    query_weight_grad, key_weight_grad, value_weight_grad, output_weight_grad = near_total(near)
    normed_in_grad = shares[0] + swap(shares[1]).astype(f32)
    scaled = normed_in_grad * mixing_scale_factor
    input_norm_grad = factor_in * (
        scaled
        - inputs * factor_in * factor_in * jnp.mean(scaled * inputs, axis=-1, keepdims=True)
    )
    input_grad = hidden_grad + input_norm_grad

    small = small.reshape(64, 6144).astype(f32)
    early = (
        small[:, :count]
        .reshape(64, small_rows, small_cols)
        .transpose(1, 0, 2)
        .reshape(small_rows, half_width)
    )
    gains = jnp.sum(small[:, count : count + 4 * half_width], axis=0).reshape(4, half_width)
    totals = beside_other_half(jnp.concatenate([early, gains]), core)
    router_weight_grad, all_counts, gains = totals[:experts].T, totals[experts:-4], totals[-4:]
    got_counts = jnp.sum(
        jnp.where(
            (jnp.arange(2)[:, None, None] == core) & (expert_iota[None, None, :] == me),
            all_counts.reshape(2, experts, experts),
            0.0,
        ),
        axis=(0, 2),
    ).astype(jnp.int32)
    return (
        block_output[None],
        input_grad[None],
        gains[0],
        query_weight_grad,
        key_weight_grad,
        value_weight_grad,
        output_weight_grad,
        gains[1],
        gains[2],
        gains[3],
        router_weight_grad,
        gate_weight_grad[None],
        up_weight_grad[None],
        down_weight_grad[None],
        got_counts[None],
    )


def solution(mesh):
    placed = (
        P("expert", "dp", None),
        P("expert", "dp", None),
        P("expert", "dp", None),
        P("expert", None),
        P(),
        P(),
        P("expert", "dp"),
        P("expert", "dp"),
        P("expert", "dp"),
        P(("dp", "expert"), None),
        P(),
        P(),
        P(),
        P(),
        P("expert", None, None),
        P("expert", None, None),
        P("expert", None, None),
    )
    return jax.shard_map(
        shards,
        mesh=mesh,
        in_specs=placed,
        out_specs=(
            P("expert", "dp", None),
            P("expert", "dp", None),
            P(),
            P("expert", "dp"),
            P("expert", "dp"),
            P("expert", "dp"),
            P(("dp", "expert"), None),
            P(),
            P(),
            P(),
            P(),
            P("expert", None, "dp"),
            P("expert", None, "dp"),
            P("expert", "dp", None),
            P("expert", "dp"),
        ),
        check_vma=False,
    )
```
